256 devices in a mesh: seq: 64 (over z, x, core), mlp: 4 (over y).
Axes of the slice: x: 4, y: 4, z: 8, core: 2. Of those that a mesh axis runs over, the one named last changes fastest.
Arguments:
- tokens: bfloat16 [32768, 1024], P('seq'), may hold values from -6 to 6
- positions: int32 [4096], replicated, may hold values from 0 to 32767, as said below
- value_proj: bfloat16 [1024, 1024], replicated, may hold values from -0.1875 to 0.1875
- write_proj: bfloat16 [1024, 128], replicated, may hold values from -0.1875 to 0.1875
- read_proj: bfloat16 [1024, 128], replicated, may hold values from -0.1875 to 0.1875
- step_proj: bfloat16 [1024, 16], replicated, may hold values from -0.1875 to 0.1875
- step_bias: float32 [16], replicated, may hold values from -1 to 1
- decay_rate: float32 [16], replicated, may hold values from 6.1035156e-06 to 0.035, as said below
- reset_depth: float32 [32768], P('seq'), may hold values from 0 to 0.7, as said below
- out_proj: bfloat16 [1024, 1024], replicated, may hold values from -0.1875 to 0.1875
- router: float32 [1024], replicated, may hold values from -0.1875 to 0.1875
- pad_vector: bfloat16 [1024], replicated, may hold values from -6 to 6
- up_weight: bfloat16 [2048, 4096], P(None, 'mlp'), may hold values from -0.125 to 0.125
- down_weight: bfloat16 [1024, 4096], P(None, 'mlp'), may hold values from -0.09375 to 0.09375
- cotangent: bfloat16 [32768, 1024], P('seq'), may hold values from -16 to 16
Outputs:
- mixed: bfloat16 [32768, 1024], P('seq')
- up_grad: float32 [2048, 4096], P('seq', 'mlp')
- down_grad: float32 [1024, 4096], P('seq', 'mlp')
The draws below stay inside these ranges and needn't reach their ends.
Inputs may be any that keep to these rules, and one draw needn't show every extreme that they name: `positions`: strictly increasing; every multiple of 512 is among them; each aligned block of 512 bytes holds between 1 and 127 of them, and both counts are reached. `decay_rate`: positive rates. `reset_depth`: Nonnegative.
All inputs are finite; a program needn't handle non-finite values.
Results may differ from the reference program's by a relative error of at most 0.017.
Values may be sent and summed in bfloat16 or wider, within the bound.
A program may use at most 128 MiB of HBM per device.

```python
import jax
import jax.numpy as jnp
from jax import lax

D = 1024
NH = 16
P_SIZE = 64
NS = 128
DI = 2048
FF = 4096
L_DEV = 512
CH_DEV = 64
SEQ_LEN = 32768
NCH = 4096


def draw_decay_rate(key, part):
    ranking = jax.random.permutation(jax.random.fold_in(key, 11), NH)
    slow_count = NH // 2
    uniform_draw = jax.random.uniform(jax.random.fold_in(key, 12), (NH,), jnp.float32)
    slow_rate = (0.2 + 1.3 * uniform_draw) / SEQ_LEN
    fast_rate = 0.02 + 0.015 * uniform_draw
    return jnp.where(ranking < slow_count, slow_rate, fast_rate).astype(jnp.float32)


def draw_reset_depth(key, part):
    key = jax.random.fold_in(key, 31)
    block_count = SEQ_LEN // L_DEV
    chosen = jax.random.permutation(jax.random.fold_in(key, 1), block_count) < (block_count + 1) // 2
    spots = jax.random.randint(jax.random.fold_in(key, 2), (block_count,), 0, L_DEV)
    depths = jax.random.uniform(jax.random.fold_in(key, 3), (block_count,), jnp.float32, 0.22, 0.69)
    depths = jnp.where(chosen, depths, 0.0)
    hits = (jnp.arange(L_DEV, dtype=jnp.int32)[None, :] == spots[:, None]).astype(jnp.float32)
    return (hits * depths[:, None]).reshape(-1).astype(jnp.float32)


def draw_positions(key, part):
    block_count = SEQ_LEN // L_DEV
    half_count = block_count // 2
    shuffled = jax.random.permutation(jax.random.fold_in(key, 21), block_count)
    spreads = jax.random.randint(jax.random.fold_in(key, 22), (half_count,), 0, CH_DEV)
    spreads = spreads.at[0].set(CH_DEV - 1).astype(jnp.int32)
    shifts = jnp.zeros((block_count,), jnp.int32).at[shuffled[:half_count]].set(spreads)
    shifts = shifts.at[shuffled[half_count:2 * half_count]].set(-spreads)
    counts = CH_DEV + shifts
    block_keys = jax.random.split(jax.random.fold_in(key, 23), block_count)

    def one_block(block_key, group_count):
        placed = jax.random.permutation(block_key, L_DEV - 1) + 1
        chosen = (jnp.arange(L_DEV - 1) < group_count - 1).astype(jnp.int32)
        marks = jnp.zeros((L_DEV,), jnp.int32).at[placed].set(chosen)
        return marks.at[0].set(1)
    marks = jax.vmap(one_block)(block_keys, counts).reshape(-1)
    return jnp.nonzero(marks, size=NCH)[0].astype(jnp.int32)


def raised(values, key, source, target, blocks, factor):
    def block_of(position):
        return (jnp.arange(values.shape[position]) // (values.shape[position] // blocks)).reshape((-1,) + (1,) * (values.ndim - 1 - position))

    first = jax.random.permutation(key, blocks)[block_of(target)]
    far = (block_of(target) + blocks // 2) % blocks
    return jnp.where((block_of(source) == first) | (block_of(source) == far), factor * values, values)


def level_of(own_key, dims, cuts, least, top_value):
    def one(axis_at, parts):
        draws = jax.random.uniform(jax.random.fold_in(jax.random.fold_in(own_key, 6), axis_at), (parts,), jnp.float32, least / len(cuts), top_value / len(cuts))
        return jnp.repeat(jnp.exp(draws), dims[axis_at] // parts).reshape((-1,) + (1,) * (len(dims) - axis_at - 1))

    factor_of = one(*cuts[0])
    for cut in cuts[1:]:
        factor_of = factor_of * one(*cut)
    return factor_of


def bell_draw(rng, dims, scale, bound, cuts=(), kind=jnp.bfloat16):
    values = jax.random.normal(rng, dims, jnp.float32) * scale
    if len(cuts) > 0:
        values = level_of(rng, dims, cuts, -0.22, 0.18) * values
    return jnp.clip(values, min=-bound, max=bound).astype(kind)


def heavy_noise(key, extent, spread, reach, cuts, heavy, kind=jnp.bfloat16):
    entries = spread * jax.random.normal(key, extent, jnp.float32)
    if cuts:
        entries = entries * level_of(key, extent, cuts, -0.22, 0.18)
    return jnp.clip(raised(entries, jax.random.fold_in(key, 3), *heavy), -reach, reach).astype(kind)


def setup_inputs(seed: int = 0) -> dict:
    key_list = jax.random.split(jax.random.key(seed), 16)
    return {
        "tokens": bell_draw(key_list[0], (SEQ_LEN, D), 1.0, 6.0, ((0, 64),)),
        "positions": draw_positions(jax.random.fold_in(key_list[15], 71), 0),
        "value_proj": bell_draw(key_list[2], (D, NH * P_SIZE), D ** -0.5, 0.1875),
        "write_proj": bell_draw(key_list[3], (D, NS), D ** -0.5, 0.1875),
        "read_proj": bell_draw(key_list[4], (D, NS), D ** -0.5, 0.1875),
        "step_proj": bell_draw(key_list[5], (D, NH), D ** -0.5, 0.1875),
        "step_bias": jnp.clip(jax.random.uniform(key_list[6], (NH,), jnp.float32, -1.0, 1.0), -1.0, 1.0),
        "decay_rate": draw_decay_rate(jax.random.fold_in(key_list[15], 71), 0),
        "reset_depth": draw_reset_depth(jax.random.fold_in(key_list[15], 71), 0),
        "out_proj": bell_draw(key_list[9], (NH * P_SIZE, D), (NH * P_SIZE) ** -0.5, 0.1875),
        "router": bell_draw(key_list[10], (D,), D ** -0.5, 0.1875, (), jnp.float32),
        "pad_vector": bell_draw(key_list[11], (DI - D,), 1.0, 6.0),
        "up_weight": bell_draw(key_list[12], (DI, FF), DI ** -0.5, 0.125, ((1, 4),)),
        "down_weight": bell_draw(key_list[13], (D, FF), FF ** -0.5, 0.09375, ((1, 4),)),
        "cotangent": heavy_noise(key_list[14], (SEQ_LEN, D), 1.0, 16.0, ((0, 64),), (0, 1, 64, 4.0)),
    }


HIGHEST = lax.Precision.HIGHEST

def norm_rows(field):
    return field * lax.rsqrt(lax.optimization_barrier(jnp.mean(field * field, axis=-1, keepdims=True)) + 1e-05)

def smooth_gate(field):
    return jax.nn.gelu(field, approximate=True)

def block_terms(values, write_keys, read_keys, step_size, log_decay):
    cum_decay = jnp.cumsum(log_decay, axis=0)
    scores = lax.dot_general(read_keys, write_keys, (((1,), (1,)), ((), ())), preferred_element_type=jnp.float32)
    step_ids = jnp.arange(log_decay.shape[0])
    causal = step_ids[:, None] >= step_ids[None, :]
    log_gap = cum_decay[:, None, :] - cum_decay[None, :, :]
    decays = jnp.exp(jnp.where(causal[:, :, None], log_gap, -jnp.inf))
    mixing = scores[:, :, None] * decays
    weighted = step_size[:, :, None] * values.astype(jnp.float32)
    within = jnp.einsum('tsh,shp->thp', mixing, weighted, precision=HIGHEST)
    tail_weight = jnp.exp(cum_decay[-1][None, :] - cum_decay) * step_size
    fresh_state = jnp.einsum('shp,sn->hpn', tail_weight[:, :, None] * values.astype(jnp.float32), write_keys.astype(jnp.float32), precision=HIGHEST)
    return (within, cum_decay, jnp.exp(cum_decay[-1]), fresh_state)

def carried_terms(ssd_state, read_keys, cum_decay):
    return jnp.exp(cum_decay)[:, :, None] * jnp.einsum('hpn,tn->thp', ssd_state, read_keys.astype(jnp.float32), precision=HIGHEST)

def advance(ssd_state, block_data):
    within, cum_decay, block_decay, fresh_state = block_terms(*block_data)
    scanned = within + carried_terms(ssd_state, block_data[2], cum_decay)
    return (block_decay[:, None, None] * ssd_state + fresh_state, scanned)

def inner_layer(group_rows, group_grad, pad_vector, up_weight, down_weight):
    row_count = group_rows.shape[0]
    widened = jnp.concatenate([group_rows, jnp.broadcast_to(pad_vector, (row_count, pad_vector.shape[0]))], axis=1)
    inner_normed = norm_rows(widened.astype(jnp.float32)).astype(jnp.bfloat16)
    hidden_pre = jnp.dot(inner_normed, up_weight, preferred_element_type=jnp.float32)
    hidden = smooth_gate(hidden_pre).astype(jnp.bfloat16)
    summed = lax.dot_general(hidden, down_weight, (((1,), (1,)), ((), ())), preferred_element_type=jnp.float32)
    inner_out = (group_rows.astype(jnp.float32) + summed).astype(jnp.bfloat16)
    down_grad = lax.dot_general(group_grad, hidden, (((0,), (0,)), ((), ())), preferred_element_type=jnp.float32)
    hidden_grad = jnp.dot(group_grad, down_weight, preferred_element_type=jnp.float32)
    unused, pull_back = jax.vjp(smooth_gate, hidden_pre)
    pre_grad = pull_back(hidden_grad)[0].astype(jnp.bfloat16)
    up_grad = lax.dot_general(inner_normed, pre_grad, (((0,), (0,)), ((), ())), preferred_element_type=jnp.float32)
    return (inner_out, up_grad, down_grad)

def reference(tokens, positions, value_proj, write_proj, read_proj, step_proj, step_bias, decay_rate, reset_depth, out_proj, router, pad_vector, up_weight, down_weight, cotangent):
    wide_tokens = tokens.astype(jnp.float32)
    normed = norm_rows(wide_tokens).astype(jnp.bfloat16)
    values = jnp.dot(normed, value_proj, preferred_element_type=jnp.float32).astype(jnp.bfloat16)
    write_keys = jnp.dot(normed, write_proj, preferred_element_type=jnp.float32).astype(jnp.bfloat16)
    read_keys = jnp.dot(normed, read_proj, preferred_element_type=jnp.float32).astype(jnp.bfloat16)
    step_size = jax.nn.softplus(jnp.dot(normed, step_proj, preferred_element_type=jnp.float32) + step_bias)
    log_decay = -step_size * decay_rate - reset_depth[:, None]
    block_count = SEQ_LEN // L_DEV
    blocks_in = (values.reshape(block_count, L_DEV, NH, P_SIZE), write_keys.reshape(block_count, L_DEV, NS), read_keys.reshape(block_count, L_DEV, NS), step_size.reshape(block_count, L_DEV, NH), log_decay.reshape(block_count, L_DEV, NH))
    start_state = jnp.zeros((NH, P_SIZE, NS), jnp.float32)
    unused, scanned = lax.scan(advance, start_state, blocks_in)
    scan_normed = norm_rows(scanned.reshape(SEQ_LEN, NH * P_SIZE)).astype(jnp.bfloat16)
    encoded = (wide_tokens + jnp.dot(scan_normed, out_proj, preferred_element_type=jnp.float32)).astype(jnp.bfloat16)
    encoded_f32 = encoded.astype(jnp.float32)
    confidence = jax.nn.sigmoid(jnp.dot(encoded_f32, router, precision=HIGHEST))
    marks = jnp.zeros((SEQ_LEN,), jnp.int32).at[positions].set(1)
    group_of = (jnp.cumsum(marks) - 1).astype(jnp.int32)
    group_rows = encoded[positions]
    group_grad = jax.ops.segment_sum(confidence[:, None] * cotangent.astype(jnp.float32), group_of, num_segments=NCH).astype(jnp.bfloat16)
    inner_out, up_grad, down_grad = inner_layer(group_rows, group_grad, pad_vector, up_weight, down_weight)
    mixed = (encoded_f32 + confidence[:, None] * inner_out[group_of].astype(jnp.float32)).astype(jnp.bfloat16)
    return (mixed, up_grad, down_grad)
```

```python
import functools

import jax
import jax.numpy as jnp
from jax import lax
from jax.experimental import pallas as pl
from jax.experimental.pallas import tpu as pltpu
from jax.sharding import PartitionSpec as P

F32, BF16 = jnp.float32, jnp.bfloat16
HIGHEST = lax.Precision.HIGHEST
MESH = pl.DeviceIdType.MESH

ROWS = 512
D = 1024
HEADS = 16
HEAD = 64
NS = 128
Q = 128
CHUNKS = ROWS // Q
SLOTS = 128
XN, CN = 4, 2
PLANE = XN * CN
NQ = 4
W = D // NQ
PIECE = 272
EPS = 1e-05
G0, G1 = 0.7978845608028654, 0.044715


def nn(a, b):
    return jnp.dot(a, b, preferred_element_type=F32)


def nt(a, b):
    return lax.dot_general(a, b, (((1,), (1,)), ((), ())), preferred_element_type=F32)


def split3(x):
    hi = x.astype(BF16).astype(F32)
    mid = (x - hi).astype(BF16).astype(F32)
    return hi, mid, x - hi - mid


def in_rows(parts, shape):
    ids = lax.broadcasted_iota(jnp.int32, shape, 0)
    block = jnp.zeros(shape, F32)
    for i, part in enumerate(parts):
        block = jnp.where(ids == i, part, block)
    return block


def kernel(
    zn, yn,
    tokens, positions, value_proj, write_proj, read_proj, step_proj, step_bias, decay_rate, reset_depth,
    out_proj, router, pad_vector, up_weight, down_weight, cotangent,
    mixed, up_out, down_out,
    tok, pos, vp, wr, sp, bias, rate, reset, op, rout, pad, up, down, cot,
    normed, kr, vals, zrow, zcol, expander, dtv, ece, state, chunk_state, dpre, within,
    p1s, p1r, p2s, p2r, p3s, incoming,
    encoded, groups, select, mct, padup, pad_col, padsq,
    xn, gg, scale, slope, fac, turned, lt, lto, vx, vr,
    partial, ars, ar1, io,
    own, prod, ra1, rb1, ra_left, ra_right, rb_left, rb_right, total, zs, zd, zu, zv,
    load, ss, rs,
):
    sn = zn * PLANE
    ru, rd = 2 * D // sn, D // sn
    zh = zn // 2
    qw = D // yn
    seq, y = lax.axis_index("seq"), lax.axis_index("mlp")
    z, me = seq // PLANE, lax.rem(seq, PLANE)
    x, core = me // CN, lax.rem(me, CN)

    def plane_at(j):
        return z * PLANE + j

    pairs = [
        (tokens, tok), (write_proj, wr.at[:, 0:NS]), (read_proj, wr.at[:, NS : 2 * NS]), (step_proj, sp),
        (step_bias, bias), (decay_rate, rate), (reset_depth, reset), (value_proj, vp), (positions, pos),
        (pad_vector, pad), (out_proj, op), (router, rout), (up_weight, up), (cotangent, cot), (down_weight, down),
    ]
    loads = [pltpu.make_async_copy(a, b, load.at[i]) for i, (a, b) in enumerate(pairs)]
    for copy in loads:
        copy.start()

    barrier = pltpu.get_barrier_semaphore()
    peers = 0
    for oy in range(yn):
        for o in range(PLANE):
            if o or oy:
                peers += 1
                pl.semaphore_signal(
                    barrier, inc=1, device_id_type=MESH,
                    device_id=(plane_at(lax.rem(me + o, PLANE)), lax.rem(y + oy, yn)),
                )
    for o in range(1, zn):
        peers += 1
        pl.semaphore_signal(
            barrier, inc=1, device_id_type=MESH, device_id=(lax.rem(z + o, zn) * PLANE + me, y)
        )

    count = [0]

    def ids(n):
        count[0] += n
        return count[0] - n

    def rdma(src, dst, i, to_seq, to_y):
        return pltpu.make_async_remote_copy(
            src_ref=src, dst_ref=dst, send_sem=ss.at[i], recv_sem=rs.at[i],
            device_id=(to_seq, to_y), device_id_type=MESH,
        )

    for copy in loads[:7]:
        copy.wait()

    def norm(b, carry):
        rows = pl.ds(pl.multiple_of(b * Q, Q), Q)
        field = tok[rows, :].astype(F32)
        ms = jnp.mean(field * field, axis=-1, keepdims=True)
        normed[rows, :] = (field * lax.rsqrt(ms + EPS)).astype(BF16)
        return carry

    lax.fori_loop(0, CHUNKS, norm, 0)
    e_row = lax.rem(lax.broadcasted_iota(jnp.int32, (2 * Q, D), 0), HEADS)
    e_col = lax.broadcasted_iota(jnp.int32, (2 * Q, D), 1) // HEAD
    expander[...] = (e_row == e_col).astype(F32).astype(BF16)

    eye = lax.broadcasted_iota(jnp.int32, (HEADS, HEADS), 0) == lax.broadcasted_iota(jnp.int32, (HEADS, HEADS), 1)

    def column(row):
        return jnp.sum(jnp.where(eye, jnp.broadcast_to(row, (HEADS, HEADS)), 0.0), axis=1, keepdims=True)

    kr[...] = nn(normed[...], wr[...]).astype(BF16)
    step_t = sp[...].astype(F32).T.astype(BF16)
    raw = nt(step_t, normed[...]) + column(bias[...])
    dt_all = jnp.maximum(raw, 0.0) + jnp.log1p(jnp.exp(-jnp.abs(raw)))
    ld_all = -dt_all * column(rate[...]) - reset[...]
    s_id = lax.broadcasted_iota(jnp.int32, (Q, Q), 0)
    t_id = lax.broadcasted_iota(jnp.int32, (Q, Q), 1)
    before = (s_id <= t_id).astype(F32)
    for c in range(CHUNKS):
        cols = slice(c * Q, (c + 1) * Q)
        dt = dt_all[:, cols]
        cum = jnp.dot(ld_all[:, cols], before, precision=HIGHEST, preferred_element_type=F32)
        tail = jnp.exp(cum[:, Q - 1 : Q] - cum) * dt
        block = jnp.concatenate([dt, cum, tail, jnp.exp(cum), jnp.zeros((64, Q), F32)], axis=0)
        zrow[c] = block
        zcol[c] = block.T
    loads[7].wait()

    def values(b, carry):
        rows = pl.ds(pl.multiple_of(b * 256, 256), 256)
        vals[rows, :] = nn(normed[rows, :], vp[...]).astype(BF16)
        return carry

    lax.fori_loop(0, ROWS // 256, values, 0)

    state[...] = jnp.zeros_like(state)

    def chunk(c, decay):
        rows = pl.ds(pl.multiple_of(c * Q, Q), Q)
        zt = zcol[c]
        hi, mid, unused = split3(zt)
        kind = lax.broadcasted_iota(jnp.int32, (Q, Q), 1) // HEADS

        def expand(k):
            lhs = jnp.concatenate([jnp.where(kind == k, hi, 0.0), jnp.where(kind == k, mid, 0.0)], axis=1)
            return nn(lhs.astype(BF16), expander[...])

        v = vals[rows, :].astype(F32)
        dtv[rows, :] = (expand(0) * v).astype(BF16)
        weighted = (expand(2) * v).astype(BF16)
        grown = expand(3)
        ece[rows, :] = grown
        keys_t = kr[rows, 0:NS].astype(F32).T.astype(BF16)
        old = state[...]
        chunk_state[c] = old
        dpre[c] = jnp.broadcast_to(decay, (8, D))
        last = grown[Q - 1 : Q, :]
        state[...] = last * old + nn(keys_t, weighted)
        return decay * last

    decay = lax.fori_loop(0, CHUNKS, chunk, jnp.ones((1, D), F32))

    dpre[CHUNKS] = jnp.broadcast_to(decay, (8, D))
    mine = pl.ds(pl.multiple_of(y * qw, qw), qw)
    decay_rows = in_rows(split3(dpre[CHUNKS, 0:1, mine]), (16, qw)).astype(BF16)
    for j in range(PLANE):
        p1s[j, 0:16, :] = state[16 * j : 16 * j + 16, mine].astype(BF16)
        p1s[j, 16:32, :] = decay_rows
    p1r[0] = p1s[me]
    pl.semaphore_wait(barrier, peers)
    base = ids(PLANE)
    step1 = []
    for o in range(1, PLANE):
        j = lax.rem(me + o, PLANE)
        step1.append(rdma(p1s.at[j], p1r.at[o], base + o, plane_at(j), y))
        step1[-1].start()

    def intra(c, carry):
        rows = pl.ds(pl.multiple_of(c * Q, Q), Q)
        scores = nt(kr[rows, NS : 2 * NS], kr[rows, 0:NS])
        scores = jnp.where(s_id >= t_id, scores, 0.0)
        first = lax.broadcasted_iota(jnp.int32, (Q, 2 * HEAD), 1) < HEAD
        zr, zt = zrow[c], zcol[c]
        for pair in range(HEADS // 2):
            lanes = slice(2 * HEAD * pair, 2 * HEAD * (pair + 1))
            both = dtv[rows, lanes].astype(F32)
            right = jnp.concatenate([jnp.where(first, both, 0.0), jnp.where(first, 0.0, both)], axis=0)
            mixing = []
            for h in (2 * pair, 2 * pair + 1):
                gap = zt[:, HEADS + h : HEADS + h + 1] - zr[HEADS + h : HEADS + h + 1, :]
                mixing.append(scores * jnp.exp(jnp.minimum(gap, 0.0)))
            within[rows, lanes] = nn(jnp.concatenate(mixing, axis=1).astype(BF16), right.astype(BF16))
        return carry

    lax.fori_loop(0, CHUNKS // 2, intra, 0)

    def read(block):
        block = block.astype(F32)
        return block[0:16], block[16:17] + block[17:18] + block[18:19]

    for copy in step1:
        copy.wait_recv()
    pre, pre_decay = [jnp.zeros((16, qw), F32)], [jnp.ones((1, qw), F32)]
    for k in range(PLANE):
        new, by = read(p1r[lax.rem(me - k + PLANE, PLANE)])
        pre.append(by * pre[-1] + new)
        pre_decay.append(by * pre_decay[-1])
    p2s[0:16, :] = pre[-1].astype(BF16)
    p2s[16:32, :] = in_rows(split3(pre_decay[-1]), (16, qw)).astype(BF16)
    p2r[0] = p2s[...]
    base = ids(zn)
    step2 = [None]
    for o in range(1, zn):
        step2.append(rdma(p2s, p2r.at[o], base + o, lax.rem(z + o, zn) * PLANE + me, y))
        pl.when(z + o < zn)(step2[o].start)

    lax.fori_loop(CHUNKS // 2, CHUNKS, intra, 0)

    for o in range(1, zn):
        pl.when(z >= o)(step2[o].wait_recv)
    start = jnp.zeros((16, qw), F32)
    for k in range(zn - 1):
        new, by = read(p2r[jnp.maximum(z - k, 0)])
        start = jnp.where(k < z, by * start + new, start)
    for k in range(PLANE):
        p3s[k] = (pre_decay[k] * start + pre[k]).astype(BF16)

    def landing(j, at_y):
        return incoming.at[pl.ds(pl.multiple_of(j * 16, 16), 16), pl.ds(pl.multiple_of(at_y * qw, qw), qw)]

    base = ids(PLANE * yn)
    step3, from3 = [], []
    for o in range(PLANE):
        for oy in range(yn):
            if o or oy:
                i = base + o * yn + oy
                j, at_y = lax.rem(me + o, PLANE), lax.rem(y + oy, yn)
                step3.append(rdma(p3s.at[j], landing(me, y), i, plane_at(j), at_y))
                step3[-1].start()
                j, at_y = lax.rem(me - o + PLANE, PLANE), lax.rem(y - oy + yn, yn)
                from3.append(rdma(p3s.at[j], landing(j, at_y), i, plane_at(j), at_y))
    incoming[pl.ds(pl.multiple_of(me * 16, 16), 16), mine] = p3s[me]

    for copy in loads[8:]:
        copy.wait()
    local = pos[...] - seq * ROWS
    n_pos = local.shape[1]
    high, low = local >> 7, local & 127
    ids8 = lax.broadcasted_iota(jnp.int32, (8, n_pos), 0)
    left = jnp.where((jnp.broadcast_to(high, (8, n_pos)) == ids8) & (ids8 < CHUNKS), 1.0, 0.0).astype(BF16)
    ids128 = lax.broadcasted_iota(jnp.int32, (Q, n_pos), 0)
    right = jnp.where(jnp.broadcast_to(low, (Q, n_pos)) == ids128, 1.0, 0.0).astype(BF16)
    marks = nt(left, right)
    running = nn(marks.astype(BF16), before.astype(BF16))
    parts, so_far = [], jnp.zeros((1, 1), F32)
    for c in range(CHUNKS):
        parts.append(running[c : c + 1] + so_far)
        so_far = parts[-1][:, Q - 1 : Q]
    group_of = jnp.concatenate(parts, axis=1) - 1.0
    mark = jnp.concatenate([marks[c : c + 1] for c in range(CHUNKS)], axis=1)
    slot = lax.broadcasted_iota(jnp.int32, (SLOTS, ROWS), 0).astype(F32)
    member = jnp.where(slot == group_of, 1.0, 0.0)
    select[...] = (member * mark).astype(BF16)
    pad_row = pad[...].astype(F32)
    padsq[...] = jnp.broadcast_to(jnp.sum(pad_row * pad_row, axis=-1, keepdims=True), (8, 128))
    pad_col[...] = jnp.broadcast_to(pad_row, (128, D)).T
    padup[...] = nn(jnp.broadcast_to(pad_row, (16, D)).astype(BF16), up[D : 2 * D, :])

    for copy in from3:
        copy.wait_recv()

    def encode(b, carry):
        for k in range(2):
            c = 2 * b + k
            rows = pl.ds(pl.multiple_of(c * Q, Q), Q)
            full = chunk_state[c] + dpre[c, 0:1, :] * incoming[...].astype(F32)
            carried = nn(kr[rows, NS : 2 * NS], full.astype(BF16))
            scanned = within[rows, :] + ece[rows, :] * carried
            ms = jnp.mean(scanned * scanned, axis=-1, keepdims=True)
            normed[rows, :] = (scanned * lax.rsqrt(ms + EPS)).astype(BF16)
        rows = pl.ds(pl.multiple_of(b * 256, 256), 256)
        encoded[rows, :] = (tok[rows, :].astype(F32) + nn(normed[rows, :], op[...])).astype(BF16)
        return carry

    lax.fori_loop(0, 2, encode, 0)
    logits = nt(in_rows(split3(rout[...]), (16, D)).astype(BF16), encoded[...])
    confidence = 1.0 / (1.0 + jnp.exp(-jnp.sum(logits, axis=0, keepdims=True)))
    weight = member * confidence
    weight_hi = weight.astype(BF16)
    weight_lo = (weight - weight_hi.astype(F32)).astype(BF16)
    mct[:, 0:SLOTS] = weight_hi.astype(F32).T.astype(BF16)
    mct[:, SLOTS : 2 * SLOTS] = weight_lo.astype(F32).T.astype(BF16)
    groups[...] = nn(select[...], encoded[...])
    grads = nn(weight_hi, cot[...]) + nn(weight_lo, cot[...])
    gg[...] = grads.astype(BF16)
    rows_f = groups[...]
    ms = (jnp.sum(rows_f * rows_f, axis=-1, keepdims=True) + padsq[0:1, 0:1]) * (0.5 / D)
    r = lax.rsqrt(ms + EPS)
    scale[...] = jnp.broadcast_to(r, (SLOTS, 128))
    inner = rows_f * r
    xn[...] = inner.astype(BF16)

    def turn(field, first_row, each, blocks):
        turned[...] = field.T.astype(BF16)
        for k in range(XN):
            at = lax.rem(x + k, XN)
            for b in range(blocks):
                rows = slice(first_row + b * each, first_row + (b + 1) * each)
                begin = (b * PLANE + at * CN + core) * each
                lt[k, rows, 0:SLOTS] = turned[pl.ds(pl.multiple_of(begin, 16), each), :]
                begin = (b * PLANE + at * CN + 1 - core) * each
                lto[k, rows, :] = turned[pl.ds(pl.multiple_of(begin, 16), each), :]

    turn(inner, 0, ru, zh)
    turn(grads, 128, rd, zn)
    mate = plane_at(x * CN + 1 - core)
    base = ids(4)
    swaps = [
        rdma(lto, lt.at[:, :, SLOTS : 2 * SLOTS], base, mate, y),
        rdma(fac.at[1, 0:SLOTS, :], fac.at[1, SLOTS : 2 * SLOTS, :], base + 1, mate, y),
        rdma(fac.at[0, 0:SLOTS, :], fac.at[0, SLOTS : 2 * SLOTS, :], base + 2, mate, y),
        rdma(vx, vr, base + 3, mate, y),
    ]
    swaps[0].start()

    def forward(b, carry):
        cols = pl.ds(pl.multiple_of(b * 256, 256), 256)
        pre_act = nn(xn[...], up[0:D, cols]) + scale[:, 0:1] * padup[0:1, cols]
        square = pre_act * pre_act
        bend = jnp.tanh(G0 * pre_act * (1.0 + G1 * square))
        fac[1, 0:SLOTS, cols] = (0.5 * pre_act * (1.0 + bend)).astype(BF16)
        slope[:, cols] = 0.5 * (1.0 + bend) + 0.5 * pre_act * (1.0 - bend * bend) * (
            G0 * (1.0 + 3.0 * G1 * square)
        )
        return carry

    lax.fori_loop(0, 4, forward, 0)
    swaps[1].start()

    def backward(b, carry):
        cols = pl.ds(pl.multiple_of(b * 256, 256), 256)
        pre_grad = (nn(gg[...], down[:, cols]) * slope[:, cols]).astype(BF16)
        fac[0, 0:SLOTS, cols] = pre_grad
        pad_term = jnp.sum(pre_grad.astype(F32) * scale[:, 0:1], axis=0, keepdims=True)
        vx[:, cols] = jnp.broadcast_to(pad_term, (8, 256))
        return carry

    lax.fori_loop(0, 4, backward, 0)
    swaps[2].start()
    swaps[3].start()

    rq = SLOTS // yn
    partial[...] = nt(fac[1, 0:SLOTS, :], down[...])
    ars[...] = partial[...].astype(BF16)
    base = ids(2 * yn)
    share1, share2, from2 = [], [], []
    my_rows = pl.ds(pl.multiple_of(y * rq, rq), rq)
    for o in range(1, yn):
        at_y = lax.rem(y + o, yn)
        share1.append(rdma(ars.at[pl.ds(pl.multiple_of(at_y * rq, rq), rq), :], ar1.at[o - 1], base + o, seq, at_y))
        share1[-1].start()
        share2.append(rdma(io.at[my_rows, :], io.at[my_rows, :], base + yn + o, seq, at_y))
        at_y = lax.rem(y - o + yn, yn)
        other = pl.ds(pl.multiple_of(at_y * rq, rq), rq)
        from2.append(rdma(io.at[other, :], io.at[other, :], base + yn + o, seq, at_y))

    for copy in swaps:
        copy.wait_recv()
    right_x = plane_at(lax.rem(x + 1, XN) * CN + core)
    left_x = plane_at(lax.rem(x + XN - 1, XN) * CN + core)
    upper, lower = slice(0, 128), slice(128, PIECE)
    ahead, later, along = [], [], []

    def multiply(q):
        cols = slice(q * W, (q + 1) * W)
        pad_rows = in_rows([vx[0:1, cols] + vr[0:1, cols]], (16, W))
        own[q, 256:PIECE, :] = pad_rows
        for k in range(1, XN):
            prod[k, q, 256:PIECE, :] = pad_rows.astype(BF16)
        for part in range(2):
            rows = slice(128 * part, 128 * part + 128)
            for k in (2, 1, 3, 0):
                term = nn(lt[k, rows, :], fac[part, :, cols])
                if k:
                    prod[k, q, rows, :] = term.astype(BF16)
                else:
                    own[q, rows, :] = term

    def send_ahead(q):
        base = ids(4)
        ahead.append([
            rdma(prod.at[2, q, upper, :], ra1.at[q], base, right_x, y),
            rdma(prod.at[2, q, lower, :], rb1.at[q], base + 1, left_x, y),
            rdma(prod.at[1, q, lower, :], rb_left.at[q], base + 2, right_x, y),
            rdma(prod.at[3, q, upper, :], ra_right.at[q], base + 3, left_x, y),
        ])
        for copy in ahead[q]:
            copy.start()

    def send_later(q):
        base = ids(2)
        later.append([
            rdma(prod.at[1, q, upper, :], ra_left.at[q], base, right_x, y),
            rdma(prod.at[3, q, lower, :], rb_right.at[q], base + 1, left_x, y),
        ])
        ahead[q][0].wait_recv()
        prod[1, q, upper, :] = (prod[1, q, upper, :].astype(F32) + ra1[q].astype(F32)).astype(BF16)
        later[q][0].start()
        ahead[q][1].wait_recv()
        prod[3, q, lower, :] = (prod[3, q, lower, :].astype(F32) + rb1[q].astype(F32)).astype(BF16)
        later[q][1].start()

    def send_along(q):
        for copy in ahead[q][2:] + later[q]:
            copy.wait_recv()
        a = own[q, upper, :] + ra_left[q].astype(F32) + ra_right[q].astype(F32)
        b = own[q, lower, :] + rb_left[q].astype(F32) + rb_right[q].astype(F32)
        total[q, upper, :] = a
        total[q, lower, :] = b
        zs[q, upper, :] = a.astype(BF16)
        zs[q, lower, :] = b.astype(BF16)
        base = ids(2 * zn)
        for o in range(1, zn):
            to = lax.rem(z + o, zn)
            dev = to * PLANE + me
            up_rows = pl.ds(pl.multiple_of(ru * jnp.minimum(to, zh - 1), 16), ru)
            down_rows = pl.ds(pl.multiple_of(128 + rd * to, 16), rd)
            c_down = rdma(zs.at[q, down_rows, :], zd.at[q, o - 1], base + o, dev, y)
            c_up = rdma(zs.at[q, up_rows, :], zu.at[q, o - 1], base + zn + o, dev, y)
            c_pad = rdma(zs.at[q, 256:PIECE, :], zv.at[q, o - 1], base + zn + o, dev, y)
            pl.when(to < zh)(c_up.start)
            pl.when(to >= zh)(c_pad.start)
            c_down.start()
            along.append((q, to, c_down, c_up, c_pad))

    def reduce_share():
        for copy in share1:
            copy.wait_recv()
        summed = groups[my_rows, :] + partial[my_rows, :]
        for o in range(1, yn):
            summed = summed + ar1[o - 1].astype(F32)
        io[my_rows, :] = summed.astype(BF16)
        for copy in share2:
            copy.start()

    def mix():
        for copy in from2:
            copy.wait_recv()

        def some(c, carry):
            rows = pl.ds(pl.multiple_of(c * Q, Q), Q)
            both = io[...]
            spread = nn(mct[rows, :], jnp.concatenate([both, both], axis=0))
            mixed[rows, :] = (encoded[rows, :].astype(F32) + spread).astype(BF16)
            return carry

        lax.fori_loop(0, CHUNKS, some, 0)

    multiply(0)
    send_ahead(0)
    multiply(1)
    send_ahead(1)
    reduce_share()
    send_later(0)
    for q in range(2, NQ):
        multiply(q)
        send_ahead(q)
        send_later(q - 1)
        if q == 2:
            mix()
        send_along(q - 2)
    send_later(NQ - 1)
    send_along(NQ - 2)
    send_along(NQ - 1)

    pad_part = pad_col[pl.ds(pl.multiple_of(ru * jnp.maximum(seq - sn // 2, 0), 16), ru), 0:1]
    for q in range(NQ):
        cols = slice(q * W, (q + 1) * W)
        for at, to, c_down, c_up, c_pad in along:
            if at == q:
                c_down.wait_recv()
                pl.when(z < zh)(c_up.wait_recv)
                pl.when(z >= zh)(c_pad.wait_recv)
        down_sum = total[q, pl.ds(pl.multiple_of(128 + rd * z, 16), rd), :]
        for o in range(zn - 1):
            down_sum = down_sum + zd[q, o].astype(F32)
        down_out[:, cols] = down_sum

        @pl.when(z < zh)
        def _():
            up_sum = total[q, pl.ds(pl.multiple_of(ru * jnp.minimum(z, zh - 1), 16), ru), :]
            for o in range(zn - 1):
                up_sum = up_sum + zu[q, o].astype(F32)
            up_out[:, cols] = up_sum

        @pl.when(z >= zh)
        def _():
            pad_sum = total[q, 256:257, :]
            for o in range(zn - 1):
                pad_sum = pad_sum + zv[q, o, 0:1, :].astype(F32)
            up_out[:, cols] = pad_part * pad_sum

    for copy in step1 + step3 + swaps + share1 + share2:
        copy.wait_send()
    for o in range(1, zn):
        pl.when(z + o < zn)(step2[o].wait_send)
    for q in range(NQ):
        for copy in ahead[q] + later[q]:
            copy.wait_send()
    for q, to, c_down, c_up, c_pad in along:
        c_down.wait_send()
        pl.when(to < zh)(c_up.wait_send)
        pl.when(to >= zh)(c_pad.wait_send)


def on_device(
    zn, yn, tokens, positions, value_proj, write_proj, read_proj, step_proj, step_bias, decay_rate, reset_depth,
    out_proj, router, pad_vector, up_weight, down_weight, cotangent,
):
    sn = zn * PLANE
    ru, rd, qw = 2 * D // sn, D // sn, D // yn
    n_pos = positions.shape[0]
    vm = pltpu.VMEM
    n_sem = PLANE + zn + PLANE * yn + 4 + 2 * yn + NQ * (6 + 2 * zn)
    scratch = [
        vm((ROWS, D), BF16), vm((1, n_pos), jnp.int32), vm((D, D), BF16), vm((D, 2 * NS), BF16), vm((D, HEADS), BF16),
        vm((1, HEADS), F32), vm((1, HEADS), F32), vm((1, ROWS), F32), vm((D, D), BF16), vm((1, D), F32),
        vm((1, D), BF16), vm((2 * D, D), BF16), vm((D, D), BF16), vm((ROWS, D), BF16),
        vm((ROWS, D), BF16), vm((ROWS, 2 * NS), BF16), vm((ROWS, D), BF16), vm((CHUNKS, Q, Q), F32),
        vm((CHUNKS, Q, Q), F32), vm((2 * Q, D), BF16), vm((ROWS, D), BF16), vm((ROWS, D), F32), vm((NS, D), F32),
        vm((CHUNKS, NS, D), F32), vm((CHUNKS + 1, 8, D), F32), vm((ROWS, D), F32),
        vm((PLANE, 32, qw), BF16), vm((PLANE, 32, qw), BF16), vm((32, qw), BF16), vm((zn, 32, qw), BF16),
        vm((PLANE, 16, qw), BF16), vm((NS, D), BF16),
        vm((ROWS, D), BF16), vm((SLOTS, D), F32), vm((SLOTS, ROWS), BF16), vm((ROWS, 2 * SLOTS), BF16),
        vm((16, D), F32), vm((D, 128), F32), vm((8, 128), F32),
        vm((SLOTS, D), BF16), vm((SLOTS, D), BF16), vm((SLOTS, 128), F32), vm((SLOTS, D), F32),
        vm((2, 2 * SLOTS, D), BF16), vm((D, SLOTS), BF16), vm((XN, 256, 2 * SLOTS), BF16), vm((XN, 256, SLOTS), BF16),
        vm((8, D), F32), vm((8, D), F32),
        vm((SLOTS, D), F32), vm((SLOTS, D), BF16), vm((max(yn - 1, 1), SLOTS // yn, D), BF16), vm((SLOTS, D), BF16),
        vm((NQ, PIECE, W), F32), vm((XN, NQ, PIECE, W), BF16), vm((NQ, 128, W), BF16), vm((NQ, 144, W), BF16),
        vm((NQ, 128, W), BF16), vm((NQ, 128, W), BF16), vm((NQ, 144, W), BF16), vm((NQ, 144, W), BF16),
        vm((NQ, PIECE, W), F32), vm((NQ, PIECE, W), BF16), vm((NQ, zn - 1, rd, W), BF16), vm((NQ, zn - 1, ru, W), BF16),
        vm((NQ, zn - 1, 16, W), BF16),
        pltpu.SemaphoreType.DMA((15,)), pltpu.SemaphoreType.DMA((n_sem,)), pltpu.SemaphoreType.DMA((n_sem,)),
    ]
    return pl.pallas_call(
        functools.partial(kernel, zn, yn),
        out_shape=(
            jax.ShapeDtypeStruct((ROWS, D), BF16),
            jax.ShapeDtypeStruct((ru, D), F32),
            jax.ShapeDtypeStruct((rd, D), F32),
        ),
        in_specs=[pl.BlockSpec(memory_space=pl.ANY)] * 15,
        out_specs=(pl.BlockSpec(memory_space=pltpu.VMEM),) * 3,
        scratch_shapes=scratch,
        compiler_params=pltpu.CompilerParams(
            collective_id=0, has_side_effects=True, vmem_limit_bytes=60 * 2**20
        ),
    )(
        tokens, positions.reshape(1, n_pos), value_proj, write_proj, read_proj, step_proj, step_bias.reshape(1, HEADS),
        decay_rate.reshape(1, HEADS), reset_depth.reshape(1, ROWS), out_proj, router.reshape(1, D),
        pad_vector.reshape(1, D), up_weight, down_weight, cotangent,
    )


def solution(mesh):
    placed = (
        P("seq", None), P(), P(), P(), P(), P(), P(), P(), P("seq"), P(), P(), P(),
        P(None, "mlp"), P(None, "mlp"), P("seq", None),
    )
    return jax.shard_map(
        functools.partial(on_device, mesh.shape["seq"] // PLANE, mesh.shape["mlp"]),
        mesh=mesh,
        in_specs=placed,
        out_specs=(P("seq", None), P("seq", "mlp"), P("seq", "mlp")),
        check_vma=False,
    )
```

```python
import functools

import jax
import jax.numpy as jnp
from jax import lax
from jax.experimental import pallas as pl
from jax.experimental.pallas import tpu as pltpu
from jax.sharding import PartitionSpec as P

F32, BF16 = jnp.float32, jnp.bfloat16
HIGHEST = lax.Precision.HIGHEST
MESH = pl.DeviceIdType.MESH

ROWS = 512
D = 1024
HEADS = 16
HEAD = 64
NS = 128
Q = 128
CHUNKS = ROWS // Q
SLOTS = 128
XN, CN = 4, 2
PLANE = XN * CN
NQ = 4
W = D // NQ
PIECE = 272
EPS = 1e-05
G0, G1 = 0.7978845608028654, 0.044715


def nn(a, b):
    return jnp.dot(a, b, preferred_element_type=F32)


def nt(a, b):
    return lax.dot_general(a, b, (((1,), (1,)), ((), ())), preferred_element_type=F32)


def split3(x):
    hi = x.astype(BF16).astype(F32)
    mid = (x - hi).astype(BF16).astype(F32)
    return hi, mid, x - hi - mid


def in_rows(parts, shape):
    ids = lax.broadcasted_iota(jnp.int32, shape, 0)
    block = jnp.zeros(shape, F32)
    for i, part in enumerate(parts):
        block = jnp.where(ids == i, part, block)
    return block


def kernel(
    zn, yn,
    tokens, positions, value_proj, write_proj, read_proj, step_proj, step_bias, decay_rate, reset_depth,
    out_proj, router, pad_vector, up_weight, down_weight, cotangent,
    encoded_out, mct_out, io_out, up_out, down_out,
    tok, pos, vp, wr, sp, bias, rate, reset, op, rout, pad, up, down, cot,
    normed, kr, vals, zrow, zcol, expander, dtv, ece, state, chunk_state, dpre, within,
    p1s, p1r, p2s, p2r, p3s, incoming,
    encoded, groups, select, mct, padup, pad_col, padsq,
    xn, gg, scale, slope, fac, turned, lt, lto, vx, vr,
    partial, ars, ar1, io,
    own, prod, ra1, rb1, ra_left, ra_right, rb_left, rb_right, total, zs, zd, zu, zv,
    load, store, ss, rs,
):
    sn = zn * PLANE
    ru, rd = 2 * D // sn, D // sn
    zh = zn // 2
    qw = D // yn
    seq, y = lax.axis_index("seq"), lax.axis_index("mlp")
    z, me = seq // PLANE, lax.rem(seq, PLANE)
    x, core = me // CN, lax.rem(me, CN)

    def plane_at(j):
        return z * PLANE + j

    pairs = [
        (tokens, tok), (write_proj, wr.at[:, 0:NS]), (read_proj, wr.at[:, NS : 2 * NS]), (step_proj, sp),
        (step_bias, bias), (decay_rate, rate), (reset_depth, reset), (value_proj, vp), (positions, pos),
        (pad_vector, pad), (out_proj, op), (router, rout), (up_weight, up), (cotangent, cot), (down_weight, down),
    ]
    loads = [pltpu.make_async_copy(a, b, load.at[i]) for i, (a, b) in enumerate(pairs)]
    for copy in loads[:8]:
        copy.start()

    barrier = pltpu.get_barrier_semaphore()
    peers = 0
    for oy in range(yn):
        for o in range(PLANE):
            if o or oy:
                peers += 1
                pl.semaphore_signal(
                    barrier, inc=1, device_id_type=MESH,
                    device_id=(plane_at(lax.rem(me + o, PLANE)), lax.rem(y + oy, yn)),
                )
    for o in range(1, zn):
        peers += 1
        pl.semaphore_signal(
            barrier, inc=1, device_id_type=MESH, device_id=(lax.rem(z + o, zn) * PLANE + me, y)
        )

    count = [0]

    def ids(n):
        count[0] += n
        return count[0] - n

    def rdma(src, dst, i, to_seq, to_y):
        return pltpu.make_async_remote_copy(
            src_ref=src, dst_ref=dst, send_sem=ss.at[i], recv_sem=rs.at[i],
            device_id=(to_seq, to_y), device_id_type=MESH,
        )

    step1, step2, step3, from3, swaps, share1, share2, from2 = [], [None], [], [], [], [], [], []
    ahead, later, along = [], [], []

    for copy in loads[:7]:
        copy.wait()

    def norm(b, carry):
        rows = pl.ds(pl.multiple_of(b * Q, Q), Q)
        field = tok[rows, :].astype(F32)
        ms = jnp.mean(field * field, axis=-1, keepdims=True)
        normed[rows, :] = (field * lax.rsqrt(ms + EPS)).astype(BF16)
        return carry

    lax.fori_loop(0, CHUNKS, norm, 0)
    e_row = lax.rem(lax.broadcasted_iota(jnp.int32, (2 * Q, D), 0), HEADS)
    e_col = lax.broadcasted_iota(jnp.int32, (2 * Q, D), 1) // HEAD
    expander[...] = (e_row == e_col).astype(F32).astype(BF16)

    eye = lax.broadcasted_iota(jnp.int32, (HEADS, HEADS), 0) == lax.broadcasted_iota(jnp.int32, (HEADS, HEADS), 1)

    def column(row):
        return jnp.sum(jnp.where(eye, jnp.broadcast_to(row, (HEADS, HEADS)), 0.0), axis=1, keepdims=True)

    kr[...] = nn(normed[...], wr[...]).astype(BF16)
    raw = nt(sp[...], normed[...]) + column(bias[...])
    dt_all = jnp.maximum(raw, 0.0) + jnp.log1p(jnp.exp(-jnp.abs(raw)))
    ld_all = -dt_all * column(rate[...]) - reset[...]
    s_id = lax.broadcasted_iota(jnp.int32, (Q, Q), 0)
    t_id = lax.broadcasted_iota(jnp.int32, (Q, Q), 1)
    before = (s_id <= t_id).astype(F32)
    for c in range(CHUNKS):
        cols = slice(c * Q, (c + 1) * Q)
        dt = dt_all[:, cols]
        cum = jnp.dot(ld_all[:, cols], before, precision=HIGHEST, preferred_element_type=F32)
        tail = jnp.exp(cum[:, Q - 1 : Q] - cum) * dt
        block = jnp.concatenate([dt, cum, tail, jnp.exp(cum), jnp.zeros((64, Q), F32)], axis=0)
        zrow[c] = block
        zcol[c] = block.T
    loads[7].wait()
    for copy in loads[8:]:
        copy.start()

    def values(b, carry):
        rows = pl.ds(pl.multiple_of(b * 256, 256), 256)
        vals[rows, :] = nn(normed[rows, :], vp[...]).astype(BF16)
        return carry

    lax.fori_loop(0, ROWS // 256, values, 0)

    state[...] = jnp.zeros_like(state)

    def chunk(c, decay):
        rows = pl.ds(pl.multiple_of(c * Q, Q), Q)
        zt = zcol[c]
        hi, mid, unused = split3(zt)
        kind = lax.broadcasted_iota(jnp.int32, (Q, Q), 1) // HEADS

        def expand(k):
            lhs = jnp.concatenate([jnp.where(kind == k, hi, 0.0), jnp.where(kind == k, mid, 0.0)], axis=1)
            return nn(lhs.astype(BF16), expander[...])

        v = vals[rows, :].astype(F32)
        dtv[rows, :] = (expand(0) * v).astype(BF16)
        weighted = (expand(2) * v).astype(BF16)
        grown = expand(3)
        ece[rows, :] = grown
        keys_t = kr[rows, 0:NS].astype(F32).T.astype(BF16)
        old = state[...]
        chunk_state[c] = old
        dpre[c] = jnp.broadcast_to(decay, (8, D))
        last = grown[Q - 1 : Q, :]
        state[...] = last * old + nn(keys_t, weighted)
        return decay * last

    decay = lax.fori_loop(0, CHUNKS, chunk, jnp.ones((1, D), F32))

    dpre[CHUNKS] = jnp.broadcast_to(decay, (8, D))
    mine = pl.ds(pl.multiple_of(y * qw, qw), qw)
    decay_rows = in_rows(split3(dpre[CHUNKS, 0:1, mine]), (16, qw)).astype(BF16)
    for j in range(PLANE):
        p1s[j, 0:16, :] = state[16 * j : 16 * j + 16, mine].astype(BF16)
        p1s[j, 16:32, :] = decay_rows
    p1r[0] = p1s[me]
    pl.semaphore_wait(barrier, peers)
    base = ids(PLANE)
    for o in range(1, PLANE):
        j = lax.rem(me + o, PLANE)
        step1.append(rdma(p1s.at[j], p1r.at[o], base + o, plane_at(j), y))
        step1[-1].start()

    def intra(c, carry):
        rows = pl.ds(pl.multiple_of(c * Q, Q), Q)
        scores = nt(kr[rows, NS : 2 * NS], kr[rows, 0:NS])
        scores = jnp.where(s_id >= t_id, scores, 0.0)
        first = lax.broadcasted_iota(jnp.int32, (Q, 2 * HEAD), 1) < HEAD
        zr, zt = zrow[c], zcol[c]
        for pair in range(HEADS // 2):
            lanes = slice(2 * HEAD * pair, 2 * HEAD * (pair + 1))
            both = dtv[rows, lanes].astype(F32)
            right = jnp.concatenate([jnp.where(first, both, 0.0), jnp.where(first, 0.0, both)], axis=0)
            mixing = []
            for h in (2 * pair, 2 * pair + 1):
                gap = zt[:, HEADS + h : HEADS + h + 1] - zr[HEADS + h : HEADS + h + 1, :]
                mixing.append(scores * jnp.exp(jnp.minimum(gap, 0.0)))
            within[rows, lanes] = nn(jnp.concatenate(mixing, axis=1).astype(BF16), right.astype(BF16))
        return carry

    lax.fori_loop(0, CHUNKS // 2, intra, 0)

    def read(block):
        block = block.astype(F32)
        return block[0:16], block[16:17] + block[17:18] + block[18:19]

    for copy in step1:
        copy.wait_recv()
    pre, pre_decay = [jnp.zeros((16, qw), F32)], [jnp.ones((1, qw), F32)]
    for k in range(PLANE):
        new, by = read(p1r[lax.rem(me - k + PLANE, PLANE)])
        pre.append(by * pre[-1] + new)
        pre_decay.append(by * pre_decay[-1])
    p2s[0:16, :] = pre[-1].astype(BF16)
    p2s[16:32, :] = in_rows(split3(pre_decay[-1]), (16, qw)).astype(BF16)
    p2r[0] = p2s[...]
    base = ids(zn)
    for o in range(1, zn):
        step2.append(rdma(p2s, p2r.at[o], base + o, lax.rem(z + o, zn) * PLANE + me, y))
        pl.when(z + o < zn)(step2[o].start)

    lax.fori_loop(CHUNKS // 2, CHUNKS, intra, 0)

    for o in range(1, zn):
        pl.when(z >= o)(step2[o].wait_recv)
    start = jnp.zeros((16, qw), F32)
    for k in range(zn - 1):
        new, by = read(p2r[jnp.maximum(z - k, 0)])
        start = jnp.where(k < z, by * start + new, start)
    for k in range(PLANE):
        p3s[k] = (pre_decay[k] * start + pre[k]).astype(BF16)

    def landing(j, at_y):
        return incoming.at[pl.ds(pl.multiple_of(j * 16, 16), 16), pl.ds(pl.multiple_of(at_y * qw, qw), qw)]

    base = ids(PLANE * yn)
    for o in range(PLANE):
        for oy in range(yn):
            if o or oy:
                i = base + o * yn + oy
                j, at_y = lax.rem(me + o, PLANE), lax.rem(y + oy, yn)
                step3.append(rdma(p3s.at[j], landing(me, y), i, plane_at(j), at_y))
                step3[-1].start()
                j, at_y = lax.rem(me - o + PLANE, PLANE), lax.rem(y - oy + yn, yn)
                from3.append(rdma(p3s.at[j], landing(j, at_y), i, plane_at(j), at_y))
    incoming[pl.ds(pl.multiple_of(me * 16, 16), 16), mine] = p3s[me]

    for copy in loads[8:]:
        copy.wait()
    local = pos[...] - seq * ROWS
    n_pos = local.shape[1]
    high, low = local >> 7, local & 127
    ids8 = lax.broadcasted_iota(jnp.int32, (8, n_pos), 0)
    left = jnp.where((jnp.broadcast_to(high, (8, n_pos)) == ids8) & (ids8 < CHUNKS), 1.0, 0.0).astype(BF16)
    ids128 = lax.broadcasted_iota(jnp.int32, (Q, n_pos), 0)
    right = jnp.where(jnp.broadcast_to(low, (Q, n_pos)) == ids128, 1.0, 0.0).astype(BF16)
    marks = nt(left, right)
    running = nn(marks.astype(BF16), before.astype(BF16))
    parts, so_far = [], jnp.zeros((1, 1), F32)
    for c in range(CHUNKS):
        parts.append(running[c : c + 1] + so_far)
        so_far = parts[-1][:, Q - 1 : Q]
    group_of = jnp.concatenate(parts, axis=1) - 1.0
    mark = jnp.concatenate([marks[c : c + 1] for c in range(CHUNKS)], axis=1)
    slot = lax.broadcasted_iota(jnp.int32, (SLOTS, ROWS), 0).astype(F32)
    member = jnp.where(slot == group_of, 1.0, 0.0)
    select[...] = (member * mark).astype(BF16)
    pad_rows = pad[...].astype(F32)
    pad_row = jnp.concatenate([pad_rows[i : i + 1] for i in range(8)], axis=1)
    padsq[...] = jnp.broadcast_to(jnp.sum(pad_row * pad_row, axis=-1, keepdims=True), (8, 128))
    pad_col[...] = jnp.broadcast_to(pad_row, (128, D)).T
    padup[...] = nn(jnp.broadcast_to(pad_row, (16, D)).astype(BF16), up[D : 2 * D, :])

    for copy in from3:
        copy.wait_recv()

    def encode(b, carry):
        for k in range(2):
            c = 2 * b + k
            rows = pl.ds(pl.multiple_of(c * Q, Q), Q)
            full = chunk_state[c] + dpre[c, 0:1, :] * incoming[...].astype(F32)
            carried = nn(kr[rows, NS : 2 * NS], full.astype(BF16))
            scanned = within[rows, :] + ece[rows, :] * carried
            ms = jnp.mean(scanned * scanned, axis=-1, keepdims=True)
            normed[rows, :] = (scanned * lax.rsqrt(ms + EPS)).astype(BF16)
        rows = pl.ds(pl.multiple_of(b * 256, 256), 256)
        encoded[rows, :] = (tok[rows, :].astype(F32) + nn(normed[rows, :], op[...])).astype(BF16)
        return carry

    lax.fori_loop(0, 2, encode, 0)
    logits = nt(in_rows(split3(rout[...]), (16, D)).astype(BF16), encoded[...])
    confidence = 1.0 / (1.0 + jnp.exp(-jnp.sum(logits, axis=0, keepdims=True)))
    weight = member * confidence
    weight_hi = weight.astype(BF16)
    weight_lo = (weight - weight_hi.astype(F32)).astype(BF16)
    mct[:, 0:SLOTS] = weight_hi.astype(F32).T.astype(BF16)
    mct[:, SLOTS : 2 * SLOTS] = weight_lo.astype(F32).T.astype(BF16)
    stores = [pltpu.make_async_copy(encoded, encoded_out, store.at[0]), pltpu.make_async_copy(mct, mct_out, store.at[1])]
    for copy in stores:
        copy.start()
    groups[...] = nn(select[...], encoded[...])
    grads = nn(weight_hi, cot[...]) + nn(weight_lo, cot[...])
    gg[...] = grads.astype(BF16)
    rows_f = groups[...]
    ms = (jnp.sum(rows_f * rows_f, axis=-1, keepdims=True) + padsq[0:1, 0:1]) * (0.5 / D)
    r = lax.rsqrt(ms + EPS)
    scale[...] = jnp.broadcast_to(r, (SLOTS, 128))
    inner = rows_f * r
    xn[...] = inner.astype(BF16)

    def turn(field, first_row, each, blocks):
        turned[...] = field.T.astype(BF16)
        for k in range(XN):
            at = lax.rem(x + k, XN)
            for b in range(blocks):
                rows = slice(first_row + b * each, first_row + (b + 1) * each)
                begin = (b * PLANE + at * CN + core) * each
                lt[k, rows, 0:SLOTS] = turned[pl.ds(pl.multiple_of(begin, 16), each), :]
                begin = (b * PLANE + at * CN + 1 - core) * each
                lto[k, rows, :] = turned[pl.ds(pl.multiple_of(begin, 16), each), :]

    turn(inner, 0, ru, zh)
    turn(grads, 128, rd, zn)
    mate = plane_at(x * CN + 1 - core)
    base = ids(4)
    swaps += [
        rdma(lto, lt.at[:, :, SLOTS : 2 * SLOTS], base, mate, y),
        rdma(fac.at[1, 0:SLOTS, :], fac.at[1, SLOTS : 2 * SLOTS, :], base + 1, mate, y),
        rdma(fac.at[0, 0:SLOTS, :], fac.at[0, SLOTS : 2 * SLOTS, :], base + 2, mate, y),
        rdma(vx, vr, base + 3, mate, y),
    ]
    swaps[0].start()

    def forward(b, carry):
        cols = pl.ds(pl.multiple_of(b * 256, 256), 256)
        pre_act = nn(xn[...], up[0:D, cols]) + scale[:, 0:1] * padup[0:1, cols]
        square = pre_act * pre_act
        bend = jnp.tanh(G0 * pre_act * (1.0 + G1 * square))
        fac[1, 0:SLOTS, cols] = (0.5 * pre_act * (1.0 + bend)).astype(BF16)
        slope[:, cols] = 0.5 * (1.0 + bend) + 0.5 * pre_act * (1.0 - bend * bend) * (
            G0 * (1.0 + 3.0 * G1 * square)
        )
        return carry

    lax.fori_loop(0, 4, forward, 0)
    swaps[1].start()

    def backward(b, carry):
        cols = pl.ds(pl.multiple_of(b * 256, 256), 256)
        pre_grad = (nn(gg[...], down[:, cols]) * slope[:, cols]).astype(BF16)
        fac[0, 0:SLOTS, cols] = pre_grad
        pad_term = jnp.sum(pre_grad.astype(F32) * scale[:, 0:1], axis=0, keepdims=True)
        vx[:, cols] = jnp.broadcast_to(pad_term, (8, 256))
        return carry

    lax.fori_loop(0, 4, backward, 0)
    swaps[2].start()
    swaps[3].start()

    rq = SLOTS // yn
    partial[...] = nt(fac[1, 0:SLOTS, :], down[...])
    ars[...] = partial[...].astype(BF16)
    base = ids(2 * yn)
    my_rows = pl.ds(pl.multiple_of(y * rq, rq), rq)
    for o in range(1, yn):
        at_y = lax.rem(y + o, yn)
        share1.append(rdma(ars.at[pl.ds(pl.multiple_of(at_y * rq, rq), rq), :], ar1.at[o - 1], base + o, seq, at_y))
        share1[-1].start()
        share2.append(rdma(io.at[my_rows, :], io.at[my_rows, :], base + yn + o, seq, at_y))
        at_y = lax.rem(y - o + yn, yn)
        other = pl.ds(pl.multiple_of(at_y * rq, rq), rq)
        from2.append(rdma(io.at[other, :], io.at[other, :], base + yn + o, seq, at_y))

    for copy in swaps:
        copy.wait_recv()
    right_x = plane_at(lax.rem(x + 1, XN) * CN + core)
    left_x = plane_at(lax.rem(x + XN - 1, XN) * CN + core)
    upper, lower = slice(0, 128), slice(128, PIECE)
    def multiply(q):
        cols = slice(q * W, (q + 1) * W)
        pad_rows = in_rows([vx[0:1, cols] + vr[0:1, cols]], (16, W))
        own[q, 256:PIECE, :] = pad_rows
        for k in range(1, XN):
            prod[k, q, 256:PIECE, :] = pad_rows.astype(BF16)
        for part in range(2):
            rows = slice(128 * part, 128 * part + 128)
            for k in (2, 1, 3, 0):
                term = nn(lt[k, rows, :], fac[part, :, cols])
                if k:
                    prod[k, q, rows, :] = term.astype(BF16)
                else:
                    own[q, rows, :] = term

    def send_ahead(q):
        base = ids(4)
        ahead.append([
            rdma(prod.at[2, q, upper, :], ra1.at[q], base, right_x, y),
            rdma(prod.at[2, q, lower, :], rb1.at[q], base + 1, left_x, y),
            rdma(prod.at[1, q, lower, :], rb_left.at[q], base + 2, right_x, y),
            rdma(prod.at[3, q, upper, :], ra_right.at[q], base + 3, left_x, y),
        ])
        for copy in ahead[q]:
            copy.start()

    def send_later(q):
        base = ids(2)
        later.append([
            rdma(prod.at[1, q, upper, :], ra_left.at[q], base, right_x, y),
            rdma(prod.at[3, q, lower, :], rb_right.at[q], base + 1, left_x, y),
        ])
        ahead[q][0].wait_recv()
        prod[1, q, upper, :] = (prod[1, q, upper, :].astype(F32) + ra1[q].astype(F32)).astype(BF16)
        later[q][0].start()
        ahead[q][1].wait_recv()
        prod[3, q, lower, :] = (prod[3, q, lower, :].astype(F32) + rb1[q].astype(F32)).astype(BF16)
        later[q][1].start()

    def send_along(q):
        for copy in ahead[q][2:] + later[q]:
            copy.wait_recv()
        a = own[q, upper, :] + ra_left[q].astype(F32) + ra_right[q].astype(F32)
        b = own[q, lower, :] + rb_left[q].astype(F32) + rb_right[q].astype(F32)
        total[q, upper, :] = a
        total[q, lower, :] = b
        zs[q, upper, :] = a.astype(BF16)
        zs[q, lower, :] = b.astype(BF16)
        base = ids(2 * zn)
        for o in range(1, zn):
            to = lax.rem(z + o, zn)
            dev = to * PLANE + me
            up_rows = pl.ds(pl.multiple_of(ru * jnp.minimum(to, zh - 1), 16), ru)
            down_rows = pl.ds(pl.multiple_of(128 + rd * to, 16), rd)
            c_down = rdma(zs.at[q, down_rows, :], zd.at[q, o - 1], base + o, dev, y)
            c_up = rdma(zs.at[q, up_rows, :], zu.at[q, o - 1], base + zn + o, dev, y)
            c_pad = rdma(zs.at[q, 256:PIECE, :], zv.at[q, o - 1], base + zn + o, dev, y)
            pl.when(to < zh)(c_up.start)
            pl.when(to >= zh)(c_pad.start)
            c_down.start()
            along.append((q, to, c_down, c_up, c_pad))

    def reduce_share():
        for copy in share1:
            copy.wait_recv()
        summed = groups[my_rows, :] + partial[my_rows, :]
        for o in range(1, yn):
            summed = summed + ar1[o - 1].astype(F32)
        io[my_rows, :] = summed.astype(BF16)
        for copy in share2:
            copy.start()

    def share():
        for copy in from2:
            copy.wait_recv()
        stores.append(pltpu.make_async_copy(io, io_out, store.at[2]))
        stores[2].start()

    multiply(0)
    send_ahead(0)
    multiply(1)
    send_ahead(1)
    reduce_share()
    send_later(0)
    for q in range(2, NQ):
        multiply(q)
        send_ahead(q)
        send_later(q - 1)
        if q == 2:
            share()
        send_along(q - 2)
    send_later(NQ - 1)
    send_along(NQ - 2)
    send_along(NQ - 1)

    pad_part = pad_col[pl.ds(pl.multiple_of(ru * jnp.maximum(seq - sn // 2, 0), 16), ru), 0:1]
    for q in range(NQ):
        cols = slice(q * W, (q + 1) * W)
        for at, to, c_down, c_up, c_pad in along:
            if at == q:
                c_down.wait_recv()
                pl.when(z < zh)(c_up.wait_recv)
                pl.when(z >= zh)(c_pad.wait_recv)
        down_sum = total[q, pl.ds(pl.multiple_of(128 + rd * z, 16), rd), :]
        for o in range(zn - 1):
            down_sum = down_sum + zd[q, o].astype(F32)
        down_out[:, cols] = down_sum

        @pl.when(z < zh)
        def _():
            up_sum = total[q, pl.ds(pl.multiple_of(ru * jnp.minimum(z, zh - 1), 16), ru), :]
            for o in range(zn - 1):
                up_sum = up_sum + zu[q, o].astype(F32)
            up_out[:, cols] = up_sum

        @pl.when(z >= zh)
        def _():
            pad_sum = total[q, 256:257, :]
            for o in range(zn - 1):
                pad_sum = pad_sum + zv[q, o, 0:1, :].astype(F32)
            up_out[:, cols] = pad_part * pad_sum

    for copy in stores:
        copy.wait()
    for copy in step1 + step3 + swaps + share1 + share2:
        copy.wait_send()
    for o in range(1, len(step2)):
        pl.when(z + o < zn)(step2[o].wait_send)
    for copies in ahead + later:
        for copy in copies:
            copy.wait_send()
    for q, to, c_down, c_up, c_pad in along:
        c_down.wait_send()
        pl.when(to < zh)(c_up.wait_send)
        pl.when(to >= zh)(c_pad.wait_send)


def finish(encoded, mct, io, up_sum, down_sum, mixed, up_out, down_out):
    both = io[...]
    spread = nn(mct[...], jnp.concatenate([both, both], axis=0))
    mixed[...] = (encoded[...].astype(F32) + spread).astype(BF16)
    up_out[...] = up_sum[...]
    down_out[...] = down_sum[...]


def on_device(
    zn, yn, tokens, positions, value_proj, write_proj, read_proj, step_proj, step_bias, decay_rate, reset_depth,
    out_proj, router, pad_vector, up_weight, down_weight, cotangent,
):
    sn = zn * PLANE
    ru, rd, qw = 2 * D // sn, D // sn, D // yn
    n_pos = positions.shape[0]
    vm = pltpu.VMEM
    n_sem = PLANE + zn + PLANE * yn + 4 + 2 * yn + NQ * (6 + 2 * zn)
    scratch = [
        vm((ROWS, D), BF16), vm((1, n_pos), jnp.int32), vm((D, D), BF16), vm((D, 2 * NS), BF16), vm((HEADS, D), BF16),
        vm((1, HEADS), F32), vm((1, HEADS), F32), vm((1, ROWS), F32), vm((D, D), BF16), vm((1, D), F32),
        vm((8, D // 8), BF16), vm((2 * D, D), BF16), vm((D, D), BF16), vm((ROWS, D), BF16),
        vm((ROWS, D), BF16), vm((ROWS, 2 * NS), BF16), vm((ROWS, D), BF16), vm((CHUNKS, Q, Q), F32),
        vm((CHUNKS, Q, Q), F32), vm((2 * Q, D), BF16), vm((ROWS, D), BF16), vm((ROWS, D), F32), vm((NS, D), F32),
        vm((CHUNKS, NS, D), F32), vm((CHUNKS + 1, 8, D), F32), vm((ROWS, D), F32),
        vm((PLANE, 32, qw), BF16), vm((PLANE, 32, qw), BF16), vm((32, qw), BF16), vm((zn, 32, qw), BF16),
        vm((PLANE, 16, qw), BF16), vm((NS, D), BF16),
        vm((ROWS, D), BF16), vm((SLOTS, D), F32), vm((SLOTS, ROWS), BF16), vm((ROWS, 2 * SLOTS), BF16),
        vm((16, D), F32), vm((D, 128), F32), vm((8, 128), F32),
        vm((SLOTS, D), BF16), vm((SLOTS, D), BF16), vm((SLOTS, 128), F32), vm((SLOTS, D), F32),
        vm((2, 2 * SLOTS, D), BF16), vm((D, SLOTS), BF16), vm((XN, 256, 2 * SLOTS), BF16), vm((XN, 256, SLOTS), BF16),
        vm((8, D), F32), vm((8, D), F32),
        vm((SLOTS, D), F32), vm((SLOTS, D), BF16), vm((max(yn - 1, 1), SLOTS // yn, D), BF16), vm((SLOTS, D), BF16),
        vm((NQ, PIECE, W), F32), vm((XN, NQ, PIECE, W), BF16), vm((NQ, 128, W), BF16), vm((NQ, 144, W), BF16),
        vm((NQ, 128, W), BF16), vm((NQ, 128, W), BF16), vm((NQ, 144, W), BF16), vm((NQ, 144, W), BF16),
        vm((NQ, PIECE, W), F32), vm((NQ, PIECE, W), BF16), vm((NQ, zn - 1, rd, W), BF16), vm((NQ, zn - 1, ru, W), BF16),
        vm((NQ, zn - 1, 16, W), BF16),
        pltpu.SemaphoreType.DMA((15,)), pltpu.SemaphoreType.DMA((3,)), pltpu.SemaphoreType.DMA((n_sem,)), pltpu.SemaphoreType.DMA((n_sem,)),
    ]
    encoded, mct, io, up_sum, down_sum = pl.pallas_call(
        functools.partial(kernel, zn, yn),
        out_shape=(
            jax.ShapeDtypeStruct((ROWS, D), BF16),
            jax.ShapeDtypeStruct((ROWS, 2 * SLOTS), BF16),
            jax.ShapeDtypeStruct((SLOTS, D), BF16),
            jax.ShapeDtypeStruct((ru, D), F32),
            jax.ShapeDtypeStruct((rd, D), F32),
        ),
        in_specs=[pl.BlockSpec(memory_space=pl.ANY)] * 15,
        out_specs=(pl.BlockSpec(memory_space=pl.ANY),) * 3 + (pl.BlockSpec(memory_space=pltpu.VMEM),) * 2,
        scratch_shapes=scratch,
        compiler_params=pltpu.CompilerParams(
            collective_id=0, has_side_effects=True, vmem_limit_bytes=60 * 2**20
        ),
    )(
        tokens, positions.reshape(1, n_pos), value_proj, write_proj, read_proj, step_proj.T, step_bias.reshape(1, HEADS),
        decay_rate.reshape(1, HEADS), reset_depth.reshape(1, ROWS), out_proj, router.reshape(1, D),
        pad_vector.reshape(8, D // 8), up_weight, down_weight, cotangent,
    )
    half = ROWS // 2
    return pl.pallas_call(
        finish,
        grid=(2,),
        out_shape=(
            jax.ShapeDtypeStruct((ROWS, D), BF16),
            jax.ShapeDtypeStruct((ru, D), F32),
            jax.ShapeDtypeStruct((rd, D), F32),
        ),
        in_specs=[
            pl.BlockSpec((half, D), lambda i: (i, 0)),
            pl.BlockSpec((half, 2 * SLOTS), lambda i: (i, 0)),
            pl.BlockSpec((SLOTS, D), lambda i: (0, 0)),
            pl.BlockSpec((ru // 2, D), lambda i: (i, 0)),
            pl.BlockSpec((rd // 2, D), lambda i: (i, 0)),
        ],
        out_specs=(
            pl.BlockSpec((half, D), lambda i: (i, 0)),
            pl.BlockSpec((ru // 2, D), lambda i: (i, 0)),
            pl.BlockSpec((rd // 2, D), lambda i: (i, 0)),
        ),
        compiler_params=pltpu.CompilerParams(vmem_limit_bytes=60 * 2**20),
    )(encoded, mct, io, up_sum, down_sum)


def solution(mesh):
    placed = (
        P("seq", None), P(), P(), P(), P(), P(), P(), P(), P("seq"), P(), P(), P(),
        P(None, "mlp"), P(None, "mlp"), P("seq", None),
    )
    return jax.shard_map(
        functools.partial(on_device, mesh.shape["seq"] // PLANE, mesh.shape["mlp"]),
        mesh=mesh,
        in_specs=placed,
        out_specs=(P("seq", None), P("seq", "mlp"), P("seq", "mlp")),
        check_vma=False,
    )
```

```python
import functools

import jax
import jax.numpy as jnp
from jax import lax
from jax.experimental import pallas as pl
from jax.experimental.pallas import tpu as pltpu
from jax.sharding import PartitionSpec as P

F32, BF16 = jnp.float32, jnp.bfloat16
HIGHEST = lax.Precision.HIGHEST
MESH = pl.DeviceIdType.MESH

ROWS = 512
D = 1024
HEADS = 16
HEAD = 64
NS = 128
Q = 128
CHUNKS = ROWS // Q
SLOTS = 128
XN, CN = 4, 2
PLANE = XN * CN
NQ = 8
NZ = 2
NX = NQ - NZ
W = D // NQ
ORDER = (0, 1, 2, 3, 0, 1, 4, 2, 0, 3, 1, 5, 4, 0, 2, 1, 3, 6, 0, 5, 2, 4, 7, 1, 6, 0, 3, 5, 2, 4, 7, 1, 3, 6, 0, 5, 4, 7, 1, 6, 5, 7, 6, 7)
SHARE_AT, STORE_AT = 3, 20
PIECE = 272
EPS = 1e-05
G0, G1 = 0.7978845608028654, 0.044715


def nn(a, b):
    return jnp.dot(a, b, preferred_element_type=F32)


def nt(a, b):
    return lax.dot_general(a, b, (((1,), (1,)), ((), ())), preferred_element_type=F32)


def split3(x):
    hi = x.astype(BF16).astype(F32)
    mid = (x - hi).astype(BF16).astype(F32)
    return hi, mid, x - hi - mid


def in_rows(parts, shape):
    ids = lax.broadcasted_iota(jnp.int32, shape, 0)
    block = jnp.zeros(shape, F32)
    for i, part in enumerate(parts):
        block = jnp.where(ids == i, part, block)
    return block


def kernel(
    zn, yn,
    tokens, positions, value_proj, write_proj, read_proj, step_proj, step_bias, decay_rate, reset_depth,
    out_proj, router, pad_vector, up_weight, down_weight, cotangent,
    encoded_out, mct_out, io_out, up_out, down_out,
    tok, pos, vp, wr, sp, bias, rate, reset, op, rout, pad, up, down, cot,
    normed, kr, vals, zrow, zcol, expander, dtv, ece, state, chunk_state, dpre, within,
    p1s, p1r, p2s, p2r, p3s, incoming,
    encoded, groups, select, mct, padup, pad_col, padsq,
    xn, gg, scale, slope, fac, turned, lt, lto, vx, vr,
    partial, ars, ar1, io,
    own, prod, xa, xb, za_up, za_down, za_up_in, za_down_in, zb, zb_in,
    prod_z, ring_up, ring_down, ring_up_in, ring_down_in, prod_x, xa_z, xb_z,
    load, store, ss, rs,
):
    sn = zn * PLANE
    ru, rd = 2 * D // sn, D // sn
    zh = zn // 2
    qw = D // yn
    seq, y = lax.axis_index("seq"), lax.axis_index("mlp")
    z, me = seq // PLANE, lax.rem(seq, PLANE)
    x, core = me // CN, lax.rem(me, CN)

    def plane_at(j):
        return z * PLANE + j

    pairs = [
        (tokens, tok), (write_proj, wr.at[:, 0:NS]), (read_proj, wr.at[:, NS : 2 * NS]), (step_proj, sp),
        (step_bias, bias), (decay_rate, rate), (reset_depth, reset), (value_proj, vp), (positions, pos),
        (pad_vector, pad), (out_proj, op), (router, rout), (up_weight, up), (cotangent, cot), (down_weight, down),
    ]
    loads = [pltpu.make_async_copy(a, b, load.at[i]) for i, (a, b) in enumerate(pairs)]
    for copy in loads[:8]:
        copy.start()

    barrier = pltpu.get_barrier_semaphore()
    peers = 0
    for oy in range(yn):
        for o in range(PLANE):
            if o or oy:
                peers += 1
                pl.semaphore_signal(
                    barrier, inc=1, device_id_type=MESH,
                    device_id=(plane_at(lax.rem(me + o, PLANE)), lax.rem(y + oy, yn)),
                )
    for o in range(1, zn):
        peers += 1
        pl.semaphore_signal(
            barrier, inc=1, device_id_type=MESH, device_id=(lax.rem(z + o, zn) * PLANE + me, y)
        )

    count = [0]

    def ids(n):
        count[0] += n
        return count[0] - n

    def rdma(src, dst, i, to_seq, to_y):
        return pltpu.make_async_remote_copy(
            src_ref=src, dst_ref=dst, send_sem=ss.at[i], recv_sem=rs.at[i],
            device_id=(to_seq, to_y), device_id_type=MESH,
        )

    step1, step2, step3, from3, swaps, share1, share2, from2 = [], [None], [], [], [], [], [], []
    copies = []

    for copy in loads[:7]:
        copy.wait()

    def norm(b, carry):
        rows = pl.ds(pl.multiple_of(b * Q, Q), Q)
        field = tok[rows, :].astype(F32)
        ms = jnp.mean(field * field, axis=-1, keepdims=True)
        normed[rows, :] = (field * lax.rsqrt(ms + EPS)).astype(BF16)
        return carry

    lax.fori_loop(0, CHUNKS, norm, 0)
    e_row = lax.rem(lax.broadcasted_iota(jnp.int32, (2 * Q, D), 0), HEADS)
    e_col = lax.broadcasted_iota(jnp.int32, (2 * Q, D), 1) // HEAD
    expander[...] = (e_row == e_col).astype(F32).astype(BF16)

    eye = lax.broadcasted_iota(jnp.int32, (HEADS, HEADS), 0) == lax.broadcasted_iota(jnp.int32, (HEADS, HEADS), 1)

    def column(row):
        return jnp.sum(jnp.where(eye, jnp.broadcast_to(row, (HEADS, HEADS)), 0.0), axis=1, keepdims=True)

    kr[...] = nn(normed[...], wr[...]).astype(BF16)
    raw = nt(sp[...], normed[...]) + column(bias[...])
    dt_all = jnp.maximum(raw, 0.0) + jnp.log1p(jnp.exp(-jnp.abs(raw)))
    ld_all = -dt_all * column(rate[...]) - reset[...]
    s_id = lax.broadcasted_iota(jnp.int32, (Q, Q), 0)
    t_id = lax.broadcasted_iota(jnp.int32, (Q, Q), 1)
    before = (s_id <= t_id).astype(F32)
    for c in range(CHUNKS):
        cols = slice(c * Q, (c + 1) * Q)
        dt = dt_all[:, cols]
        cum = jnp.dot(ld_all[:, cols], before, precision=HIGHEST, preferred_element_type=F32)
        tail = jnp.exp(cum[:, Q - 1 : Q] - cum) * dt
        block = jnp.concatenate([dt, cum, tail, jnp.exp(cum), jnp.zeros((64, Q), F32)], axis=0)
        zrow[c] = block
        zcol[c] = block.T
    loads[7].wait()
    for copy in loads[8:]:
        copy.start()

    def values(b, carry):
        rows = pl.ds(pl.multiple_of(b * 256, 256), 256)
        vals[rows, :] = nn(normed[rows, :], vp[...]).astype(BF16)
        return carry

    lax.fori_loop(0, ROWS // 256, values, 0)

    state[...] = jnp.zeros_like(state)

    def chunk(c, decay):
        rows = pl.ds(pl.multiple_of(c * Q, Q), Q)
        zt = zcol[c]
        hi, mid, unused = split3(zt)
        kind = lax.broadcasted_iota(jnp.int32, (Q, Q), 1) // HEADS

        def expand(k):
            lhs = jnp.concatenate([jnp.where(kind == k, hi, 0.0), jnp.where(kind == k, mid, 0.0)], axis=1)
            return nn(lhs.astype(BF16), expander[...])

        v = vals[rows, :].astype(F32)
        dtv[rows, :] = (expand(0) * v).astype(BF16)
        weighted = (expand(2) * v).astype(BF16)
        grown = expand(3)
        ece[rows, :] = grown
        keys_t = kr[rows, 0:NS].astype(F32).T.astype(BF16)
        old = state[...]
        chunk_state[c] = old
        dpre[c] = jnp.broadcast_to(decay, (8, D))
        last = grown[Q - 1 : Q, :]
        state[...] = last * old + nn(keys_t, weighted)
        return decay * last

    decay = lax.fori_loop(0, CHUNKS, chunk, jnp.ones((1, D), F32))

    dpre[CHUNKS] = jnp.broadcast_to(decay, (8, D))
    mine = pl.ds(pl.multiple_of(y * qw, qw), qw)
    decay_rows = in_rows(split3(dpre[CHUNKS, 0:1, mine]), (16, qw)).astype(BF16)
    for j in range(PLANE):
        p1s[j, 0:16, :] = state[16 * j : 16 * j + 16, mine].astype(BF16)
        p1s[j, 16:32, :] = decay_rows
    p1r[0] = p1s[me]
    pl.semaphore_wait(barrier, peers)
    base = ids(PLANE)
    for o in range(1, PLANE):
        j = lax.rem(me + o, PLANE)
        step1.append(rdma(p1s.at[j], p1r.at[o], base + o, plane_at(j), y))
        step1[-1].start()

    def intra(c, carry):
        rows = pl.ds(pl.multiple_of(c * Q, Q), Q)
        scores = nt(kr[rows, NS : 2 * NS], kr[rows, 0:NS])
        scores = jnp.where(s_id >= t_id, scores, 0.0)
        first = lax.broadcasted_iota(jnp.int32, (Q, 2 * HEAD), 1) < HEAD
        zr, zt = zrow[c], zcol[c]
        for pair in range(HEADS // 2):
            lanes = slice(2 * HEAD * pair, 2 * HEAD * (pair + 1))
            both = dtv[rows, lanes].astype(F32)
            right = jnp.concatenate([jnp.where(first, both, 0.0), jnp.where(first, 0.0, both)], axis=0)
            mixing = []
            for h in (2 * pair, 2 * pair + 1):
                gap = zt[:, HEADS + h : HEADS + h + 1] - zr[HEADS + h : HEADS + h + 1, :]
                mixing.append(scores * jnp.exp(jnp.minimum(gap, 0.0)))
            within[rows, lanes] = nn(jnp.concatenate(mixing, axis=1).astype(BF16), right.astype(BF16))
        return carry

    lax.fori_loop(0, CHUNKS // 2, intra, 0)

    def read(block):
        block = block.astype(F32)
        return block[0:16], block[16:17] + block[17:18] + block[18:19]

    for copy in step1:
        copy.wait_recv()
    pre, pre_decay = [jnp.zeros((16, qw), F32)], [jnp.ones((1, qw), F32)]
    for k in range(PLANE):
        new, by = read(p1r[lax.rem(me - k + PLANE, PLANE)])
        pre.append(by * pre[-1] + new)
        pre_decay.append(by * pre_decay[-1])
    p2s[0:16, :] = pre[-1].astype(BF16)
    p2s[16:32, :] = in_rows(split3(pre_decay[-1]), (16, qw)).astype(BF16)
    p2r[0] = p2s[...]
    base = ids(zn)
    for o in range(1, zn):
        step2.append(rdma(p2s, p2r.at[o], base + o, lax.rem(z + o, zn) * PLANE + me, y))
        pl.when(z + o < zn)(step2[o].start)

    lax.fori_loop(CHUNKS // 2, CHUNKS, intra, 0)

    for o in range(1, zn):
        pl.when(z >= o)(step2[o].wait_recv)
    start = jnp.zeros((16, qw), F32)
    for k in range(zn - 1):
        new, by = read(p2r[jnp.maximum(z - k, 0)])
        start = jnp.where(k < z, by * start + new, start)
    for k in range(PLANE):
        p3s[k] = (pre_decay[k] * start + pre[k]).astype(BF16)

    def landing(j, at_y):
        return incoming.at[pl.ds(pl.multiple_of(j * 16, 16), 16), pl.ds(pl.multiple_of(at_y * qw, qw), qw)]

    base = ids(PLANE * yn)
    for o in range(PLANE):
        for oy in range(yn):
            if o or oy:
                i = base + o * yn + oy
                j, at_y = lax.rem(me + o, PLANE), lax.rem(y + oy, yn)
                step3.append(rdma(p3s.at[j], landing(me, y), i, plane_at(j), at_y))
                step3[-1].start()
                j, at_y = lax.rem(me - o + PLANE, PLANE), lax.rem(y - oy + yn, yn)
                from3.append(rdma(p3s.at[j], landing(j, at_y), i, plane_at(j), at_y))
    incoming[pl.ds(pl.multiple_of(me * 16, 16), 16), mine] = p3s[me]

    for copy in loads[8:]:
        copy.wait()
    local = pos[...] - seq * ROWS
    n_pos = local.shape[1]
    high, low = local >> 7, local & 127
    ids8 = lax.broadcasted_iota(jnp.int32, (8, n_pos), 0)
    left = jnp.where((jnp.broadcast_to(high, (8, n_pos)) == ids8) & (ids8 < CHUNKS), 1.0, 0.0).astype(BF16)
    ids128 = lax.broadcasted_iota(jnp.int32, (Q, n_pos), 0)
    right = jnp.where(jnp.broadcast_to(low, (Q, n_pos)) == ids128, 1.0, 0.0).astype(BF16)
    marks = nt(left, right)
    running = nn(marks.astype(BF16), before.astype(BF16))
    parts, so_far = [], jnp.zeros((1, 1), F32)
    for c in range(CHUNKS):
        parts.append(running[c : c + 1] + so_far)
        so_far = parts[-1][:, Q - 1 : Q]
    group_of = jnp.concatenate(parts, axis=1) - 1.0
    mark = jnp.concatenate([marks[c : c + 1] for c in range(CHUNKS)], axis=1)
    slot = lax.broadcasted_iota(jnp.int32, (SLOTS, ROWS), 0).astype(F32)
    member = jnp.where(slot == group_of, 1.0, 0.0)
    select[...] = (member * mark).astype(BF16)
    pad_rows = pad[...].astype(F32)
    pad_row = jnp.concatenate([pad_rows[i : i + 1] for i in range(8)], axis=1)
    padsq[...] = jnp.broadcast_to(jnp.sum(pad_row * pad_row, axis=-1, keepdims=True), (8, 128))
    pad_col[...] = jnp.broadcast_to(pad_row, (128, D)).T
    padup[...] = nn(jnp.broadcast_to(pad_row, (16, D)).astype(BF16), up[D : 2 * D, :])

    for copy in from3:
        copy.wait_recv()

    def encode(b, carry):
        for k in range(2):
            c = 2 * b + k
            rows = pl.ds(pl.multiple_of(c * Q, Q), Q)
            full = chunk_state[c] + dpre[c, 0:1, :] * incoming[...].astype(F32)
            carried = nn(kr[rows, NS : 2 * NS], full.astype(BF16))
            scanned = within[rows, :] + ece[rows, :] * carried
            ms = jnp.mean(scanned * scanned, axis=-1, keepdims=True)
            normed[rows, :] = (scanned * lax.rsqrt(ms + EPS)).astype(BF16)
        rows = pl.ds(pl.multiple_of(b * 256, 256), 256)
        encoded[rows, :] = (tok[rows, :].astype(F32) + nn(normed[rows, :], op[...])).astype(BF16)
        return carry

    lax.fori_loop(0, 2, encode, 0)
    logits = nt(in_rows(split3(rout[...]), (16, D)).astype(BF16), encoded[...])
    confidence = 1.0 / (1.0 + jnp.exp(-jnp.sum(logits, axis=0, keepdims=True)))
    weight = member * confidence
    weight_hi = weight.astype(BF16)
    weight_lo = (weight - weight_hi.astype(F32)).astype(BF16)
    mct[:, 0:SLOTS] = weight_hi.astype(F32).T.astype(BF16)
    mct[:, SLOTS : 2 * SLOTS] = weight_lo.astype(F32).T.astype(BF16)
    stores = [pltpu.make_async_copy(encoded, encoded_out, store.at[0]), pltpu.make_async_copy(mct, mct_out, store.at[1])]
    for copy in stores:
        copy.start()
    groups[...] = nn(select[...], encoded[...])
    grads = nn(weight_hi, cot[...]) + nn(weight_lo, cot[...])
    gg[...] = grads.astype(BF16)
    rows_f = groups[...]
    ms = (jnp.sum(rows_f * rows_f, axis=-1, keepdims=True) + padsq[0:1, 0:1]) * (0.5 / D)
    r = lax.rsqrt(ms + EPS)
    scale[...] = jnp.broadcast_to(r, (SLOTS, 128))
    inner = rows_f * r
    xn[...] = inner.astype(BF16)

    def turn(field, part, each, blocks):
        turned[...] = field.T.astype(BF16)
        for k in range(XN):
            at = lax.rem(x + k, XN)
            for b in range(blocks):
                rows = slice(b * each, (b + 1) * each)
                begin = (b * PLANE + at * CN + core) * each
                lt[part, k, rows, 0:SLOTS] = turned[pl.ds(pl.multiple_of(begin, 16), each), :]
                begin = (b * PLANE + at * CN + 1 - core) * each
                lto[part, k, rows, :] = turned[pl.ds(pl.multiple_of(begin, 16), each), :]

    turn(inner, 0, ru, zh)
    turn(grads, 1, rd, zn)
    mate = plane_at(x * CN + 1 - core)
    base = ids(4)
    swaps += [
        rdma(lto, lt.at[:, :, :, SLOTS : 2 * SLOTS], base, mate, y),
        rdma(fac.at[1, 0:SLOTS, :], fac.at[1, SLOTS : 2 * SLOTS, :], base + 1, mate, y),
        rdma(fac.at[0, 0:SLOTS, :], fac.at[0, SLOTS : 2 * SLOTS, :], base + 2, mate, y),
        rdma(vx, vr, base + 3, mate, y),
    ]
    swaps[0].start()

    def forward(b, carry):
        cols = pl.ds(pl.multiple_of(b * 256, 256), 256)
        pre_act = nn(xn[...], up[0:D, cols]) + scale[:, 0:1] * padup[0:1, cols]
        square = pre_act * pre_act
        bend = jnp.tanh(G0 * pre_act * (1.0 + G1 * square))
        fac[1, 0:SLOTS, cols] = (0.5 * pre_act * (1.0 + bend)).astype(BF16)
        slope[:, cols] = 0.5 * (1.0 + bend) + 0.5 * pre_act * (1.0 - bend * bend) * (
            G0 * (1.0 + 3.0 * G1 * square)
        )
        return carry

    lax.fori_loop(0, 4, forward, 0)
    swaps[1].start()

    def backward(b, carry):
        cols = pl.ds(pl.multiple_of(b * 256, 256), 256)
        pre_grad = (nn(gg[...], down[:, cols]) * slope[:, cols]).astype(BF16)
        fac[0, 0:SLOTS, cols] = pre_grad
        pad_term = jnp.sum(pre_grad.astype(F32) * scale[:, 0:1], axis=0, keepdims=True)
        vx[:, cols] = jnp.broadcast_to(pad_term, (8, 256))
        return carry

    lax.fori_loop(0, 4, backward, 0)
    swaps[2].start()
    swaps[3].start()

    rq = SLOTS // yn
    partial[...] = nt(fac[1, 0:SLOTS, :], down[...])
    ars[...] = partial[...].astype(BF16)
    base = ids(2 * yn)
    my_rows = pl.ds(pl.multiple_of(y * rq, rq), rq)
    for o in range(1, yn):
        at_y = lax.rem(y + o, yn)
        share1.append(rdma(ars.at[pl.ds(pl.multiple_of(at_y * rq, rq), rq), :], ar1.at[o - 1], base + o, seq, at_y))
        share1[-1].start()
        share2.append(rdma(io.at[my_rows, :], io.at[my_rows, :], base + yn + o, seq, at_y))
        at_y = lax.rem(y - o + yn, yn)
        other = pl.ds(pl.multiple_of(at_y * rq, rq), rq)
        from2.append(rdma(io.at[other, :], io.at[other, :], base + yn + o, seq, at_y))

    for copy in swaps:
        copy.wait_recv()
    right_x = plane_at(lax.rem(x + 1, XN) * CN + core)
    left_x = plane_at(lax.rem(x + XN - 1, XN) * CN + core)

    def on_z(o):
        return lax.rem(z + o + zn, zn)

    def device_z(o):
        return on_z(o) * PLANE + me

    def sent(*args):
        copy = rdma(*args)
        copy.start()
        copies.append(copy)
        return copy

    def f32(block):
        return block.astype(F32)

    class AlongX:
        def __init__(self, src, upper, lower, a_in, b_in):
            self.src, self.upper, self.lower, self.a_in, self.b_in = src, upper, lower, a_in, b_in
            self.base = ids(6)

        def ahead(self):
            src, up_rows, low_rows, i = self.src, self.upper, self.lower, self.base
            self.far_a = sent(src.at[2, up_rows, :], self.a_in.at[0], i, right_x, y)
            self.far_b = sent(src.at[2, low_rows, :], self.b_in.at[0], i + 1, left_x, y)
            self.rest = [
                sent(src.at[1, low_rows, :], self.b_in.at[1], i + 2, right_x, y),
                sent(src.at[3, up_rows, :], self.a_in.at[1], i + 3, left_x, y),
            ]

        def later(self):
            src, up_rows, low_rows, i = self.src, self.upper, self.lower, self.base
            self.far_a.wait_recv()
            src[1, up_rows, :] = (f32(src[1, up_rows, :]) + f32(self.a_in[0])).astype(BF16)
            self.rest.append(sent(src.at[1, up_rows, :], self.a_in.at[2], i + 4, right_x, y))
            self.far_b.wait_recv()
            src[3, low_rows, :] = (f32(src[3, low_rows, :]) + f32(self.b_in[0])).astype(BF16)
            self.rest.append(sent(src.at[3, low_rows, :], self.b_in.at[2], i + 5, left_x, y))

        def arrived(self):
            for copy in self.rest:
                copy.wait_recv()
            return f32(self.a_in[1]) + f32(self.a_in[2]), f32(self.b_in[1]) + f32(self.b_in[2])

    def up_rows(t):
        return pl.ds(pl.multiple_of(jnp.where(t < zh, ru * t, 256), 16), ru)

    def down_rows(t):
        return pl.ds(pl.multiple_of(128 + rd * t, 16), rd)

    pad_part = pad_col[pl.ds(pl.multiple_of(ru * jnp.maximum(seq - sn // 2, 0), 16), ru), 0:1]

    def write(q, up_sum, down_sum):
        cols = slice(q * W, (q + 1) * W)
        up_out[:, cols] = jnp.where(z < zh, up_sum, pad_part * up_sum[0:1])
        down_out[:, cols] = down_sum

    def terms(q):
        cols = slice(q * W, (q + 1) * W)
        for part in range(2):
            yield nn(lt[part].reshape(XN * 128, 2 * SLOTS), fac[part, :, cols])
        yield in_rows([vx[0:1, cols] + vr[0:1, cols]], (32, W))

    def x_first(q):
        n = q - NZ
        along_x = AlongX(prod.at[n], slice(0, 128), slice(128, PIECE), xa.at[n], xb.at[n])
        base = ids(6)

        def piece(o):
            t = on_z(o)
            return own[n, up_rows(t), :], own[n, down_rows(t), :]

        def first():
            for part, term in enumerate(terms(q)):
                if part < 2:
                    rows = slice(128 * part, 128 * part + 128)
                    own[n, rows, :] = term[0:128]
                    for k in range(1, XN):
                        prod[n, k, rows, :] = term[128 * k : 128 * k + 128].astype(BF16)
                else:
                    own[n, 256:288, :] = term
                    for k in range(1, XN):
                        prod[n, k, 256:PIECE, :] = term[0:16].astype(BF16)
            along_x.ahead()

        def two_away():
            a, b = along_x.arrived()
            own[n, 0:128, :] += a
            own[n, 128:PIECE, :] += b
            za_up[n, 0:32, :] = piece(4)[0].astype(BF16)
            near = piece(3)
            za_up[n, 32:64, :] = near[0].astype(BF16)
            za_up[n, 64:80, :] = near[1].astype(BF16)
            far.append(sent(za_up.at[n], za_up_in.at[n], base, device_z(2), y))
            za_down[n, 0:16, :] = piece(-4)[1].astype(BF16)
            near = piece(-3)
            za_down[n, 16:32, :] = near[1].astype(BF16)
            za_down[n, 32:64, :] = near[0].astype(BF16)
            far.append(sent(za_down.at[n], za_down_in.at[n], base + 1, device_z(-2), y))

        far, last = [], []

        def nearer():
            for copy in far:
                copy.wait_recv()
            from_up, from_down = f32(za_up_in[n]), f32(za_down_in[n])
            for i, o in enumerate((2, -2, 1, -1)):
                up_sum, down_sum = piece(o)
                if o == 2:
                    up_sum = up_sum + from_up[0:32]
                elif o == -2:
                    down_sum = down_sum + from_down[0:16]
                elif o == 1:
                    up_sum, down_sum = up_sum + from_up[32:64], down_sum + from_up[64:80]
                else:
                    up_sum, down_sum = up_sum + from_down[32:64], down_sum + from_down[16:32]
                zb[n, i, 0:32, :] = up_sum.astype(BF16)
                zb[n, i, 32:48, :] = down_sum.astype(BF16)
                last.append(sent(zb.at[n, i], zb_in.at[n, i], base + 2 + i, device_z(o), y))

        def final():
            for copy in last:
                copy.wait_recv()
            up_sum, down_sum = piece(0)
            for i in range(4):
                up_sum = up_sum + f32(zb_in[n, i, 0:32, :])
                down_sum = down_sum + f32(zb_in[n, i, 32:48, :])
            write(q, up_sum, down_sum)

        return [first, along_x.later, two_away, nearer, final]

    def z_first(n):
        along_x = AlongX(prod_x.at[n], slice(0, 32), slice(32, 48), xa_z.at[n], xb_z.at[n])
        base = ids(8)
        up_copy, down_copy = [], []

        def piece(o):
            t = on_z(o)
            return prod_z[n, :, up_rows(t), :], prod_z[n, :, down_rows(t), :]

        def hop(i):
            if i == 0:
                for part, term in enumerate(terms(n)):
                    for k in range(XN):
                        if part < 2:
                            prod_z[n, k, 128 * part : 128 * part + 128, :] = term[128 * k : 128 * k + 128]
                        else:
                            prod_z[n, k, 256:288, :] = term
                ring_up[n, 0, :, 0:32, :] = piece(4)[0].astype(BF16)
                ring_down[n, 0, :, 32:48, :] = piece(-4)[1].astype(BF16)
                rows_up, rows_down = slice(0, 32), slice(32, 48)
            else:
                up_copy[i - 1].wait_recv()
                up_sum, down_sum = piece(4 - i)
                up_sum = up_sum + f32(ring_up_in[n, i - 1, :, 0:32, :])
                if i > 1:
                    down_sum = down_sum + f32(ring_up_in[n, i - 1, :, 32:48, :])
                ring_up[n, i, :, 0:32, :] = up_sum.astype(BF16)
                ring_up[n, i, :, 32:48, :] = down_sum.astype(BF16)
                down_copy[i - 1].wait_recv()
                up_sum, down_sum = piece(i - 4)
                down_sum = down_sum + f32(ring_down_in[n, i - 1, :, 32:48, :])
                if i > 1:
                    up_sum = up_sum + f32(ring_down_in[n, i - 1, :, 0:32, :])
                ring_down[n, i, :, 0:32, :] = up_sum.astype(BF16)
                ring_down[n, i, :, 32:48, :] = down_sum.astype(BF16)
                rows_up = rows_down = slice(0, 48)
            up_copy.append(
                sent(ring_up.at[n, i, :, rows_up, :], ring_up_in.at[n, i, :, rows_up, :], base + i, device_z(1), y)
            )
            down_copy.append(
                sent(ring_down.at[n, i, :, rows_down, :], ring_down_in.at[n, i, :, rows_down, :], base + 4 + i, device_z(-1), y)
            )

        mine_z = []

        def collect():
            up_copy[3].wait_recv()
            down_copy[3].wait_recv()
            up_sum, down_sum = piece(0)
            up_sum = up_sum + f32(ring_up_in[n, 3, :, 0:32, :]) + f32(ring_down_in[n, 3, :, 0:32, :])
            down_sum = down_sum + f32(ring_up_in[n, 3, :, 32:48, :]) + f32(ring_down_in[n, 3, :, 32:48, :])
            prod_x[n, :, 0:32, :] = up_sum.astype(BF16)
            prod_x[n, :, 32:48, :] = down_sum.astype(BF16)
            mine_z.extend([up_sum[0], down_sum[0]])
            along_x.ahead()

        def final():
            a, b = along_x.arrived()
            write(n, mine_z[0] + a, mine_z[1] + b)

        return [functools.partial(hop, i) for i in range(4)] + [collect, along_x.later, final]

    def reduce_share():
        for copy in share1:
            copy.wait_recv()
        summed = groups[my_rows, :] + partial[my_rows, :]
        for o in range(1, yn):
            summed = summed + ar1[o - 1].astype(F32)
        io[my_rows, :] = summed.astype(BF16)
        for copy in share2:
            copy.start()

    def share():
        for copy in from2:
            copy.wait_recv()
        stores.append(pltpu.make_async_copy(io, io_out, store.at[2]))
        stores[2].start()

    steps = [iter(z_first(q) if q < NZ else x_first(q)) for q in range(NQ)]
    for i, q in enumerate(ORDER):
        if i == SHARE_AT:
            reduce_share()
        if i == STORE_AT:
            share()
        next(steps[q])()

    for copy in stores:
        copy.wait()
    for copy in step1 + step3 + swaps + share1 + share2:
        copy.wait_send()
    for o in range(1, len(step2)):
        pl.when(z + o < zn)(step2[o].wait_send)
    for copy in copies:
        copy.wait_send()


def finish(encoded, mct, io, up_sum, down_sum, mixed, up_out, down_out):
    both = io[...]
    spread = nn(mct[...], jnp.concatenate([both, both], axis=0))
    mixed[...] = (encoded[...].astype(F32) + spread).astype(BF16)
    up_out[...] = up_sum[...]
    down_out[...] = down_sum[...]


def on_device(
    zn, yn, tokens, positions, value_proj, write_proj, read_proj, step_proj, step_bias, decay_rate, reset_depth,
    out_proj, router, pad_vector, up_weight, down_weight, cotangent,
):
    sn = zn * PLANE
    ru, rd, qw = 2 * D // sn, D // sn, D // yn
    n_pos = positions.shape[0]
    vm = pltpu.VMEM
    n_sem = PLANE + zn + PLANE * yn + 4 + 2 * yn + NX * 12 + NZ * 14
    scratch = [
        vm((ROWS, D), BF16), vm((1, n_pos), jnp.int32), vm((D, D), BF16), vm((D, 2 * NS), BF16), vm((HEADS, D), BF16),
        vm((1, HEADS), F32), vm((1, HEADS), F32), vm((1, ROWS), F32), vm((D, D), BF16), vm((1, D), F32),
        vm((8, D // 8), BF16), vm((2 * D, D), BF16), vm((D, D), BF16), vm((ROWS, D), BF16),
        vm((ROWS, D), BF16), vm((ROWS, 2 * NS), BF16), vm((ROWS, D), BF16), vm((CHUNKS, Q, Q), F32),
        vm((CHUNKS, Q, Q), F32), vm((2 * Q, D), BF16), vm((ROWS, D), BF16), vm((ROWS, D), F32), vm((NS, D), F32),
        vm((CHUNKS, NS, D), F32), vm((CHUNKS + 1, 8, D), F32), vm((ROWS, D), F32),
        vm((PLANE, 32, qw), BF16), vm((PLANE, 32, qw), BF16), vm((32, qw), BF16), vm((zn, 32, qw), BF16),
        vm((PLANE, 16, qw), BF16), vm((NS, D), BF16),
        vm((ROWS, D), BF16), vm((SLOTS, D), F32), vm((SLOTS, ROWS), BF16), vm((ROWS, 2 * SLOTS), BF16),
        vm((16, D), F32), vm((D, 128), F32), vm((8, 128), F32),
        vm((SLOTS, D), BF16), vm((SLOTS, D), BF16), vm((SLOTS, 128), F32), vm((SLOTS, D), F32),
        vm((2, 2 * SLOTS, D), BF16), vm((D, SLOTS), BF16), vm((2, XN, 128, 2 * SLOTS), BF16),
        vm((2, XN, 128, SLOTS), BF16),
        vm((8, D), F32), vm((8, D), F32),
        vm((SLOTS, D), F32), vm((SLOTS, D), BF16), vm((max(yn - 1, 1), SLOTS // yn, D), BF16), vm((SLOTS, D), BF16),
        vm((NX, 288, W), F32), vm((NX, XN, PIECE, W), BF16), vm((NX, 3, 128, W), BF16), vm((NX, 3, 144, W), BF16),
        vm((NX, 80, W), BF16), vm((NX, 64, W), BF16), vm((NX, 80, W), BF16), vm((NX, 64, W), BF16),
        vm((NX, 4, 48, W), BF16), vm((NX, 4, 48, W), BF16),
        vm((NZ, XN, 288, W), F32), vm((NZ, 4, XN, 48, W), BF16), vm((NZ, 4, XN, 48, W), BF16),
        vm((NZ, 4, XN, 48, W), BF16), vm((NZ, 4, XN, 48, W), BF16), vm((NZ, XN, 48, W), BF16),
        vm((NZ, 3, 32, W), BF16), vm((NZ, 3, 16, W), BF16),
        pltpu.SemaphoreType.DMA((15,)), pltpu.SemaphoreType.DMA((3,)), pltpu.SemaphoreType.DMA((n_sem,)), pltpu.SemaphoreType.DMA((n_sem,)),
    ]
    encoded, mct, io, up_sum, down_sum = pl.pallas_call(
        functools.partial(kernel, zn, yn),
        out_shape=(
            jax.ShapeDtypeStruct((ROWS, D), BF16),
            jax.ShapeDtypeStruct((ROWS, 2 * SLOTS), BF16),
            jax.ShapeDtypeStruct((SLOTS, D), BF16),
            jax.ShapeDtypeStruct((ru, D), F32),
            jax.ShapeDtypeStruct((rd, D), F32),
        ),
        in_specs=[pl.BlockSpec(memory_space=pl.ANY)] * 15,
        out_specs=(pl.BlockSpec(memory_space=pl.ANY),) * 3 + (pl.BlockSpec(memory_space=pltpu.VMEM),) * 2,
        scratch_shapes=scratch,
        compiler_params=pltpu.CompilerParams(
            collective_id=0, has_side_effects=True, vmem_limit_bytes=60 * 2**20
        ),
    )(
        tokens, positions.reshape(1, n_pos), value_proj, write_proj, read_proj, step_proj.T, step_bias.reshape(1, HEADS),
        decay_rate.reshape(1, HEADS), reset_depth.reshape(1, ROWS), out_proj, router.reshape(1, D),
        pad_vector.reshape(8, D // 8), up_weight, down_weight, cotangent,
    )
    half = ROWS // 2
    return pl.pallas_call(
        finish,
        grid=(2,),
        out_shape=(
            jax.ShapeDtypeStruct((ROWS, D), BF16),
            jax.ShapeDtypeStruct((ru, D), F32),
            jax.ShapeDtypeStruct((rd, D), F32),
        ),
        in_specs=[
            pl.BlockSpec((half, D), lambda i: (i, 0)),
            pl.BlockSpec((half, 2 * SLOTS), lambda i: (i, 0)),
            pl.BlockSpec((SLOTS, D), lambda i: (0, 0)),
            pl.BlockSpec((ru // 2, D), lambda i: (i, 0)),
            pl.BlockSpec((rd // 2, D), lambda i: (i, 0)),
        ],
        out_specs=(
            pl.BlockSpec((half, D), lambda i: (i, 0)),
            pl.BlockSpec((ru // 2, D), lambda i: (i, 0)),
            pl.BlockSpec((rd // 2, D), lambda i: (i, 0)),
        ),
        compiler_params=pltpu.CompilerParams(vmem_limit_bytes=60 * 2**20),
    )(encoded, mct, io, up_sum, down_sum)


def solution(mesh):
    placed = (
        P("seq", None), P(), P(), P(), P(), P(), P(), P(), P("seq"), P(), P(), P(),
        P(None, "mlp"), P(None, "mlp"), P("seq", None),
    )
    return jax.shard_map(
        functools.partial(on_device, mesh.shape["seq"] // PLANE, mesh.shape["mlp"]),
        mesh=mesh,
        in_specs=placed,
        out_specs=(P("seq", None), P("seq", "mlp"), P("seq", "mlp")),
        check_vma=False,
    )
```

```python
import functools

import jax
import jax.numpy as jnp
from jax import lax
from jax.experimental import pallas as pl
from jax.experimental.pallas import tpu as pltpu
from jax.sharding import PartitionSpec as P

F32, BF16 = jnp.float32, jnp.bfloat16
HIGHEST = lax.Precision.HIGHEST
MESH = pl.DeviceIdType.MESH

ROWS = 512
D = 1024
HEADS = 16
HEAD = 64
NS = 128
Q = 128
CHUNKS = ROWS // Q
SLOTS = 128
XN, CN = 4, 2
PLANE = XN * CN
WIDTHS_Z, WIDTHS_X = (128, 128), (256, 256, 128, 128)
NZ, NQ = len(WIDTHS_Z), len(WIDTHS_Z + WIDTHS_X)
ORDER = (
    3, 0, 1, 2, 0, 1, 3, 0, 5, 1, 2, 3, 4, 1, 5, 0, 2, 3, 4, 1, 5, 0, 4, 2, 0, 3, 1, 5, 4, 1, 0, 2, 5, 4,
)
SHARE_AT, STORE_AT = 3, 20
PIECE = 272
EPS = 1e-05
G0, G1 = 0.7978845608028654, 0.044715


def nn(a, b):
    return jnp.dot(a, b, preferred_element_type=F32)


def nt(a, b):
    return lax.dot_general(a, b, (((1,), (1,)), ((), ())), preferred_element_type=F32)


def split3(x):
    hi = x.astype(BF16).astype(F32)
    mid = (x - hi).astype(BF16).astype(F32)
    return hi, mid, x - hi - mid


def in_rows(parts, shape):
    ids = lax.broadcasted_iota(jnp.int32, shape, 0)
    block = jnp.zeros(shape, F32)
    for i, part in enumerate(parts):
        block = jnp.where(ids == i, part, block)
    return block


def kernel(
    zn, yn,
    tokens, positions, value_proj, write_proj, read_proj, step_proj, step_bias, decay_rate, reset_depth,
    out_proj, router, pad_vector, up_weight, down_weight, cotangent,
    encoded_out, mct_out, io_out, up_out, down_out,
    tok, pos, vp, wr, sp, bias, rate, reset, op, rout, pad, up, down, cot,
    normed, kr, vals, zrow, zcol, expander, dtv, ece, state, chunk_state, dpre, within,
    p1s, p1r, p2s, p2r, p3s, incoming,
    encoded, groups, select, mct, padup, pad_col, padsq,
    xn, gg, scale, slope, fac, turned, lt, lto, vx, vr,
    partial, ars, ar1, io,
    along_z, along_x,
    load, store, ss, rs,
):
    sn = zn * PLANE
    ru, rd = 2 * D // sn, D // sn
    zh = zn // 2
    qw = D // yn
    seq, y = lax.axis_index("seq"), lax.axis_index("mlp")
    z, me = seq // PLANE, lax.rem(seq, PLANE)
    x, core = me // CN, lax.rem(me, CN)

    def plane_at(j):
        return z * PLANE + j

    pairs = [
        (tokens, tok), (write_proj, wr.at[:, 0:NS]), (read_proj, wr.at[:, NS : 2 * NS]), (step_proj, sp),
        (step_bias, bias), (decay_rate, rate), (reset_depth, reset), (value_proj, vp), (positions, pos),
        (pad_vector, pad), (out_proj, op), (router, rout), (up_weight, up), (cotangent, cot), (down_weight, down),
    ]
    loads = [pltpu.make_async_copy(a, b, load.at[i]) for i, (a, b) in enumerate(pairs)]
    for copy in loads[:8]:
        copy.start()

    barrier = pltpu.get_barrier_semaphore()
    partners = [(plane_at(lax.rem(me + o, PLANE)), y) for o in range(1, PLANE)]
    partners += [(lax.rem(z + o, zn) * PLANE + me, y) for o in range(1, zn)]
    partners += [(seq, lax.rem(y + o, yn)) for o in range(1, yn)]
    for partner in partners:
        pl.semaphore_signal(barrier, inc=1, device_id=partner, device_id_type=MESH)

    count = [0]

    def ids(n):
        count[0] += n
        return count[0] - n

    def rdma(src, dst, i, to_seq, to_y):
        return pltpu.make_async_remote_copy(
            src_ref=src, dst_ref=dst, send_sem=ss.at[i], recv_sem=rs.at[i],
            device_id=(to_seq, to_y), device_id_type=MESH,
        )

    step1, step2, step3, from3, swaps, share1, share2, from2 = [], [None], [], [], [], [], [], []
    copies = []

    for copy in loads[:7]:
        copy.wait()

    def norm(b, carry):
        rows = pl.ds(pl.multiple_of(b * Q, Q), Q)
        field = tok[rows, :].astype(F32)
        ms = jnp.mean(field * field, axis=-1, keepdims=True)
        normed[rows, :] = (field * lax.rsqrt(ms + EPS)).astype(BF16)
        return carry

    lax.fori_loop(0, CHUNKS, norm, 0)
    e_row = lax.rem(lax.broadcasted_iota(jnp.int32, (2 * Q, D), 0), HEADS)
    e_col = lax.broadcasted_iota(jnp.int32, (2 * Q, D), 1) // HEAD
    expander[...] = (e_row == e_col).astype(F32).astype(BF16)

    eye = lax.broadcasted_iota(jnp.int32, (HEADS, HEADS), 0) == lax.broadcasted_iota(jnp.int32, (HEADS, HEADS), 1)

    def column(row):
        return jnp.sum(jnp.where(eye, jnp.broadcast_to(row, (HEADS, HEADS)), 0.0), axis=1, keepdims=True)

    kr[...] = nn(normed[...], wr[...]).astype(BF16)
    raw = nt(sp[...], normed[...]) + column(bias[...])
    dt_all = jnp.maximum(raw, 0.0) + jnp.log1p(jnp.exp(-jnp.abs(raw)))
    ld_all = -dt_all * column(rate[...]) - reset[...]
    s_id = lax.broadcasted_iota(jnp.int32, (Q, Q), 0)
    t_id = lax.broadcasted_iota(jnp.int32, (Q, Q), 1)
    before = (s_id <= t_id).astype(F32)
    for c in range(CHUNKS):
        cols = slice(c * Q, (c + 1) * Q)
        dt = dt_all[:, cols]
        cum = jnp.dot(ld_all[:, cols], before, precision=HIGHEST, preferred_element_type=F32)
        tail = jnp.exp(cum[:, Q - 1 : Q] - cum) * dt
        block = jnp.concatenate([dt, cum, tail, jnp.exp(cum), jnp.zeros((64, Q), F32)], axis=0)
        zrow[c] = block
        zcol[c] = block.T
    loads[7].wait()
    for copy in loads[8:]:
        copy.start()

    def values(b, carry):
        rows = pl.ds(pl.multiple_of(b * 256, 256), 256)
        vals[rows, :] = nn(normed[rows, :], vp[...]).astype(BF16)
        return carry

    lax.fori_loop(0, ROWS // 256, values, 0)

    state[...] = jnp.zeros_like(state)

    def chunk(c, decay):
        rows = pl.ds(pl.multiple_of(c * Q, Q), Q)
        zt = zcol[c]
        hi, mid, unused = split3(zt)
        kind = lax.broadcasted_iota(jnp.int32, (Q, Q), 1) // HEADS

        def expand(k):
            lhs = jnp.concatenate([jnp.where(kind == k, hi, 0.0), jnp.where(kind == k, mid, 0.0)], axis=1)
            return nn(lhs.astype(BF16), expander[...])

        v = vals[rows, :].astype(F32)
        dtv[rows, :] = (expand(0) * v).astype(BF16)
        weighted = (expand(2) * v).astype(BF16)
        grown = expand(3)
        ece[rows, :] = grown
        keys_t = kr[rows, 0:NS].astype(F32).T.astype(BF16)
        old = state[...]
        chunk_state[c] = old
        dpre[c] = jnp.broadcast_to(decay, (8, D))
        last = grown[Q - 1 : Q, :]
        state[...] = last * old + nn(keys_t, weighted)
        return decay * last

    decay = lax.fori_loop(0, CHUNKS, chunk, jnp.ones((1, D), F32))

    dpre[CHUNKS] = jnp.broadcast_to(decay, (8, D))
    mine = pl.ds(pl.multiple_of(y * qw, qw), qw)
    decay_rows = in_rows(split3(dpre[CHUNKS, 0:1, mine]), (16, qw)).astype(BF16)
    for j in range(PLANE):
        p1s[j, 0:16, :] = state[16 * j : 16 * j + 16, mine].astype(BF16)
        p1s[j, 16:32, :] = decay_rows
    p1r[0] = p1s[me]
    pl.semaphore_wait(barrier, len(partners))
    base = ids(PLANE)
    for o in range(1, PLANE):
        j = lax.rem(me + o, PLANE)
        step1.append(rdma(p1s.at[j], p1r.at[o], base + o, plane_at(j), y))
        step1[-1].start()

    def intra(c, carry):
        rows = pl.ds(pl.multiple_of(c * Q, Q), Q)
        scores = nt(kr[rows, NS : 2 * NS], kr[rows, 0:NS])
        scores = jnp.where(s_id >= t_id, scores, 0.0)
        first = lax.broadcasted_iota(jnp.int32, (Q, 2 * HEAD), 1) < HEAD
        zr, zt = zrow[c], zcol[c]
        for pair in range(HEADS // 2):
            lanes = slice(2 * HEAD * pair, 2 * HEAD * (pair + 1))
            both = dtv[rows, lanes].astype(F32)
            right = jnp.concatenate([jnp.where(first, both, 0.0), jnp.where(first, 0.0, both)], axis=0)
            mixing = []
            for h in (2 * pair, 2 * pair + 1):
                gap = zt[:, HEADS + h : HEADS + h + 1] - zr[HEADS + h : HEADS + h + 1, :]
                mixing.append(scores * jnp.exp(jnp.minimum(gap, 0.0)))
            within[rows, lanes] = nn(jnp.concatenate(mixing, axis=1).astype(BF16), right.astype(BF16))
        return carry

    lax.fori_loop(0, CHUNKS // 2, intra, 0)

    def read(block):
        block = block.astype(F32)
        return block[0:16], block[16:17] + block[17:18] + block[18:19]

    for copy in step1:
        copy.wait_recv()
    pre, pre_decay = [jnp.zeros((16, qw), F32)], [jnp.ones((1, qw), F32)]
    for k in range(PLANE):
        new, by = read(p1r[lax.rem(me - k + PLANE, PLANE)])
        pre.append(by * pre[-1] + new)
        pre_decay.append(by * pre_decay[-1])
    p2s[0:16, :] = pre[-1].astype(BF16)
    p2s[16:32, :] = in_rows(split3(pre_decay[-1]), (16, qw)).astype(BF16)
    p2r[0] = p2s[...]
    base = ids(zn)
    for o in range(1, zn):
        step2.append(rdma(p2s, p2r.at[o], base + o, lax.rem(z + o, zn) * PLANE + me, y))
        pl.when(z + o < zn)(step2[o].start)

    lax.fori_loop(CHUNKS // 2, CHUNKS, intra, 0)

    for o in range(1, zn):
        pl.when(z >= o)(step2[o].wait_recv)
    start = jnp.zeros((16, qw), F32)
    for k in range(zn - 1):
        new, by = read(p2r[jnp.maximum(z - k, 0)])
        start = jnp.where(k < z, by * start + new, start)
    for k in range(PLANE):
        p3s[k] = (pre_decay[k] * start + pre[k]).astype(BF16)

    def landing(j, at_y):
        return incoming.at[pl.ds(pl.multiple_of(j * 16, 16), 16), pl.ds(pl.multiple_of(at_y * qw, qw), qw)]

    base = ids(PLANE + yn)
    for o in range(1, PLANE):
        j = lax.rem(me + o, PLANE)
        step3.append(rdma(p3s.at[j], landing(me, y), base + o, plane_at(j), y))
        step3[-1].start()
        j = lax.rem(me - o + PLANE, PLANE)
        from3.append(rdma(p3s.at[j], landing(j, y), base + o, plane_at(j), y))
    incoming[pl.ds(pl.multiple_of(me * 16, 16), 16), mine] = p3s[me]

    for copy in from3:
        copy.wait_recv()
    from3.clear()
    for o in range(1, yn):
        at_y = lax.rem(y + o, yn)
        step3.append(rdma(incoming.at[:, mine], incoming.at[:, mine], base + PLANE + o, seq, at_y))
        step3[-1].start()
        at_y = lax.rem(y - o + yn, yn)
        theirs = incoming.at[:, pl.ds(pl.multiple_of(at_y * qw, qw), qw)]
        from3.append(rdma(theirs, theirs, base + PLANE + o, seq, at_y))

    for copy in loads[8:]:
        copy.wait()
    local = pos[...] - seq * ROWS
    n_pos = local.shape[1]
    high, low = local >> 7, local & 127
    ids8 = lax.broadcasted_iota(jnp.int32, (8, n_pos), 0)
    left = jnp.where((jnp.broadcast_to(high, (8, n_pos)) == ids8) & (ids8 < CHUNKS), 1.0, 0.0).astype(BF16)
    ids128 = lax.broadcasted_iota(jnp.int32, (Q, n_pos), 0)
    right = jnp.where(jnp.broadcast_to(low, (Q, n_pos)) == ids128, 1.0, 0.0).astype(BF16)
    marks = nt(left, right)
    running = nn(marks.astype(BF16), before.astype(BF16))
    parts, so_far = [], jnp.zeros((1, 1), F32)
    for c in range(CHUNKS):
        parts.append(running[c : c + 1] + so_far)
        so_far = parts[-1][:, Q - 1 : Q]
    group_of = jnp.concatenate(parts, axis=1) - 1.0
    mark = jnp.concatenate([marks[c : c + 1] for c in range(CHUNKS)], axis=1)
    slot = lax.broadcasted_iota(jnp.int32, (SLOTS, ROWS), 0).astype(F32)
    member = jnp.where(slot == group_of, 1.0, 0.0)
    select[...] = (member * mark).astype(BF16)
    pad_rows = pad[...].astype(F32)
    pad_row = jnp.concatenate([pad_rows[i : i + 1] for i in range(8)], axis=1)
    padsq[...] = jnp.broadcast_to(jnp.sum(pad_row * pad_row, axis=-1, keepdims=True), (8, 128))
    pad_col[...] = jnp.broadcast_to(pad_row, (128, D)).T
    padup[...] = nn(jnp.broadcast_to(pad_row, (16, D)).astype(BF16), up[D : 2 * D, :])

    for copy in from3:
        copy.wait_recv()

    def encode(b, carry):
        for k in range(2):
            c = 2 * b + k
            rows = pl.ds(pl.multiple_of(c * Q, Q), Q)
            full = chunk_state[c] + dpre[c, 0:1, :] * incoming[...].astype(F32)
            carried = nn(kr[rows, NS : 2 * NS], full.astype(BF16))
            scanned = within[rows, :] + ece[rows, :] * carried
            ms = jnp.mean(scanned * scanned, axis=-1, keepdims=True)
            normed[rows, :] = (scanned * lax.rsqrt(ms + EPS)).astype(BF16)
        rows = pl.ds(pl.multiple_of(b * 256, 256), 256)
        encoded[rows, :] = (tok[rows, :].astype(F32) + nn(normed[rows, :], op[...])).astype(BF16)
        return carry

    lax.fori_loop(0, 2, encode, 0)
    logits = nt(in_rows(split3(rout[...]), (16, D)).astype(BF16), encoded[...])
    confidence = 1.0 / (1.0 + jnp.exp(-jnp.sum(logits, axis=0, keepdims=True)))
    weight = member * confidence
    weight_hi = weight.astype(BF16)
    weight_lo = (weight - weight_hi.astype(F32)).astype(BF16)
    mct[:, 0:SLOTS] = weight_hi.astype(F32).T.astype(BF16)
    mct[:, SLOTS : 2 * SLOTS] = weight_lo.astype(F32).T.astype(BF16)
    stores = [pltpu.make_async_copy(encoded, encoded_out, store.at[0]), pltpu.make_async_copy(mct, mct_out, store.at[1])]
    for copy in stores:
        copy.start()
    groups[...] = nn(select[...], encoded[...])
    grads = nn(weight_hi, cot[...]) + nn(weight_lo, cot[...])
    gg[...] = grads.astype(BF16)
    rows_f = groups[...]
    ms = (jnp.sum(rows_f * rows_f, axis=-1, keepdims=True) + padsq[0:1, 0:1]) * (0.5 / D)
    r = lax.rsqrt(ms + EPS)
    scale[...] = jnp.broadcast_to(r, (SLOTS, 128))
    inner = rows_f * r
    xn[...] = inner.astype(BF16)

    def turn(field, part, each, blocks):
        turned[...] = field.T.astype(BF16)
        for k in range(XN):
            at = lax.rem(x + k, XN)
            for b in range(blocks):
                rows = slice(b * each, (b + 1) * each)
                begin = (b * PLANE + at * CN + core) * each
                lt[part, k, rows, 0:SLOTS] = turned[pl.ds(pl.multiple_of(begin, 16), each), :]
                begin = (b * PLANE + at * CN + 1 - core) * each
                lto[part, k, rows, :] = turned[pl.ds(pl.multiple_of(begin, 16), each), :]

    turn(inner, 0, ru, zh)
    turn(grads, 1, rd, zn)
    mate = plane_at(x * CN + 1 - core)
    base = ids(4)
    swaps += [
        rdma(lto, lt.at[:, :, :, SLOTS : 2 * SLOTS], base, mate, y),
        rdma(fac.at[1, 0:SLOTS, :], fac.at[1, SLOTS : 2 * SLOTS, :], base + 1, mate, y),
        rdma(fac.at[0, 0:SLOTS, :], fac.at[0, SLOTS : 2 * SLOTS, :], base + 2, mate, y),
        rdma(vx, vr, base + 3, mate, y),
    ]
    swaps[0].start()

    def forward(b, carry):
        cols = pl.ds(pl.multiple_of(b * 256, 256), 256)
        pre_act = nn(xn[...], up[0:D, cols]) + scale[:, 0:1] * padup[0:1, cols]
        square = pre_act * pre_act
        bend = jnp.tanh(G0 * pre_act * (1.0 + G1 * square))
        fac[1, 0:SLOTS, cols] = (0.5 * pre_act * (1.0 + bend)).astype(BF16)
        slope[:, cols] = 0.5 * (1.0 + bend) + 0.5 * pre_act * (1.0 - bend * bend) * (
            G0 * (1.0 + 3.0 * G1 * square)
        )
        return carry

    lax.fori_loop(0, 4, forward, 0)
    swaps[1].start()

    def backward(b, carry):
        cols = pl.ds(pl.multiple_of(b * 256, 256), 256)
        pre_grad = (nn(gg[...], down[:, cols]) * slope[:, cols]).astype(BF16)
        fac[0, 0:SLOTS, cols] = pre_grad
        pad_term = jnp.sum(pre_grad.astype(F32) * scale[:, 0:1], axis=0, keepdims=True)
        vx[:, cols] = jnp.broadcast_to(pad_term, (8, 256))
        return carry

    lax.fori_loop(0, 4, backward, 0)
    swaps[2].start()
    swaps[3].start()

    rq = SLOTS // yn
    partial[...] = nt(fac[1, 0:SLOTS, :], down[...])
    ars[...] = partial[...].astype(BF16)
    base = ids(2 * yn)
    my_rows = pl.ds(pl.multiple_of(y * rq, rq), rq)
    for o in range(1, yn):
        at_y = lax.rem(y + o, yn)
        share1.append(rdma(ars.at[pl.ds(pl.multiple_of(at_y * rq, rq), rq), :], ar1.at[o - 1], base + o, seq, at_y))
        share1[-1].start()
        share2.append(rdma(io.at[my_rows, :], io.at[my_rows, :], base + yn + o, seq, at_y))
        at_y = lax.rem(y - o + yn, yn)
        other = pl.ds(pl.multiple_of(at_y * rq, rq), rq)
        from2.append(rdma(io.at[other, :], io.at[other, :], base + yn + o, seq, at_y))

    for copy in swaps:
        copy.wait_recv()
    right_x = plane_at(lax.rem(x + 1, XN) * CN + core)
    left_x = plane_at(lax.rem(x + XN - 1, XN) * CN + core)

    def on_z(o):
        return lax.rem(z + o + zn, zn)

    def device_z(o):
        return on_z(o) * PLANE + me

    def sent(*args):
        copy = rdma(*args)
        copy.start()
        copies.append(copy)
        return copy

    def f32(block):
        return block.astype(F32)

    class AlongX:
        def __init__(self, upper, lower, refs):
            self.near_r, self.near_l, self.end_r, self.end_l = refs[:4]
            self.near_r_in, self.near_l_in, self.end_r_in, self.end_l_in = refs[4:]
            self.cut_r, self.cut_l = upper, lower
            self.up = {1: self.end_r, 2: self.near_r.at[0:upper, :], 3: self.near_l.at[lower:, :]}
            self.low = {1: self.near_r.at[upper:, :], 2: self.near_l.at[0:lower, :], 3: self.end_l}
            self.base = ids(4)

        def ahead(self):
            self.near = [
                sent(self.near_r, self.near_r_in, self.base, right_x, y),
                sent(self.near_l, self.near_l_in, self.base + 1, left_x, y),
            ]

        def later(self):
            self.near[0].wait_recv()
            self.end_r[...] = (f32(self.end_r[...]) + f32(self.near_r_in[0 : self.cut_r, :])).astype(BF16)
            first = sent(self.end_r, self.end_r_in, self.base + 2, right_x, y)
            self.near[1].wait_recv()
            self.end_l[...] = (f32(self.end_l[...]) + f32(self.near_l_in[0 : self.cut_l, :])).astype(BF16)
            self.end = [first, sent(self.end_l, self.end_l_in, self.base + 3, left_x, y)]

        def arrived(self):
            for copy in self.end:
                copy.wait_recv()
            return (
                f32(self.near_l_in[self.cut_l :, :]) + f32(self.end_r_in[...]),
                f32(self.near_r_in[self.cut_r :, :]) + f32(self.end_l_in[...]),
            )

    def up_rows(t):
        return pl.ds(pl.multiple_of(jnp.where(t < zh, ru * t, 256), 16), ru)

    def down_rows(t):
        return pl.ds(pl.multiple_of(128 + rd * t, 16), rd)

    pad_part = pad_col[pl.ds(pl.multiple_of(ru * jnp.maximum(seq - sn // 2, 0), 16), ru), 0:1]

    widths = WIDTHS_Z + WIDTHS_X

    def columns(q):
        return slice(sum(widths[:q]), sum(widths[: q + 1]))

    def write(q, up_sum, down_sum):
        cols = columns(q)
        up_out[:, cols] = jnp.where(z < zh, up_sum, pad_part * up_sum[0:1])
        down_out[:, cols] = down_sum

    def terms(q):
        cols = columns(q)
        for part in range(2):
            yield nn(lt[part].reshape(XN * 128, 2 * SLOTS), fac[part, :, cols])
        yield in_rows([vx[0:1, cols] + vr[0:1, cols]], (32, widths[q]))

    def x_first(q):
        own, za_up, za_down, za_up_in, za_down_in, zb, zb_in, *rest = along_x[q - NZ]
        by_x = AlongX(128, 144, rest)
        base = ids(6)

        def piece(o):
            t = on_z(o)
            return own[up_rows(t), :], own[down_rows(t), :]

        def first():
            for part, term in enumerate(terms(q)):
                if part < 2:
                    rows = slice(128 * part, 128 * part + 128)
                    own[rows, :] = term[0:128]
                    for k in range(1, XN):
                        (by_x.low if part else by_x.up)[k][0:128, :] = term[128 * k : 128 * k + 128].astype(BF16)
                else:
                    own[256:288, :] = term
                    for k in range(1, XN):
                        by_x.low[k][128:144, :] = term[0:16].astype(BF16)
            by_x.ahead()

        def two_away():
            a, b = by_x.arrived()
            own[0:128, :] += a
            own[128:PIECE, :] += b
            za_up[0:32, :] = piece(4)[0].astype(BF16)
            near = piece(3)
            za_up[32:64, :] = near[0].astype(BF16)
            za_up[64:80, :] = near[1].astype(BF16)
            far.append(sent(za_up, za_up_in, base, device_z(2), y))
            za_down[0:16, :] = piece(-4)[1].astype(BF16)
            near = piece(-3)
            za_down[16:32, :] = near[1].astype(BF16)
            za_down[32:64, :] = near[0].astype(BF16)
            far.append(sent(za_down, za_down_in, base + 1, device_z(-2), y))

        far, last = [], []

        def nearer():
            for copy in far:
                copy.wait_recv()
            from_up, from_down = f32(za_up_in[...]), f32(za_down_in[...])
            for i, o in enumerate((2, -2, 1, -1)):
                up_sum, down_sum = piece(o)
                if o == 2:
                    up_sum = up_sum + from_up[0:32]
                elif o == -2:
                    down_sum = down_sum + from_down[0:16]
                elif o == 1:
                    up_sum, down_sum = up_sum + from_up[32:64], down_sum + from_up[64:80]
                else:
                    up_sum, down_sum = up_sum + from_down[32:64], down_sum + from_down[16:32]
                zb[i, 0:32, :] = up_sum.astype(BF16)
                zb[i, 32:48, :] = down_sum.astype(BF16)
                last.append(sent(zb.at[i], zb_in.at[i], base + 2 + i, device_z(o), y))

        def final():
            for copy in last:
                copy.wait_recv()
            up_sum, down_sum = piece(0)
            for i in range(4):
                up_sum = up_sum + f32(zb_in[i, 0:32, :])
                down_sum = down_sum + f32(zb_in[i, 32:48, :])
            write(q, up_sum, down_sum)

        return [first, by_x.later, two_away, nearer, final]

    def z_first(n):
        prod_z, ring_up, ring_down, ring_up_in, ring_down_in, *rest = along_z[n]
        by_x = AlongX(32, 16, rest)
        base = ids(8)
        up_copy, down_copy = [], []

        def piece(o):
            t = on_z(o)
            return prod_z[:, up_rows(t), :], prod_z[:, down_rows(t), :]

        def hop(i):
            if i == 0:
                for part, term in enumerate(terms(n)):
                    for k in range(XN):
                        if part < 2:
                            prod_z[k, 128 * part : 128 * part + 128, :] = term[128 * k : 128 * k + 128]
                        else:
                            prod_z[k, 256:288, :] = term
                ring_up[0, :, 0:32, :] = piece(4)[0].astype(BF16)
                ring_down[0, :, 32:48, :] = piece(-4)[1].astype(BF16)
                rows_up, rows_down = slice(0, 32), slice(32, 48)
            else:
                up_copy[i - 1].wait_recv()
                up_sum, down_sum = piece(4 - i)
                up_sum = up_sum + f32(ring_up_in[i - 1, :, 0:32, :])
                if i > 1:
                    down_sum = down_sum + f32(ring_up_in[i - 1, :, 32:48, :])
                ring_up[i, :, 0:32, :] = up_sum.astype(BF16)
                ring_up[i, :, 32:48, :] = down_sum.astype(BF16)
                down_copy[i - 1].wait_recv()
                up_sum, down_sum = piece(i - 4)
                down_sum = down_sum + f32(ring_down_in[i - 1, :, 32:48, :])
                if i > 1:
                    up_sum = up_sum + f32(ring_down_in[i - 1, :, 0:32, :])
                ring_down[i, :, 0:32, :] = up_sum.astype(BF16)
                ring_down[i, :, 32:48, :] = down_sum.astype(BF16)
                rows_up = rows_down = slice(0, 48)
            up_copy.append(
                sent(ring_up.at[i, :, rows_up, :], ring_up_in.at[i, :, rows_up, :], base + i, device_z(1), y)
            )
            down_copy.append(
                sent(ring_down.at[i, :, rows_down, :], ring_down_in.at[i, :, rows_down, :], base + 4 + i, device_z(-1), y)
            )

        mine_z = []

        def collect():
            up_copy[3].wait_recv()
            down_copy[3].wait_recv()
            up_sum, down_sum = piece(0)
            up_sum = up_sum + f32(ring_up_in[3, :, 0:32, :]) + f32(ring_down_in[3, :, 0:32, :])
            down_sum = down_sum + f32(ring_up_in[3, :, 32:48, :]) + f32(ring_down_in[3, :, 32:48, :])
            for k in range(1, XN):
                by_x.up[k][...] = up_sum[k].astype(BF16)
                by_x.low[k][...] = down_sum[k].astype(BF16)
            mine_z.extend([up_sum[0], down_sum[0]])
            by_x.ahead()

        def final():
            a, b = by_x.arrived()
            write(n, mine_z[0] + a, mine_z[1] + b)

        return [functools.partial(hop, i) for i in range(4)] + [collect, by_x.later, final]

    def reduce_share():
        for copy in share1:
            copy.wait_recv()
        summed = groups[my_rows, :] + partial[my_rows, :]
        for o in range(1, yn):
            summed = summed + ar1[o - 1].astype(F32)
        io[my_rows, :] = summed.astype(BF16)
        for copy in share2:
            copy.start()

    def share():
        for copy in from2:
            copy.wait_recv()
        stores.append(pltpu.make_async_copy(io, io_out, store.at[2]))
        stores[2].start()

    steps = [iter(z_first(q) if q < NZ else x_first(q)) for q in range(NQ)]
    for i, q in enumerate(ORDER):
        if i == SHARE_AT:
            reduce_share()
        if i == STORE_AT:
            share()
        next(steps[q])()

    for copy in stores:
        copy.wait()
    for copy in step1 + step3 + swaps + share1 + share2:
        copy.wait_send()
    for o in range(1, len(step2)):
        pl.when(z + o < zn)(step2[o].wait_send)
    for copy in copies:
        copy.wait_send()


def finish(encoded, mct, io, up_sum, down_sum, mixed, up_out, down_out):
    both = io[...]
    spread = nn(mct[...], jnp.concatenate([both, both], axis=0))
    mixed[...] = (encoded[...].astype(F32) + spread).astype(BF16)
    up_out[...] = up_sum[...]
    down_out[...] = down_sum[...]


def on_device(
    zn, yn, tokens, positions, value_proj, write_proj, read_proj, step_proj, step_bias, decay_rate, reset_depth,
    out_proj, router, pad_vector, up_weight, down_weight, cotangent,
):
    sn = zn * PLANE
    ru, rd, qw = 2 * D // sn, D // sn, D // yn
    n_pos = positions.shape[0]
    vm = pltpu.VMEM
    n_sem = 2 * PLANE + zn + 4 + 3 * yn + NQ * 14
    scratch = [
        vm((ROWS, D), BF16), vm((1, n_pos), jnp.int32), vm((D, D), BF16), vm((D, 2 * NS), BF16), vm((HEADS, D), BF16),
        vm((1, HEADS), F32), vm((1, HEADS), F32), vm((1, ROWS), F32), vm((D, D), BF16), vm((1, D), F32),
        vm((8, D // 8), BF16), vm((2 * D, D), BF16), vm((D, D), BF16), vm((ROWS, D), BF16),
        vm((ROWS, D), BF16), vm((ROWS, 2 * NS), BF16), vm((ROWS, D), BF16), vm((CHUNKS, Q, Q), F32),
        vm((CHUNKS, Q, Q), F32), vm((2 * Q, D), BF16), vm((ROWS, D), BF16), vm((ROWS, D), F32), vm((NS, D), F32),
        vm((CHUNKS, NS, D), F32), vm((CHUNKS + 1, 8, D), F32), vm((ROWS, D), F32),
        vm((PLANE, 32, qw), BF16), vm((PLANE, 32, qw), BF16), vm((32, qw), BF16), vm((zn, 32, qw), BF16),
        vm((PLANE, 16, qw), BF16), vm((NS, D), BF16),
        vm((ROWS, D), BF16), vm((SLOTS, D), F32), vm((SLOTS, ROWS), BF16), vm((ROWS, 2 * SLOTS), BF16),
        vm((16, D), F32), vm((D, 128), F32), vm((8, 128), F32),
        vm((SLOTS, D), BF16), vm((SLOTS, D), BF16), vm((SLOTS, 128), F32), vm((SLOTS, D), F32),
        vm((2, 2 * SLOTS, D), BF16), vm((D, SLOTS), BF16), vm((2, XN, 128, 2 * SLOTS), BF16),
        vm((2, XN, 128, SLOTS), BF16),
        vm((8, D), F32), vm((8, D), F32),
        vm((SLOTS, D), F32), vm((SLOTS, D), BF16), vm((max(yn - 1, 1), SLOTS // yn, D), BF16), vm((SLOTS, D), BF16),
        [
            [vm((XN, 288, w), F32)] + [vm((4, XN, 48, w), BF16)] * 4
            + [vm((rows, w), BF16) for rows in (48, 48, 32, 16) * 2] for w in WIDTHS_Z
        ],
        [
            [vm((288, w), F32)] + [vm((rows, w), BF16) for rows in (80, 64) * 2] + [vm((4, 48, w), BF16)] * 2
            + [vm((rows, w), BF16) for rows in (PIECE, PIECE, 128, 144) * 2] for w in WIDTHS_X
        ],
        pltpu.SemaphoreType.DMA((15,)), pltpu.SemaphoreType.DMA((3,)), pltpu.SemaphoreType.DMA((n_sem,)), pltpu.SemaphoreType.DMA((n_sem,)),
    ]
    encoded, mct, io, up_sum, down_sum = pl.pallas_call(
        functools.partial(kernel, zn, yn),
        out_shape=(
            jax.ShapeDtypeStruct((ROWS, D), BF16),
            jax.ShapeDtypeStruct((ROWS, 2 * SLOTS), BF16),
            jax.ShapeDtypeStruct((SLOTS, D), BF16),
            jax.ShapeDtypeStruct((ru, D), F32),
            jax.ShapeDtypeStruct((rd, D), F32),
        ),
        in_specs=[pl.BlockSpec(memory_space=pl.ANY)] * 15,
        out_specs=(pl.BlockSpec(memory_space=pl.ANY),) * 3 + (pl.BlockSpec(memory_space=pltpu.VMEM),) * 2,
        scratch_shapes=scratch,
        compiler_params=pltpu.CompilerParams(
            collective_id=0, has_side_effects=True, vmem_limit_bytes=60 * 2**20
        ),
    )(
        tokens, positions.reshape(1, n_pos), value_proj, write_proj, read_proj, step_proj.T, step_bias.reshape(1, HEADS),
        decay_rate.reshape(1, HEADS), reset_depth.reshape(1, ROWS), out_proj, router.reshape(1, D),
        pad_vector.reshape(8, D // 8), up_weight, down_weight, cotangent,
    )
    part = ROWS // 4
    return pl.pallas_call(
        finish,
        grid=(4,),
        out_shape=(
            jax.ShapeDtypeStruct((ROWS, D), BF16),
            jax.ShapeDtypeStruct((ru, D), F32),
            jax.ShapeDtypeStruct((rd, D), F32),
        ),
        in_specs=[
            pl.BlockSpec((part, D), lambda i: (i, 0)),
            pl.BlockSpec((part, 2 * SLOTS), lambda i: (i, 0)),
            pl.BlockSpec((SLOTS, D), lambda i: (0, 0)),
            pl.BlockSpec((ru // 4, D), lambda i: (i, 0)),
            pl.BlockSpec((rd // 2, D), lambda i: (i // 2, 0)),
        ],
        out_specs=(
            pl.BlockSpec((part, D), lambda i: (i, 0)),
            pl.BlockSpec((ru // 4, D), lambda i: (i, 0)),
            pl.BlockSpec((rd // 2, D), lambda i: (i // 2, 0)),
        ),
        compiler_params=pltpu.CompilerParams(vmem_limit_bytes=60 * 2**20),
    )(encoded, mct, io, up_sum, down_sum)


def solution(mesh):
    placed = (
        P("seq", None), P(), P(), P(), P(), P(), P(), P(), P("seq"), P(), P(), P(),
        P(None, "mlp"), P(None, "mlp"), P("seq", None),
    )
    return jax.shard_map(
        functools.partial(on_device, mesh.shape["seq"] // PLANE, mesh.shape["mlp"]),
        mesh=mesh,
        in_specs=placed,
        out_specs=(P("seq", None), P("seq", "mlp"), P("seq", "mlp")),
        check_vma=False,
    )
```

```python
import functools

import jax
import jax.numpy as jnp
from jax import lax
from jax.experimental import pallas as pl
from jax.experimental.pallas import tpu as pltpu
from jax.sharding import PartitionSpec as P

F32, BF16 = jnp.float32, jnp.bfloat16
HIGHEST = lax.Precision.HIGHEST
MESH = pl.DeviceIdType.MESH

ROWS = 512
D = 1024
HEADS = 16
HEAD = 64
NS = 128
Q = 128
CHUNKS = ROWS // Q
SLOTS = 128
XN, CN = 4, 2
PLANE = XN * CN
WIDTHS_Z, WIDTHS_X = (256,), (256, 256, 128, 128)
NZ, NQ = len(WIDTHS_Z), len(WIDTHS_Z + WIDTHS_X)
ORDER = (
    0, 3, 2, 0, 1, 3, 0, 2, 4, 1, 3, 0, 2, 3, 4, 1, 0, 4, 3, 2, 0, 1, 4, 0, 2, 1, 4,
)
SHARE_AT, STORE_AT = 7, 16
PIECE = 272
EPS = 1e-05
G0, G1 = 0.7978845608028654, 0.044715


def nn(a, b):
    return jnp.dot(a, b, preferred_element_type=F32)


def nt(a, b):
    return lax.dot_general(a, b, (((1,), (1,)), ((), ())), preferred_element_type=F32)


def split3(x):
    hi = x.astype(BF16).astype(F32)
    mid = (x - hi).astype(BF16).astype(F32)
    return hi, mid, x - hi - mid


def in_rows(parts, shape):
    ids = lax.broadcasted_iota(jnp.int32, shape, 0)
    block = jnp.zeros(shape, F32)
    for i, part in enumerate(parts):
        block = jnp.where(ids == i, part, block)
    return block


def kernel(
    zn, yn,
    tokens, positions, value_proj, write_proj, read_proj, step_proj, step_bias, decay_rate, reset_depth,
    out_proj, router, pad_vector, up_weight, down_weight, cotangent,
    encoded_out, mct_out, io_out, up_out, down_out,
    tok, pos, vp, wr, sp, bias, rate, reset, op, rout, pad, up, down, cot,
    normed, kr, vals, zrow, zcol, expander, dtv, ece, state, chunk_state, dpre, within,
    p1s, p1r, p2s, p2r, p3s, incoming,
    encoded, groups, select, mct, padup, pad_col, padsq,
    xn, gg, scale, slope, fac, turned, lt, lto, vx, vr,
    partial, ars, ar1, io,
    along_z, along_x,
    load, store, ss, rs,
):
    sn = zn * PLANE
    ru, rd = 2 * D // sn, D // sn
    zh = zn // 2
    qw = D // yn
    seq, y = lax.axis_index("seq"), lax.axis_index("mlp")
    z, me = seq // PLANE, lax.rem(seq, PLANE)
    x, core = me // CN, lax.rem(me, CN)

    def plane_at(j):
        return z * PLANE + j

    pairs = [
        (tokens, tok), (write_proj, wr.at[:, 0:NS]), (read_proj, wr.at[:, NS : 2 * NS]), (step_proj, sp),
        (step_bias, bias), (decay_rate, rate), (reset_depth, reset), (value_proj, vp), (positions, pos),
        (pad_vector, pad), (out_proj, op), (router, rout), (up_weight, up), (cotangent, cot), (down_weight, down),
    ]
    loads = [pltpu.make_async_copy(a, b, load.at[i]) for i, (a, b) in enumerate(pairs)]
    for copy in loads[:8]:
        copy.start()

    barrier = pltpu.get_barrier_semaphore()
    partners = [
        (plane_at(lax.rem(me + o, PLANE)), lax.rem(y + oy, yn)) for oy in range(yn) for o in range(PLANE) if o or oy
    ]
    partners += [(lax.rem(z + o, zn) * PLANE + me, y) for o in range(1, zn)]
    for partner in partners:
        pl.semaphore_signal(barrier, inc=1, device_id=partner, device_id_type=MESH)

    count = [0]

    def ids(n):
        count[0] += n
        return count[0] - n

    def rdma(src, dst, i, to_seq, to_y):
        return pltpu.make_async_remote_copy(
            src_ref=src, dst_ref=dst, send_sem=ss.at[i], recv_sem=rs.at[i],
            device_id=(to_seq, to_y), device_id_type=MESH,
        )

    step1, step2, step3, from3, swaps, share1, share2, from2 = [], [None], [], [], [], [], [], []
    copies = []

    for copy in loads[:7]:
        copy.wait()

    def norm(b, carry):
        rows = pl.ds(pl.multiple_of(b * Q, Q), Q)
        field = tok[rows, :].astype(F32)
        ms = jnp.mean(field * field, axis=-1, keepdims=True)
        normed[rows, :] = (field * lax.rsqrt(ms + EPS)).astype(BF16)
        return carry

    lax.fori_loop(0, CHUNKS, norm, 0)
    e_row = lax.rem(lax.broadcasted_iota(jnp.int32, (2 * Q, D), 0), HEADS)
    e_col = lax.broadcasted_iota(jnp.int32, (2 * Q, D), 1) // HEAD
    expander[...] = (e_row == e_col).astype(F32).astype(BF16)

    eye = lax.broadcasted_iota(jnp.int32, (HEADS, HEADS), 0) == lax.broadcasted_iota(jnp.int32, (HEADS, HEADS), 1)

    def column(row):
        return jnp.sum(jnp.where(eye, jnp.broadcast_to(row, (HEADS, HEADS)), 0.0), axis=1, keepdims=True)

    kr[...] = nn(normed[...], wr[...]).astype(BF16)
    raw = nt(sp[...], normed[...]) + column(bias[...])
    dt_all = jnp.maximum(raw, 0.0) + jnp.log1p(jnp.exp(-jnp.abs(raw)))
    ld_all = -dt_all * column(rate[...]) - reset[...]
    s_id = lax.broadcasted_iota(jnp.int32, (Q, Q), 0)
    t_id = lax.broadcasted_iota(jnp.int32, (Q, Q), 1)
    before = (s_id <= t_id).astype(F32)
    for c in range(CHUNKS):
        cols = slice(c * Q, (c + 1) * Q)
        dt = dt_all[:, cols]
        cum = jnp.dot(ld_all[:, cols], before, precision=HIGHEST, preferred_element_type=F32)
        tail = jnp.exp(cum[:, Q - 1 : Q] - cum) * dt
        block = jnp.concatenate([dt, cum, tail, jnp.exp(cum), jnp.zeros((64, Q), F32)], axis=0)
        zrow[c] = block
        zcol[c] = block.T
    loads[7].wait()
    for copy in loads[8:]:
        copy.start()

    def values(b, carry):
        rows = pl.ds(pl.multiple_of(b * 256, 256), 256)
        vals[rows, :] = nn(normed[rows, :], vp[...]).astype(BF16)
        return carry

    lax.fori_loop(0, ROWS // 256, values, 0)

    state[...] = jnp.zeros_like(state)

    def chunk(c, decay):
        rows = pl.ds(pl.multiple_of(c * Q, Q), Q)
        zt = zcol[c]
        hi, mid, unused = split3(zt)
        kind = lax.broadcasted_iota(jnp.int32, (Q, Q), 1) // HEADS

        def expand(k):
            lhs = jnp.concatenate([jnp.where(kind == k, hi, 0.0), jnp.where(kind == k, mid, 0.0)], axis=1)
            return nn(lhs.astype(BF16), expander[...])

        v = vals[rows, :].astype(F32)
        dtv[rows, :] = (expand(0) * v).astype(BF16)
        weighted = (expand(2) * v).astype(BF16)
        grown = expand(3)
        ece[rows, :] = grown
        keys_t = kr[rows, 0:NS].astype(F32).T.astype(BF16)
        old = state[...]
        chunk_state[c] = old
        dpre[c] = jnp.broadcast_to(decay, (8, D))
        last = grown[Q - 1 : Q, :]
        state[...] = last * old + nn(keys_t, weighted)
        return decay * last

    decay = lax.fori_loop(0, CHUNKS, chunk, jnp.ones((1, D), F32))

    dpre[CHUNKS] = jnp.broadcast_to(decay, (8, D))
    mine = pl.ds(pl.multiple_of(y * qw, qw), qw)
    decay_rows = in_rows(split3(dpre[CHUNKS, 0:1, mine]), (16, qw)).astype(BF16)
    for j in range(PLANE):
        p1s[j, 0:16, :] = state[16 * j : 16 * j + 16, mine].astype(BF16)
        p1s[j, 16:32, :] = decay_rows
    p1r[0] = p1s[me]
    pl.semaphore_wait(barrier, len(partners))
    base = ids(PLANE)
    for o in range(1, PLANE):
        j = lax.rem(me + o, PLANE)
        step1.append(rdma(p1s.at[j], p1r.at[o], base + o, plane_at(j), y))
        step1[-1].start()

    def intra(c, carry):
        rows = pl.ds(pl.multiple_of(c * Q, Q), Q)
        scores = nt(kr[rows, NS : 2 * NS], kr[rows, 0:NS])
        scores = jnp.where(s_id >= t_id, scores, 0.0)
        first = lax.broadcasted_iota(jnp.int32, (Q, 2 * HEAD), 1) < HEAD
        zr, zt = zrow[c], zcol[c]
        for pair in range(HEADS // 2):
            lanes = slice(2 * HEAD * pair, 2 * HEAD * (pair + 1))
            both = dtv[rows, lanes].astype(F32)
            right = jnp.concatenate([jnp.where(first, both, 0.0), jnp.where(first, 0.0, both)], axis=0)
            mixing = []
            for h in (2 * pair, 2 * pair + 1):
                gap = zt[:, HEADS + h : HEADS + h + 1] - zr[HEADS + h : HEADS + h + 1, :]
                mixing.append(scores * jnp.exp(jnp.minimum(gap, 0.0)))
            within[rows, lanes] = nn(jnp.concatenate(mixing, axis=1).astype(BF16), right.astype(BF16))
        return carry

    lax.fori_loop(0, CHUNKS // 2, intra, 0)

    def read(block):
        block = block.astype(F32)
        return block[0:16], block[16:17] + block[17:18] + block[18:19]

    for copy in step1:
        copy.wait_recv()
    pre, pre_decay = [jnp.zeros((16, qw), F32)], [jnp.ones((1, qw), F32)]
    for k in range(PLANE):
        new, by = read(p1r[lax.rem(me - k + PLANE, PLANE)])
        pre.append(by * pre[-1] + new)
        pre_decay.append(by * pre_decay[-1])
    p2s[0:16, :] = pre[-1].astype(BF16)
    p2s[16:32, :] = in_rows(split3(pre_decay[-1]), (16, qw)).astype(BF16)
    p2r[0] = p2s[...]
    base = ids(zn)
    for o in range(1, zn):
        step2.append(rdma(p2s, p2r.at[o], base + o, lax.rem(z + o, zn) * PLANE + me, y))
        pl.when(z + o < zn)(step2[o].start)

    lax.fori_loop(CHUNKS // 2, CHUNKS, intra, 0)

    for o in range(1, zn):
        pl.when(z >= o)(step2[o].wait_recv)
    start = jnp.zeros((16, qw), F32)
    for k in range(zn - 1):
        new, by = read(p2r[jnp.maximum(z - k, 0)])
        start = jnp.where(k < z, by * start + new, start)
    for k in range(PLANE):
        p3s[k] = (pre_decay[k] * start + pre[k]).astype(BF16)

    def landing(j, at_y):
        return incoming.at[pl.ds(pl.multiple_of(j * 16, 16), 16), pl.ds(pl.multiple_of(at_y * qw, qw), qw)]

    base = ids(PLANE * yn)
    for o in range(PLANE):
        for oy in range(yn):
            if o or oy:
                i = base + o * yn + oy
                j, at_y = lax.rem(me + o, PLANE), lax.rem(y + oy, yn)
                step3.append(rdma(p3s.at[j], landing(me, y), i, plane_at(j), at_y))
                step3[-1].start()
                j, at_y = lax.rem(me - o + PLANE, PLANE), lax.rem(y - oy + yn, yn)
                from3.append(rdma(p3s.at[j], landing(j, at_y), i, plane_at(j), at_y))
    incoming[pl.ds(pl.multiple_of(me * 16, 16), 16), mine] = p3s[me]

    for copy in loads[8:]:
        copy.wait()
    local = pos[...] - seq * ROWS
    n_pos = local.shape[1]
    high, low = local >> 7, local & 127
    ids8 = lax.broadcasted_iota(jnp.int32, (8, n_pos), 0)
    left = jnp.where((jnp.broadcast_to(high, (8, n_pos)) == ids8) & (ids8 < CHUNKS), 1.0, 0.0).astype(BF16)
    ids128 = lax.broadcasted_iota(jnp.int32, (Q, n_pos), 0)
    right = jnp.where(jnp.broadcast_to(low, (Q, n_pos)) == ids128, 1.0, 0.0).astype(BF16)
    marks = nt(left, right)
    running = nn(marks.astype(BF16), before.astype(BF16))
    parts, so_far = [], jnp.zeros((1, 1), F32)
    for c in range(CHUNKS):
        parts.append(running[c : c + 1] + so_far)
        so_far = parts[-1][:, Q - 1 : Q]
    group_of = jnp.concatenate(parts, axis=1) - 1.0
    mark = jnp.concatenate([marks[c : c + 1] for c in range(CHUNKS)], axis=1)
    slot = lax.broadcasted_iota(jnp.int32, (SLOTS, ROWS), 0).astype(F32)
    member = jnp.where(slot == group_of, 1.0, 0.0)
    select[...] = (member * mark).astype(BF16)
    pad_rows = pad[...].astype(F32)
    pad_row = jnp.concatenate([pad_rows[i : i + 1] for i in range(8)], axis=1)
    padsq[...] = jnp.broadcast_to(jnp.sum(pad_row * pad_row, axis=-1, keepdims=True), (8, 128))
    pad_col[...] = jnp.broadcast_to(pad_row, (128, D)).T
    padup[...] = nn(jnp.broadcast_to(pad_row, (16, D)).astype(BF16), up[D : 2 * D, :])

    for copy in from3:
        copy.wait_recv()

    def encode(b, carry):
        for k in range(2):
            c = 2 * b + k
            rows = pl.ds(pl.multiple_of(c * Q, Q), Q)
            full = chunk_state[c] + dpre[c, 0:1, :] * incoming[...].astype(F32)
            carried = nn(kr[rows, NS : 2 * NS], full.astype(BF16))
            scanned = within[rows, :] + ece[rows, :] * carried
            ms = jnp.mean(scanned * scanned, axis=-1, keepdims=True)
            normed[rows, :] = (scanned * lax.rsqrt(ms + EPS)).astype(BF16)
        rows = pl.ds(pl.multiple_of(b * 256, 256), 256)
        encoded[rows, :] = (tok[rows, :].astype(F32) + nn(normed[rows, :], op[...])).astype(BF16)
        return carry

    lax.fori_loop(0, 2, encode, 0)
    logits = nt(in_rows(split3(rout[...]), (16, D)).astype(BF16), encoded[...])
    confidence = 1.0 / (1.0 + jnp.exp(-jnp.sum(logits, axis=0, keepdims=True)))
    weight = member * confidence
    weight_hi = weight.astype(BF16)
    weight_lo = (weight - weight_hi.astype(F32)).astype(BF16)
    mct[:, 0:SLOTS] = weight_hi.astype(F32).T.astype(BF16)
    mct[:, SLOTS : 2 * SLOTS] = weight_lo.astype(F32).T.astype(BF16)
    stores = [pltpu.make_async_copy(encoded, encoded_out, store.at[0]), pltpu.make_async_copy(mct, mct_out, store.at[1])]
    for copy in stores:
        copy.start()
    groups[...] = nn(select[...], encoded[...])
    grads = nn(weight_hi, cot[...]) + nn(weight_lo, cot[...])
    gg[...] = grads.astype(BF16)
    rows_f = groups[...]
    ms = (jnp.sum(rows_f * rows_f, axis=-1, keepdims=True) + padsq[0:1, 0:1]) * (0.5 / D)
    r = lax.rsqrt(ms + EPS)
    scale[...] = jnp.broadcast_to(r, (SLOTS, 128))
    inner = rows_f * r
    xn[...] = inner.astype(BF16)

    def turn(field, part, each, blocks):
        turned[...] = field.T.astype(BF16)
        for k in range(XN):
            at = lax.rem(x + k, XN)
            for b in range(blocks):
                rows = slice(b * each, (b + 1) * each)
                begin = (b * PLANE + at * CN + core) * each
                lt[part, k, rows, 0:SLOTS] = turned[pl.ds(pl.multiple_of(begin, 16), each), :]
                begin = (b * PLANE + at * CN + 1 - core) * each
                lto[part, k, rows, :] = turned[pl.ds(pl.multiple_of(begin, 16), each), :]

    turn(inner, 0, ru, zh)
    turn(grads, 1, rd, zn)
    mate = plane_at(x * CN + 1 - core)
    base = ids(4)
    swaps += [
        rdma(lto, lt.at[:, :, :, SLOTS : 2 * SLOTS], base, mate, y),
        rdma(fac.at[1, 0:SLOTS, :], fac.at[1, SLOTS : 2 * SLOTS, :], base + 1, mate, y),
        rdma(fac.at[0, 0:SLOTS, :], fac.at[0, SLOTS : 2 * SLOTS, :], base + 2, mate, y),
        rdma(vx, vr, base + 3, mate, y),
    ]
    swaps[0].start()

    def forward(b, carry):
        cols = pl.ds(pl.multiple_of(b * 256, 256), 256)
        pre_act = nn(xn[...], up[0:D, cols]) + scale[:, 0:1] * padup[0:1, cols]
        square = pre_act * pre_act
        bend = jnp.tanh(G0 * pre_act * (1.0 + G1 * square))
        fac[1, 0:SLOTS, cols] = (0.5 * pre_act * (1.0 + bend)).astype(BF16)
        slope[:, cols] = 0.5 * (1.0 + bend) + 0.5 * pre_act * (1.0 - bend * bend) * (
            G0 * (1.0 + 3.0 * G1 * square)
        )
        return carry

    lax.fori_loop(0, 4, forward, 0)
    swaps[1].start()

    def backward(b, carry):
        cols = pl.ds(pl.multiple_of(b * 256, 256), 256)
        pre_grad = (nn(gg[...], down[:, cols]) * slope[:, cols]).astype(BF16)
        fac[0, 0:SLOTS, cols] = pre_grad
        pad_term = jnp.sum(pre_grad.astype(F32) * scale[:, 0:1], axis=0, keepdims=True)
        vx[:, cols] = jnp.broadcast_to(pad_term, (8, 256))
        return carry

    lax.fori_loop(0, 4, backward, 0)
    swaps[2].start()
    swaps[3].start()

    rq = SLOTS // yn
    partial[...] = nt(fac[1, 0:SLOTS, :], down[...])
    ars[...] = partial[...].astype(BF16)
    base = ids(2 * yn)
    my_rows = pl.ds(pl.multiple_of(y * rq, rq), rq)
    for o in range(1, yn):
        at_y = lax.rem(y + o, yn)
        share1.append(rdma(ars.at[pl.ds(pl.multiple_of(at_y * rq, rq), rq), :], ar1.at[o - 1], base + o, seq, at_y))
        share1[-1].start()
        share2.append(rdma(io.at[my_rows, :], io.at[my_rows, :], base + yn + o, seq, at_y))
        at_y = lax.rem(y - o + yn, yn)
        other = pl.ds(pl.multiple_of(at_y * rq, rq), rq)
        from2.append(rdma(io.at[other, :], io.at[other, :], base + yn + o, seq, at_y))

    for copy in swaps:
        copy.wait_recv()
    right_x = plane_at(lax.rem(x + 1, XN) * CN + core)
    left_x = plane_at(lax.rem(x + XN - 1, XN) * CN + core)

    def on_z(o):
        return lax.rem(z + o + zn, zn)

    def device_z(o):
        return on_z(o) * PLANE + me

    def sent(*args):
        copy = rdma(*args)
        copy.start()
        copies.append(copy)
        return copy

    def f32(block):
        return block.astype(F32)

    class AlongX:
        def __init__(self, upper, lower, refs):
            self.near_r, self.near_l, self.end_r, self.end_l = refs[:4]
            self.near_r_in, self.near_l_in, self.end_r_in, self.end_l_in = refs[4:]
            self.cut_r, self.cut_l = upper, lower
            self.up = {1: self.end_r, 2: self.near_r.at[0:upper, :], 3: self.near_l.at[lower:, :]}
            self.low = {1: self.near_r.at[upper:, :], 2: self.near_l.at[0:lower, :], 3: self.end_l}
            self.base = ids(6)

        def ahead(self):
            i, far_r, far_l = self.base, slice(0, self.cut_r), slice(0, self.cut_l)
            near_r, near_l = slice(self.cut_r, None), slice(self.cut_l, None)
            self.far = [
                sent(self.near_r.at[far_r, :], self.near_r_in.at[far_r, :], i, right_x, y),
                sent(self.near_l.at[far_l, :], self.near_l_in.at[far_l, :], i + 1, left_x, y),
            ]
            self.end = [
                sent(self.near_r.at[near_r, :], self.near_r_in.at[near_r, :], i + 2, right_x, y),
                sent(self.near_l.at[near_l, :], self.near_l_in.at[near_l, :], i + 3, left_x, y),
            ]

        def later(self):
            i = self.base
            self.far[0].wait_recv()
            self.end_r[...] = (f32(self.end_r[...]) + f32(self.near_r_in[0 : self.cut_r, :])).astype(BF16)
            self.end.append(sent(self.end_r, self.end_r_in, i + 4, right_x, y))
            self.far[1].wait_recv()
            self.end_l[...] = (f32(self.end_l[...]) + f32(self.near_l_in[0 : self.cut_l, :])).astype(BF16)
            self.end.append(sent(self.end_l, self.end_l_in, i + 5, left_x, y))

        def arrived(self):
            for copy in self.end:
                copy.wait_recv()
            return (
                f32(self.near_l_in[self.cut_l :, :]) + f32(self.end_r_in[...]),
                f32(self.near_r_in[self.cut_r :, :]) + f32(self.end_l_in[...]),
            )

    def up_rows(t):
        return pl.ds(pl.multiple_of(jnp.where(t < zh, ru * t, 256), 16), ru)

    def down_rows(t):
        return pl.ds(pl.multiple_of(128 + rd * t, 16), rd)

    pad_part = pad_col[pl.ds(pl.multiple_of(ru * jnp.maximum(seq - sn // 2, 0), 16), ru), 0:1]

    widths = WIDTHS_Z + WIDTHS_X

    def columns(q):
        return slice(sum(widths[:q]), sum(widths[: q + 1]))

    def write(q, up_sum, down_sum):
        cols = columns(q)
        up_out[:, cols] = jnp.where(z < zh, up_sum, pad_part * up_sum[0:1])
        down_out[:, cols] = down_sum

    def terms(q):
        cols = columns(q)
        for part in range(2):
            yield nn(lt[part].reshape(XN * 128, 2 * SLOTS), fac[part, :, cols])
        yield in_rows([vx[0:1, cols] + vr[0:1, cols]], (32, widths[q]))

    def x_first(q):
        own, za_up, za_down, za_up_in, za_down_in, zb, zb_in, *rest = along_x[q - NZ]
        by_x = AlongX(128, 144, rest)
        base = ids(6)

        def piece(o):
            t = on_z(o)
            return own[up_rows(t), :], own[down_rows(t), :]

        def first():
            for part, term in enumerate(terms(q)):
                if part < 2:
                    rows = slice(128 * part, 128 * part + 128)
                    own[rows, :] = term[0:128]
                    for k in range(1, XN):
                        (by_x.low if part else by_x.up)[k][0:128, :] = term[128 * k : 128 * k + 128].astype(BF16)
                else:
                    own[256:288, :] = term
                    for k in range(1, XN):
                        by_x.low[k][128:144, :] = term[0:16].astype(BF16)
            by_x.ahead()

        def two_away():
            a, b = by_x.arrived()
            own[0:128, :] += a
            own[128:PIECE, :] += b
            za_up[0:32, :] = piece(4)[0].astype(BF16)
            near = piece(3)
            za_up[32:64, :] = near[0].astype(BF16)
            za_up[64:80, :] = near[1].astype(BF16)
            far.append(sent(za_up, za_up_in, base, device_z(2), y))
            za_down[0:16, :] = piece(-4)[1].astype(BF16)
            near = piece(-3)
            za_down[16:32, :] = near[1].astype(BF16)
            za_down[32:64, :] = near[0].astype(BF16)
            far.append(sent(za_down, za_down_in, base + 1, device_z(-2), y))

        far, last = [], []

        def nearer():
            for copy in far:
                copy.wait_recv()
            from_up, from_down = f32(za_up_in[...]), f32(za_down_in[...])
            for i, o in enumerate((2, -2, 1, -1)):
                up_sum, down_sum = piece(o)
                if o == 2:
                    up_sum = up_sum + from_up[0:32]
                elif o == -2:
                    down_sum = down_sum + from_down[0:16]
                elif o == 1:
                    up_sum, down_sum = up_sum + from_up[32:64], down_sum + from_up[64:80]
                else:
                    up_sum, down_sum = up_sum + from_down[32:64], down_sum + from_down[16:32]
                zb[i, 0:32, :] = up_sum.astype(BF16)
                zb[i, 32:48, :] = down_sum.astype(BF16)
                last.append(sent(zb.at[i], zb_in.at[i], base + 2 + i, device_z(o), y))

        def final():
            for copy in last:
                copy.wait_recv()
            up_sum, down_sum = piece(0)
            for i in range(4):
                up_sum = up_sum + f32(zb_in[i, 0:32, :])
                down_sum = down_sum + f32(zb_in[i, 32:48, :])
            write(q, up_sum, down_sum)

        return [first, by_x.later, two_away, nearer, final]

    def z_first(n):
        prod_z, ring_up, ring_down, ring_up_in, ring_down_in, *rest = along_z[n]
        by_x = AlongX(32, 16, rest)
        base = ids(8)
        up_copy, down_copy = [], []

        def piece(o):
            t = on_z(o)
            return prod_z[:, up_rows(t), :], prod_z[:, down_rows(t), :]

        def hop(i):
            if i == 0:
                for part, term in enumerate(terms(n)):
                    for k in range(XN):
                        if part < 2:
                            prod_z[k, 128 * part : 128 * part + 128, :] = term[128 * k : 128 * k + 128]
                        else:
                            prod_z[k, 256:288, :] = term
                ring_up[0, :, 0:32, :] = piece(4)[0].astype(BF16)
                ring_down[0, :, 32:48, :] = piece(-4)[1].astype(BF16)
                rows_up, rows_down = slice(0, 32), slice(32, 48)
            else:
                up_copy[i - 1].wait_recv()
                up_sum, down_sum = piece(4 - i)
                up_sum = up_sum + f32(ring_up_in[i - 1, :, 0:32, :])
                if i > 1:
                    down_sum = down_sum + f32(ring_up_in[i - 1, :, 32:48, :])
                ring_up[i, :, 0:32, :] = up_sum.astype(BF16)
                ring_up[i, :, 32:48, :] = down_sum.astype(BF16)
                down_copy[i - 1].wait_recv()
                up_sum, down_sum = piece(i - 4)
                down_sum = down_sum + f32(ring_down_in[i - 1, :, 32:48, :])
                if i > 1:
                    up_sum = up_sum + f32(ring_down_in[i - 1, :, 0:32, :])
                ring_down[i, :, 0:32, :] = up_sum.astype(BF16)
                ring_down[i, :, 32:48, :] = down_sum.astype(BF16)
                rows_up = rows_down = slice(0, 48)
            up_copy.append(
                sent(ring_up.at[i, :, rows_up, :], ring_up_in.at[i, :, rows_up, :], base + i, device_z(1), y)
            )
            down_copy.append(
                sent(ring_down.at[i, :, rows_down, :], ring_down_in.at[i, :, rows_down, :], base + 4 + i, device_z(-1), y)
            )

        mine_z = []

        def collect():
            up_copy[3].wait_recv()
            down_copy[3].wait_recv()
            up_sum, down_sum = piece(0)
            up_sum = up_sum + f32(ring_up_in[3, :, 0:32, :]) + f32(ring_down_in[3, :, 0:32, :])
            down_sum = down_sum + f32(ring_up_in[3, :, 32:48, :]) + f32(ring_down_in[3, :, 32:48, :])
            for k in range(1, XN):
                by_x.up[k][...] = up_sum[k].astype(BF16)
                by_x.low[k][...] = down_sum[k].astype(BF16)
            mine_z.extend([up_sum[0], down_sum[0]])
            by_x.ahead()

        def final():
            a, b = by_x.arrived()
            write(n, mine_z[0] + a, mine_z[1] + b)

        return [functools.partial(hop, i) for i in range(4)] + [collect, by_x.later, final]

    def reduce_share():
        for copy in share1:
            copy.wait_recv()
        summed = groups[my_rows, :] + partial[my_rows, :]
        for o in range(1, yn):
            summed = summed + ar1[o - 1].astype(F32)
        io[my_rows, :] = summed.astype(BF16)
        for copy in share2:
            copy.start()

    def share():
        for copy in from2:
            copy.wait_recv()
        stores.append(pltpu.make_async_copy(io, io_out, store.at[2]))
        stores[2].start()

    steps = [iter(z_first(q) if q < NZ else x_first(q)) for q in range(NQ)]
    for i, q in enumerate(ORDER):
        if i == SHARE_AT:
            reduce_share()
        if i == STORE_AT:
            share()
        next(steps[q])()

    for copy in stores:
        copy.wait()
    for copy in step1 + step3 + swaps + share1 + share2:
        copy.wait_send()
    for o in range(1, len(step2)):
        pl.when(z + o < zn)(step2[o].wait_send)
    for copy in copies:
        copy.wait_send()


def finish(encoded, mct, io, up_sum, down_sum, mixed, up_out, down_out):
    both = io[...]
    spread = nn(mct[...], jnp.concatenate([both, both], axis=0))
    mixed[...] = (encoded[...].astype(F32) + spread).astype(BF16)
    up_out[...] = up_sum[...]
    down_out[...] = down_sum[...]


def on_device(
    zn, yn, tokens, positions, value_proj, write_proj, read_proj, step_proj, step_bias, decay_rate, reset_depth,
    out_proj, router, pad_vector, up_weight, down_weight, cotangent,
):
    sn = zn * PLANE
    ru, rd, qw = 2 * D // sn, D // sn, D // yn
    n_pos = positions.shape[0]
    vm = pltpu.VMEM
    n_sem = PLANE + zn + PLANE * yn + 4 + 2 * yn + NQ * 14
    scratch = [
        vm((ROWS, D), BF16), vm((1, n_pos), jnp.int32), vm((D, D), BF16), vm((D, 2 * NS), BF16), vm((HEADS, D), BF16),
        vm((1, HEADS), F32), vm((1, HEADS), F32), vm((1, ROWS), F32), vm((D, D), BF16), vm((1, D), F32),
        vm((8, D // 8), BF16), vm((2 * D, D), BF16), vm((D, D), BF16), vm((ROWS, D), BF16),
        vm((ROWS, D), BF16), vm((ROWS, 2 * NS), BF16), vm((ROWS, D), BF16), vm((CHUNKS, Q, Q), F32),
        vm((CHUNKS, Q, Q), F32), vm((2 * Q, D), BF16), vm((ROWS, D), BF16), vm((ROWS, D), F32), vm((NS, D), F32),
        vm((CHUNKS, NS, D), F32), vm((CHUNKS + 1, 8, D), F32), vm((ROWS, D), F32),
        vm((PLANE, 32, qw), BF16), vm((PLANE, 32, qw), BF16), vm((32, qw), BF16), vm((zn, 32, qw), BF16),
        vm((PLANE, 16, qw), BF16), vm((NS, D), BF16),
        vm((ROWS, D), BF16), vm((SLOTS, D), F32), vm((SLOTS, ROWS), BF16), vm((ROWS, 2 * SLOTS), BF16),
        vm((16, D), F32), vm((D, 128), F32), vm((8, 128), F32),
        vm((SLOTS, D), BF16), vm((SLOTS, D), BF16), vm((SLOTS, 128), F32), vm((SLOTS, D), F32),
        vm((2, 2 * SLOTS, D), BF16), vm((D, SLOTS), BF16), vm((2, XN, 128, 2 * SLOTS), BF16),
        vm((2, XN, 128, SLOTS), BF16),
        vm((8, D), F32), vm((8, D), F32),
        vm((SLOTS, D), F32), vm((SLOTS, D), BF16), vm((max(yn - 1, 1), SLOTS // yn, D), BF16), vm((SLOTS, D), BF16),
        [
            [vm((XN, 288, w), F32)] + [vm((4, XN, 48, w), BF16)] * 4
            + [vm((rows, w), BF16) for rows in (48, 48, 32, 16) * 2] for w in WIDTHS_Z
        ],
        [
            [vm((288, w), F32)] + [vm((rows, w), BF16) for rows in (80, 64) * 2] + [vm((4, 48, w), BF16)] * 2
            + [vm((rows, w), BF16) for rows in (PIECE, PIECE, 128, 144) * 2] for w in WIDTHS_X
        ],
        pltpu.SemaphoreType.DMA((15,)), pltpu.SemaphoreType.DMA((3,)), pltpu.SemaphoreType.DMA((n_sem,)), pltpu.SemaphoreType.DMA((n_sem,)),
    ]
    encoded, mct, io, up_sum, down_sum = pl.pallas_call(
        functools.partial(kernel, zn, yn),
        out_shape=(
            jax.ShapeDtypeStruct((ROWS, D), BF16),
            jax.ShapeDtypeStruct((ROWS, 2 * SLOTS), BF16),
            jax.ShapeDtypeStruct((SLOTS, D), BF16),
            jax.ShapeDtypeStruct((ru, D), F32),
            jax.ShapeDtypeStruct((rd, D), F32),
        ),
        in_specs=[pl.BlockSpec(memory_space=pl.ANY)] * 15,
        out_specs=(pl.BlockSpec(memory_space=pl.ANY),) * 3 + (pl.BlockSpec(memory_space=pltpu.VMEM),) * 2,
        scratch_shapes=scratch,
        compiler_params=pltpu.CompilerParams(
            collective_id=0, has_side_effects=True, vmem_limit_bytes=60 * 2**20
        ),
    )(
        tokens, positions.reshape(1, n_pos), value_proj, write_proj, read_proj, step_proj.T, step_bias.reshape(1, HEADS),
        decay_rate.reshape(1, HEADS), reset_depth.reshape(1, ROWS), out_proj, router.reshape(1, D),
        pad_vector.reshape(8, D // 8), up_weight, down_weight, cotangent,
    )
    part = ROWS // 2
    return pl.pallas_call(
        finish,
        grid=(2,),
        out_shape=(
            jax.ShapeDtypeStruct((ROWS, D), BF16),
            jax.ShapeDtypeStruct((ru, D), F32),
            jax.ShapeDtypeStruct((rd, D), F32),
        ),
        in_specs=[
            pl.BlockSpec((part, D), lambda i: (i, 0)),
            pl.BlockSpec((part, 2 * SLOTS), lambda i: (i, 0)),
            pl.BlockSpec((SLOTS, D), lambda i: (0, 0)),
            pl.BlockSpec((ru // 2, D), lambda i: (i, 0)),
            pl.BlockSpec((rd // 2, D), lambda i: (i, 0)),
        ],
        out_specs=(
            pl.BlockSpec((part, D), lambda i: (i, 0)),
            pl.BlockSpec((ru // 2, D), lambda i: (i, 0)),
            pl.BlockSpec((rd // 2, D), lambda i: (i, 0)),
        ),
        compiler_params=pltpu.CompilerParams(vmem_limit_bytes=60 * 2**20),
    )(encoded, mct, io, up_sum, down_sum)


def solution(mesh):
    placed = (
        P("seq", None), P(), P(), P(), P(), P(), P(), P(), P("seq"), P(), P(), P(),
        P(None, "mlp"), P(None, "mlp"), P("seq", None),
    )
    return jax.shard_map(
        functools.partial(on_device, mesh.shape["seq"] // PLANE, mesh.shape["mlp"]),
        mesh=mesh,
        in_specs=placed,
        out_specs=(P("seq", None), P("seq", "mlp"), P("seq", "mlp")),
        check_vma=False,
    )
```

```python
import functools

import jax
import jax.numpy as jnp
from jax import lax
from jax.experimental import pallas as pl
from jax.experimental.pallas import tpu as pltpu
from jax.sharding import PartitionSpec as P

F32, BF16 = jnp.float32, jnp.bfloat16
HIGHEST = lax.Precision.HIGHEST
MESH = pl.DeviceIdType.MESH

ROWS = 512
D = 1024
HEADS = 16
HEAD = 64
NS = 128
Q = 128
CHUNKS = ROWS // Q
SLOTS = 128
XN, CN = 4, 2
PLANE = XN * CN
WIDTHS_Z, WIDTHS_X = (256,), (256, 256, 128, 128)
NZ, NQ = len(WIDTHS_Z), len(WIDTHS_Z + WIDTHS_X)
ORDER = (
    0, 3, 2, 0, 1, 3, 0, 2, 4, 1, 3, 0, 2, 3, 4, 1, 0, 4, 3, 2, 0, 1, 4, 0, 2, 1, 4,
)
SHARE_AT, STORE_AT = 12, 21
PIECE = 272
EPS = 1e-05
G0, G1 = 0.7978845608028654, 0.044715


def nn(a, b):
    return jnp.dot(a, b, preferred_element_type=F32)


def nt(a, b):
    return lax.dot_general(a, b, (((1,), (1,)), ((), ())), preferred_element_type=F32)


def split3(x):
    hi = x.astype(BF16).astype(F32)
    mid = (x - hi).astype(BF16).astype(F32)
    return hi, mid, x - hi - mid


def in_rows(parts, shape):
    ids = lax.broadcasted_iota(jnp.int32, shape, 0)
    block = jnp.zeros(shape, F32)
    for i, part in enumerate(parts):
        block = jnp.where(ids == i, part, block)
    return block


def kernel(
    zn, yn,
    tokens, positions, value_proj, write_proj, read_proj, step_proj, step_bias, decay_rate, reset_depth,
    out_proj, router, pad_vector, up_weight, down_weight, cotangent,
    encoded_out, mct_out, io_out, up_out, down_out,
    tok, pos, vp, wr, sp, bias, rate, reset, op, rout, pad, up, down, cot,
    normed, kr, vals, zrow, zcol, expander, dtv, ece, state, chunk_state, dpre, within,
    p1s, p1r, p2s, p2r, p3s, incoming,
    encoded, groups, select, mct, padup, pad_col, padsq,
    xn, gg, scale, slope, fac, turned, lt, lto, vx, vr,
    partial, ars, ar1, io,
    along_z, along_x,
    load, store, ss, rs,
):
    sn = zn * PLANE
    ru, rd = 2 * D // sn, D // sn
    zh = zn // 2
    qw = D // yn
    seq, y = lax.axis_index("seq"), lax.axis_index("mlp")
    z, me = seq // PLANE, lax.rem(seq, PLANE)
    x, core = me // CN, lax.rem(me, CN)

    def plane_at(j):
        return z * PLANE + j

    pairs = [
        (tokens, tok), (write_proj, wr.at[:, 0:NS]), (read_proj, wr.at[:, NS : 2 * NS]), (step_proj, sp),
        (step_bias, bias), (decay_rate, rate), (reset_depth, reset), (value_proj, vp), (positions, pos),
        (pad_vector, pad), (out_proj, op), (router, rout), (up_weight, up), (cotangent, cot), (down_weight, down),
    ]
    loads = [pltpu.make_async_copy(a, b, load.at[i]) for i, (a, b) in enumerate(pairs)]
    for copy in loads[:8]:
        copy.start()

    barrier = pltpu.get_barrier_semaphore()
    partners = [
        (plane_at(lax.rem(me + o, PLANE)), lax.rem(y + oy, yn)) for oy in range(yn) for o in range(PLANE) if o or oy
    ]
    partners += [(lax.rem(z + o, zn) * PLANE + me, y) for o in range(1, zn)]
    for partner in partners:
        pl.semaphore_signal(barrier, inc=1, device_id=partner, device_id_type=MESH)

    count = [0]

    def ids(n):
        count[0] += n
        return count[0] - n

    def rdma(src, dst, i, to_seq, to_y):
        return pltpu.make_async_remote_copy(
            src_ref=src, dst_ref=dst, send_sem=ss.at[i], recv_sem=rs.at[i],
            device_id=(to_seq, to_y), device_id_type=MESH,
        )

    step1, step2, step3, from3, swaps, share1, share2, from2 = [], [None], [], [], [], [], [], []
    copies = []

    for copy in loads[:7]:
        copy.wait()

    def norm(b, carry):
        rows = pl.ds(pl.multiple_of(b * Q, Q), Q)
        field = tok[rows, :].astype(F32)
        ms = jnp.mean(field * field, axis=-1, keepdims=True)
        normed[rows, :] = (field * lax.rsqrt(ms + EPS)).astype(BF16)
        return carry

    lax.fori_loop(0, CHUNKS, norm, 0)
    e_row = lax.rem(lax.broadcasted_iota(jnp.int32, (2 * Q, D), 0), HEADS)
    e_col = lax.broadcasted_iota(jnp.int32, (2 * Q, D), 1) // HEAD
    expander[...] = (e_row == e_col).astype(F32).astype(BF16)

    eye = lax.broadcasted_iota(jnp.int32, (HEADS, HEADS), 0) == lax.broadcasted_iota(jnp.int32, (HEADS, HEADS), 1)

    def column(row):
        return jnp.sum(jnp.where(eye, jnp.broadcast_to(row, (HEADS, HEADS)), 0.0), axis=1, keepdims=True)

    kr[...] = nn(normed[...], wr[...]).astype(BF16)
    raw = nt(sp[...], normed[...]) + column(bias[...])
    dt_all = jnp.maximum(raw, 0.0) + jnp.log1p(jnp.exp(-jnp.abs(raw)))
    ld_all = -dt_all * column(rate[...]) - reset[...]
    s_id = lax.broadcasted_iota(jnp.int32, (Q, Q), 0)
    t_id = lax.broadcasted_iota(jnp.int32, (Q, Q), 1)
    before = (s_id <= t_id).astype(F32)
    for c in range(CHUNKS):
        cols = slice(c * Q, (c + 1) * Q)
        dt = dt_all[:, cols]
        cum = jnp.dot(ld_all[:, cols], before, precision=HIGHEST, preferred_element_type=F32)
        tail = jnp.exp(cum[:, Q - 1 : Q] - cum) * dt
        block = jnp.concatenate([dt, cum, tail, jnp.exp(cum), jnp.zeros((64, Q), F32)], axis=0)
        zrow[c] = block
        zcol[c] = block.T
    loads[7].wait()
    for copy in loads[8:]:
        copy.start()

    def values(b, carry):
        rows = pl.ds(pl.multiple_of(b * 256, 256), 256)
        vals[rows, :] = nn(normed[rows, :], vp[...]).astype(BF16)
        return carry

    lax.fori_loop(0, ROWS // 256, values, 0)

    state[...] = jnp.zeros_like(state)

    def chunk(c, decay):
        rows = pl.ds(pl.multiple_of(c * Q, Q), Q)
        zt = zcol[c]
        hi, mid, unused = split3(zt)
        kind = lax.broadcasted_iota(jnp.int32, (Q, Q), 1) // HEADS

        def expand(k):
            lhs = jnp.concatenate([jnp.where(kind == k, hi, 0.0), jnp.where(kind == k, mid, 0.0)], axis=1)
            return nn(lhs.astype(BF16), expander[...])

        v = vals[rows, :].astype(F32)
        dtv[rows, :] = (expand(0) * v).astype(BF16)
        weighted = (expand(2) * v).astype(BF16)
        grown = expand(3)
        ece[rows, :] = grown
        keys_t = kr[rows, 0:NS].astype(F32).T.astype(BF16)
        old = state[...]
        chunk_state[c] = old
        dpre[c] = jnp.broadcast_to(decay, (8, D))
        last = grown[Q - 1 : Q, :]
        state[...] = last * old + nn(keys_t, weighted)
        return decay * last

    decay = lax.fori_loop(0, CHUNKS, chunk, jnp.ones((1, D), F32))

    dpre[CHUNKS] = jnp.broadcast_to(decay, (8, D))
    mine = pl.ds(pl.multiple_of(y * qw, qw), qw)
    decay_rows = in_rows(split3(dpre[CHUNKS, 0:1, mine]), (16, qw)).astype(BF16)
    for j in range(PLANE):
        p1s[j, 0:16, :] = state[16 * j : 16 * j + 16, mine].astype(BF16)
        p1s[j, 16:32, :] = decay_rows
    p1r[0] = p1s[me]
    pl.semaphore_wait(barrier, len(partners))
    base = ids(PLANE)
    for o in range(1, PLANE):
        j = lax.rem(me + o, PLANE)
        step1.append(rdma(p1s.at[j], p1r.at[o], base + o, plane_at(j), y))
        step1[-1].start()

    def intra(c, carry):
        rows = pl.ds(pl.multiple_of(c * Q, Q), Q)
        scores = nt(kr[rows, NS : 2 * NS], kr[rows, 0:NS])
        scores = jnp.where(s_id >= t_id, scores, 0.0)
        first = lax.broadcasted_iota(jnp.int32, (Q, 2 * HEAD), 1) < HEAD
        zr, zt = zrow[c], zcol[c]
        for pair in range(HEADS // 2):
            lanes = slice(2 * HEAD * pair, 2 * HEAD * (pair + 1))
            both = dtv[rows, lanes].astype(F32)
            right = jnp.concatenate([jnp.where(first, both, 0.0), jnp.where(first, 0.0, both)], axis=0)
            mixing = []
            for h in (2 * pair, 2 * pair + 1):
                gap = zt[:, HEADS + h : HEADS + h + 1] - zr[HEADS + h : HEADS + h + 1, :]
                mixing.append(scores * jnp.exp(jnp.minimum(gap, 0.0)))
            within[rows, lanes] = nn(jnp.concatenate(mixing, axis=1).astype(BF16), right.astype(BF16))
        return carry

    lax.fori_loop(0, CHUNKS // 2, intra, 0)

    def read(block):
        block = block.astype(F32)
        return block[0:16], block[16:17] + block[17:18] + block[18:19]

    for copy in step1:
        copy.wait_recv()
    pre, pre_decay = [jnp.zeros((16, qw), F32)], [jnp.ones((1, qw), F32)]
    for k in range(PLANE):
        new, by = read(p1r[lax.rem(me - k + PLANE, PLANE)])
        pre.append(by * pre[-1] + new)
        pre_decay.append(by * pre_decay[-1])
    p2s[0:16, :] = pre[-1].astype(BF16)
    p2s[16:32, :] = in_rows(split3(pre_decay[-1]), (16, qw)).astype(BF16)
    p2r[0] = p2s[...]
    base = ids(zn)
    for o in range(1, zn):
        step2.append(rdma(p2s, p2r.at[o], base + o, lax.rem(z + o, zn) * PLANE + me, y))
        pl.when(z + o < zn)(step2[o].start)

    lax.fori_loop(CHUNKS // 2, CHUNKS, intra, 0)

    for o in range(1, zn):
        pl.when(z >= o)(step2[o].wait_recv)
    start = jnp.zeros((16, qw), F32)
    for k in range(zn - 1):
        new, by = read(p2r[jnp.maximum(z - k, 0)])
        start = jnp.where(k < z, by * start + new, start)
    for k in range(PLANE):
        p3s[k] = (pre_decay[k] * start + pre[k]).astype(BF16)

    def landing(j, at_y):
        return incoming.at[pl.ds(pl.multiple_of(j * 16, 16), 16), pl.ds(pl.multiple_of(at_y * qw, qw), qw)]

    base = ids(PLANE * yn)
    for o in range(PLANE):
        for oy in range(yn):
            if o or oy:
                i = base + o * yn + oy
                j, at_y = lax.rem(me + o, PLANE), lax.rem(y + oy, yn)
                step3.append(rdma(p3s.at[j], landing(me, y), i, plane_at(j), at_y))
                step3[-1].start()
                j, at_y = lax.rem(me - o + PLANE, PLANE), lax.rem(y - oy + yn, yn)
                from3.append(rdma(p3s.at[j], landing(j, at_y), i, plane_at(j), at_y))
    incoming[pl.ds(pl.multiple_of(me * 16, 16), 16), mine] = p3s[me]

    for copy in loads[8:]:
        copy.wait()
    local = pos[...] - seq * ROWS
    n_pos = local.shape[1]
    high, low = local >> 7, local & 127
    ids8 = lax.broadcasted_iota(jnp.int32, (8, n_pos), 0)
    left = jnp.where((jnp.broadcast_to(high, (8, n_pos)) == ids8) & (ids8 < CHUNKS), 1.0, 0.0).astype(BF16)
    ids128 = lax.broadcasted_iota(jnp.int32, (Q, n_pos), 0)
    right = jnp.where(jnp.broadcast_to(low, (Q, n_pos)) == ids128, 1.0, 0.0).astype(BF16)
    marks = nt(left, right)
    running = nn(marks.astype(BF16), before.astype(BF16))
    parts, so_far = [], jnp.zeros((1, 1), F32)
    for c in range(CHUNKS):
        parts.append(running[c : c + 1] + so_far)
        so_far = parts[-1][:, Q - 1 : Q]
    group_of = jnp.concatenate(parts, axis=1) - 1.0
    mark = jnp.concatenate([marks[c : c + 1] for c in range(CHUNKS)], axis=1)
    slot = lax.broadcasted_iota(jnp.int32, (SLOTS, ROWS), 0).astype(F32)
    member = jnp.where(slot == group_of, 1.0, 0.0)
    select[...] = (member * mark).astype(BF16)
    pad_rows = pad[...].astype(F32)
    pad_row = jnp.concatenate([pad_rows[i : i + 1] for i in range(8)], axis=1)
    padsq[...] = jnp.broadcast_to(jnp.sum(pad_row * pad_row, axis=-1, keepdims=True), (8, 128))
    pad_col[...] = jnp.broadcast_to(pad_row, (128, D)).T
    padup[...] = nn(jnp.broadcast_to(pad_row, (16, D)).astype(BF16), up[D : 2 * D, :])

    for copy in from3:
        copy.wait_recv()

    def encode(b, carry):
        for k in range(2):
            c = 2 * b + k
            rows = pl.ds(pl.multiple_of(c * Q, Q), Q)
            full = chunk_state[c] + dpre[c, 0:1, :] * incoming[...].astype(F32)
            carried = nn(kr[rows, NS : 2 * NS], full.astype(BF16))
            scanned = within[rows, :] + ece[rows, :] * carried
            ms = jnp.mean(scanned * scanned, axis=-1, keepdims=True)
            normed[rows, :] = (scanned * lax.rsqrt(ms + EPS)).astype(BF16)
        rows = pl.ds(pl.multiple_of(b * 256, 256), 256)
        encoded[rows, :] = (tok[rows, :].astype(F32) + nn(normed[rows, :], op[...])).astype(BF16)
        return carry

    lax.fori_loop(0, 2, encode, 0)
    logits = nt(in_rows(split3(rout[...]), (16, D)).astype(BF16), encoded[...])
    confidence = 1.0 / (1.0 + jnp.exp(-jnp.sum(logits, axis=0, keepdims=True)))
    weight = member * confidence
    weight_hi = weight.astype(BF16)
    weight_lo = (weight - weight_hi.astype(F32)).astype(BF16)
    mct[:, 0:SLOTS] = weight_hi.astype(F32).T.astype(BF16)
    mct[:, SLOTS : 2 * SLOTS] = weight_lo.astype(F32).T.astype(BF16)
    stores = [pltpu.make_async_copy(encoded, encoded_out, store.at[0]), pltpu.make_async_copy(mct, mct_out, store.at[1])]
    for copy in stores:
        copy.start()
    groups[...] = nn(select[...], encoded[...])
    grads = nn(weight_hi, cot[...]) + nn(weight_lo, cot[...])
    gg[...] = grads.astype(BF16)
    rows_f = groups[...]
    ms = (jnp.sum(rows_f * rows_f, axis=-1, keepdims=True) + padsq[0:1, 0:1]) * (0.5 / D)
    r = lax.rsqrt(ms + EPS)
    scale[...] = jnp.broadcast_to(r, (SLOTS, 128))
    inner = rows_f * r
    xn[...] = inner.astype(BF16)

    def turn(field, part, each, blocks):
        turned[...] = field.T.astype(BF16)
        for k in range(XN):
            at = lax.rem(x + k, XN)
            for b in range(blocks):
                rows = slice(b * each, (b + 1) * each)
                begin = (b * PLANE + at * CN + core) * each
                lt[part, k, rows, 0:SLOTS] = turned[pl.ds(pl.multiple_of(begin, 16), each), :]
                begin = (b * PLANE + at * CN + 1 - core) * each
                lto[part, k, rows, :] = turned[pl.ds(pl.multiple_of(begin, 16), each), :]

    turn(inner, 0, ru, zh)
    turn(grads, 1, rd, zn)
    mate = plane_at(x * CN + 1 - core)
    base = ids(4)
    swaps += [
        rdma(lto, lt.at[:, :, :, SLOTS : 2 * SLOTS], base, mate, y),
        rdma(fac.at[1, 0:SLOTS, :], fac.at[1, SLOTS : 2 * SLOTS, :], base + 1, mate, y),
        rdma(fac.at[0, 0:SLOTS, :], fac.at[0, SLOTS : 2 * SLOTS, :], base + 2, mate, y),
        rdma(vx, vr, base + 3, mate, y),
    ]
    swaps[0].start()

    def forward(b, carry):
        cols = pl.ds(pl.multiple_of(b * 256, 256), 256)
        pre_act = nn(xn[...], up[0:D, cols]) + scale[:, 0:1] * padup[0:1, cols]
        square = pre_act * pre_act
        bend = jnp.tanh(G0 * pre_act * (1.0 + G1 * square))
        fac[1, 0:SLOTS, cols] = (0.5 * pre_act * (1.0 + bend)).astype(BF16)
        slope[:, cols] = 0.5 * (1.0 + bend) + 0.5 * pre_act * (1.0 - bend * bend) * (
            G0 * (1.0 + 3.0 * G1 * square)
        )
        return carry

    lax.fori_loop(0, 4, forward, 0)
    swaps[1].start()

    def backward(b, carry):
        cols = pl.ds(pl.multiple_of(b * 256, 256), 256)
        pre_grad = (nn(gg[...], down[:, cols]) * slope[:, cols]).astype(BF16)
        fac[0, 0:SLOTS, cols] = pre_grad
        pad_term = jnp.sum(pre_grad.astype(F32) * scale[:, 0:1], axis=0, keepdims=True)
        vx[:, cols] = jnp.broadcast_to(pad_term, (8, 256))
        return carry

    lax.fori_loop(0, 4, backward, 0)
    swaps[2].start()
    swaps[3].start()

    rq = SLOTS // yn
    partial[...] = nt(fac[1, 0:SLOTS, :], down[...])
    ars[...] = partial[...].astype(BF16)
    base = ids(2 * yn)
    my_rows = pl.ds(pl.multiple_of(y * rq, rq), rq)
    for o in range(1, yn):
        at_y = lax.rem(y + o, yn)
        share1.append(rdma(ars.at[pl.ds(pl.multiple_of(at_y * rq, rq), rq), :], ar1.at[o - 1], base + o, seq, at_y))
        share1[-1].start()
        share2.append(rdma(io.at[my_rows, :], io.at[my_rows, :], base + yn + o, seq, at_y))
        at_y = lax.rem(y - o + yn, yn)
        other = pl.ds(pl.multiple_of(at_y * rq, rq), rq)
        from2.append(rdma(io.at[other, :], io.at[other, :], base + yn + o, seq, at_y))

    for copy in swaps:
        copy.wait_recv()
    right_x = plane_at(lax.rem(x + 1, XN) * CN + core)
    left_x = plane_at(lax.rem(x + XN - 1, XN) * CN + core)

    def on_z(o):
        return lax.rem(z + o + zn, zn)

    def device_z(o):
        return on_z(o) * PLANE + me

    def sent(*args):
        copy = rdma(*args)
        copy.start()
        copies.append(copy)
        return copy

    def f32(block):
        return block.astype(F32)

    class AlongX:
        def __init__(self, upper, lower, refs):
            self.near_r, self.near_l, self.end_r, self.end_l = refs[:4]
            self.near_r_in, self.near_l_in, self.end_r_in, self.end_l_in = refs[4:]
            self.cut_r, self.cut_l = upper, lower
            self.up = {1: self.end_r, 2: self.near_r.at[0:upper, :], 3: self.near_l.at[lower:, :]}
            self.low = {1: self.near_r.at[upper:, :], 2: self.near_l.at[0:lower, :], 3: self.end_l}
            self.base = ids(6)

        def ahead(self):
            i, far_r, far_l = self.base, slice(0, self.cut_r), slice(0, self.cut_l)
            near_r, near_l = slice(self.cut_r, None), slice(self.cut_l, None)
            self.far = [
                sent(self.near_r.at[far_r, :], self.near_r_in.at[far_r, :], i, right_x, y),
                sent(self.near_l.at[far_l, :], self.near_l_in.at[far_l, :], i + 1, left_x, y),
            ]
            self.end = [
                sent(self.near_r.at[near_r, :], self.near_r_in.at[near_r, :], i + 2, right_x, y),
                sent(self.near_l.at[near_l, :], self.near_l_in.at[near_l, :], i + 3, left_x, y),
            ]

        def later(self):
            i = self.base
            self.far[0].wait_recv()
            self.end_r[...] = (f32(self.end_r[...]) + f32(self.near_r_in[0 : self.cut_r, :])).astype(BF16)
            self.end.append(sent(self.end_r, self.end_r_in, i + 4, right_x, y))
            self.far[1].wait_recv()
            self.end_l[...] = (f32(self.end_l[...]) + f32(self.near_l_in[0 : self.cut_l, :])).astype(BF16)
            self.end.append(sent(self.end_l, self.end_l_in, i + 5, left_x, y))

        def arrived(self):
            for copy in self.end:
                copy.wait_recv()
            return (
                f32(self.near_l_in[self.cut_l :, :]) + f32(self.end_r_in[...]),
                f32(self.near_r_in[self.cut_r :, :]) + f32(self.end_l_in[...]),
            )

    def up_rows(t):
        return pl.ds(pl.multiple_of(jnp.where(t < zh, ru * t, 256), 16), ru)

    def down_rows(t):
        return pl.ds(pl.multiple_of(128 + rd * t, 16), rd)

    pad_part = pad_col[pl.ds(pl.multiple_of(ru * jnp.maximum(seq - sn // 2, 0), 16), ru), 0:1]

    widths = WIDTHS_Z + WIDTHS_X

    def columns(q):
        return slice(sum(widths[:q]), sum(widths[: q + 1]))

    def write(q, up_sum, down_sum):
        cols = columns(q)
        up_out[:, cols] = jnp.where(z < zh, up_sum, pad_part * up_sum[0:1])
        down_out[:, cols] = down_sum

    def terms(q):
        cols = columns(q)
        for part in range(2):
            yield nn(lt[part].reshape(XN * 128, 2 * SLOTS), fac[part, :, cols])
        yield in_rows([vx[0:1, cols] + vr[0:1, cols]], (32, widths[q]))

    def x_first(q):
        own, za_up, za_down, za_up_in, za_down_in, zb, zb_in, *rest = along_x[q - NZ]
        by_x = AlongX(128, 144, rest)
        base = ids(6)

        def piece(o):
            t = on_z(o)
            return own[up_rows(t), :], own[down_rows(t), :]

        def first():
            for part, term in enumerate(terms(q)):
                if part < 2:
                    rows = slice(128 * part, 128 * part + 128)
                    own[rows, :] = term[0:128]
                    for k in range(1, XN):
                        (by_x.low if part else by_x.up)[k][0:128, :] = term[128 * k : 128 * k + 128].astype(BF16)
                else:
                    own[256:288, :] = term
                    for k in range(1, XN):
                        by_x.low[k][128:144, :] = term[0:16].astype(BF16)
            by_x.ahead()

        def two_away():
            a, b = by_x.arrived()
            own[0:128, :] += a
            own[128:PIECE, :] += b
            za_up[0:32, :] = piece(4)[0].astype(BF16)
            near = piece(3)
            za_up[32:64, :] = near[0].astype(BF16)
            za_up[64:80, :] = near[1].astype(BF16)
            far.append(sent(za_up, za_up_in, base, device_z(2), y))
            za_down[0:16, :] = piece(-4)[1].astype(BF16)
            near = piece(-3)
            za_down[16:32, :] = near[1].astype(BF16)
            za_down[32:64, :] = near[0].astype(BF16)
            far.append(sent(za_down, za_down_in, base + 1, device_z(-2), y))

        far, last = [], []

        def nearer():
            for copy in far:
                copy.wait_recv()
            from_up, from_down = f32(za_up_in[...]), f32(za_down_in[...])
            for i, o in enumerate((2, -2, 1, -1)):
                up_sum, down_sum = piece(o)
                if o == 2:
                    up_sum = up_sum + from_up[0:32]
                elif o == -2:
                    down_sum = down_sum + from_down[0:16]
                elif o == 1:
                    up_sum, down_sum = up_sum + from_up[32:64], down_sum + from_up[64:80]
                else:
                    up_sum, down_sum = up_sum + from_down[32:64], down_sum + from_down[16:32]
                zb[i, 0:32, :] = up_sum.astype(BF16)
                zb[i, 32:48, :] = down_sum.astype(BF16)
                last.append(sent(zb.at[i], zb_in.at[i], base + 2 + i, device_z(o), y))

        def final():
            for copy in last:
                copy.wait_recv()
            up_sum, down_sum = piece(0)
            for i in range(4):
                up_sum = up_sum + f32(zb_in[i, 0:32, :])
                down_sum = down_sum + f32(zb_in[i, 32:48, :])
            write(q, up_sum, down_sum)

        return [first, by_x.later, two_away, nearer, final]

    def z_first(n):
        prod_z, ring_up, ring_down, ring_up_in, ring_down_in, *rest = along_z[n]
        by_x = AlongX(32, 16, rest)
        base = ids(8)
        up_copy, down_copy = [], []

        def piece(o):
            t = on_z(o)
            return prod_z[:, up_rows(t), :], prod_z[:, down_rows(t), :]

        def hop(i):
            if i == 0:
                for part, term in enumerate(terms(n)):
                    for k in range(XN):
                        if part < 2:
                            prod_z[k, 128 * part : 128 * part + 128, :] = term[128 * k : 128 * k + 128]
                        else:
                            prod_z[k, 256:288, :] = term
                ring_up[0, :, 0:32, :] = piece(4)[0].astype(BF16)
                ring_down[0, :, 32:48, :] = piece(-4)[1].astype(BF16)
                rows_up, rows_down = slice(0, 32), slice(32, 48)
            else:
                up_copy[i - 1].wait_recv()
                up_sum, down_sum = piece(4 - i)
                up_sum = up_sum + f32(ring_up_in[i - 1, :, 0:32, :])
                if i > 1:
                    down_sum = down_sum + f32(ring_up_in[i - 1, :, 32:48, :])
                ring_up[i, :, 0:32, :] = up_sum.astype(BF16)
                ring_up[i, :, 32:48, :] = down_sum.astype(BF16)
                down_copy[i - 1].wait_recv()
                up_sum, down_sum = piece(i - 4)
                down_sum = down_sum + f32(ring_down_in[i - 1, :, 32:48, :])
                if i > 1:
                    up_sum = up_sum + f32(ring_down_in[i - 1, :, 0:32, :])
                ring_down[i, :, 0:32, :] = up_sum.astype(BF16)
                ring_down[i, :, 32:48, :] = down_sum.astype(BF16)
                rows_up = rows_down = slice(0, 48)
            up_copy.append(
                sent(ring_up.at[i, :, rows_up, :], ring_up_in.at[i, :, rows_up, :], base + i, device_z(1), y)
            )
            down_copy.append(
                sent(ring_down.at[i, :, rows_down, :], ring_down_in.at[i, :, rows_down, :], base + 4 + i, device_z(-1), y)
            )

        mine_z = []

        def collect():
            up_copy[3].wait_recv()
            down_copy[3].wait_recv()
            up_sum, down_sum = piece(0)
            up_sum = up_sum + f32(ring_up_in[3, :, 0:32, :]) + f32(ring_down_in[3, :, 0:32, :])
            down_sum = down_sum + f32(ring_up_in[3, :, 32:48, :]) + f32(ring_down_in[3, :, 32:48, :])
            for k in range(1, XN):
                by_x.up[k][...] = up_sum[k].astype(BF16)
                by_x.low[k][...] = down_sum[k].astype(BF16)
            mine_z.extend([up_sum[0], down_sum[0]])
            by_x.ahead()

        def final():
            a, b = by_x.arrived()
            write(n, mine_z[0] + a, mine_z[1] + b)

        return [functools.partial(hop, i) for i in range(4)] + [collect, by_x.later, final]

    def reduce_share():
        for copy in share1:
            copy.wait_recv()
        summed = groups[my_rows, :] + partial[my_rows, :]
        for o in range(1, yn):
            summed = summed + ar1[o - 1].astype(F32)
        io[my_rows, :] = summed.astype(BF16)
        for copy in share2:
            copy.start()

    def share():
        for copy in from2:
            copy.wait_recv()
        stores.append(pltpu.make_async_copy(io, io_out, store.at[2]))
        stores[2].start()

    steps = [iter(z_first(q) if q < NZ else x_first(q)) for q in range(NQ)]
    for i, q in enumerate(ORDER):
        if i == SHARE_AT:
            reduce_share()
        if i == STORE_AT:
            share()
        next(steps[q])()

    for copy in stores:
        copy.wait()
    for copy in step1 + step3 + swaps + share1 + share2:
        copy.wait_send()
    for o in range(1, len(step2)):
        pl.when(z + o < zn)(step2[o].wait_send)
    for copy in copies:
        copy.wait_send()


def finish(encoded, mct, io, up_sum, down_sum, mixed, up_out, down_out):
    both = io[...]
    spread = nn(mct[...], jnp.concatenate([both, both], axis=0))
    mixed[...] = (encoded[...].astype(F32) + spread).astype(BF16)
    up_out[...] = up_sum[...]
    down_out[...] = down_sum[...]


def on_device(
    zn, yn, tokens, positions, value_proj, write_proj, read_proj, step_proj, step_bias, decay_rate, reset_depth,
    out_proj, router, pad_vector, up_weight, down_weight, cotangent,
):
    sn = zn * PLANE
    ru, rd, qw = 2 * D // sn, D // sn, D // yn
    n_pos = positions.shape[0]
    vm = pltpu.VMEM
    n_sem = PLANE + zn + PLANE * yn + 4 + 2 * yn + NQ * 14
    scratch = [
        vm((ROWS, D), BF16), vm((1, n_pos), jnp.int32), vm((D, D), BF16), vm((D, 2 * NS), BF16), vm((HEADS, D), BF16),
        vm((1, HEADS), F32), vm((1, HEADS), F32), vm((1, ROWS), F32), vm((D, D), BF16), vm((1, D), F32),
        vm((8, D // 8), BF16), vm((2 * D, D), BF16), vm((D, D), BF16), vm((ROWS, D), BF16),
        vm((ROWS, D), BF16), vm((ROWS, 2 * NS), BF16), vm((ROWS, D), BF16), vm((CHUNKS, Q, Q), F32),
        vm((CHUNKS, Q, Q), F32), vm((2 * Q, D), BF16), vm((ROWS, D), BF16), vm((ROWS, D), F32), vm((NS, D), F32),
        vm((CHUNKS, NS, D), F32), vm((CHUNKS + 1, 8, D), F32), vm((ROWS, D), F32),
        vm((PLANE, 32, qw), BF16), vm((PLANE, 32, qw), BF16), vm((32, qw), BF16), vm((zn, 32, qw), BF16),
        vm((PLANE, 16, qw), BF16), vm((NS, D), BF16),
        vm((ROWS, D), BF16), vm((SLOTS, D), F32), vm((SLOTS, ROWS), BF16), vm((ROWS, 2 * SLOTS), BF16),
        vm((16, D), F32), vm((D, 128), F32), vm((8, 128), F32),
        vm((SLOTS, D), BF16), vm((SLOTS, D), BF16), vm((SLOTS, 128), F32), vm((SLOTS, D), F32),
        vm((2, 2 * SLOTS, D), BF16), vm((D, SLOTS), BF16), vm((2, XN, 128, 2 * SLOTS), BF16),
        vm((2, XN, 128, SLOTS), BF16),
        vm((8, D), F32), vm((8, D), F32),
        vm((SLOTS, D), F32), vm((SLOTS, D), BF16), vm((max(yn - 1, 1), SLOTS // yn, D), BF16), vm((SLOTS, D), BF16),
        [
            [vm((XN, 288, w), F32)] + [vm((4, XN, 48, w), BF16)] * 4
            + [vm((rows, w), BF16) for rows in (48, 48, 32, 16) * 2] for w in WIDTHS_Z
        ],
        [
            [vm((288, w), F32)] + [vm((rows, w), BF16) for rows in (80, 64) * 2] + [vm((4, 48, w), BF16)] * 2
            + [vm((rows, w), BF16) for rows in (PIECE, PIECE, 128, 144) * 2] for w in WIDTHS_X
        ],
        pltpu.SemaphoreType.DMA((15,)), pltpu.SemaphoreType.DMA((3,)), pltpu.SemaphoreType.DMA((n_sem,)), pltpu.SemaphoreType.DMA((n_sem,)),
    ]
    encoded, mct, io, up_sum, down_sum = pl.pallas_call(
        functools.partial(kernel, zn, yn),
        out_shape=(
            jax.ShapeDtypeStruct((ROWS, D), BF16),
            jax.ShapeDtypeStruct((ROWS, 2 * SLOTS), BF16),
            jax.ShapeDtypeStruct((SLOTS, D), BF16),
            jax.ShapeDtypeStruct((ru, D), F32),
            jax.ShapeDtypeStruct((rd, D), F32),
        ),
        in_specs=[pl.BlockSpec(memory_space=pl.ANY)] * 15,
        out_specs=(pl.BlockSpec(memory_space=pl.ANY),) * 3 + (pl.BlockSpec(memory_space=pltpu.VMEM),) * 2,
        scratch_shapes=scratch,
        compiler_params=pltpu.CompilerParams(
            collective_id=0, has_side_effects=True, vmem_limit_bytes=60 * 2**20
        ),
    )(
        tokens, positions.reshape(1, n_pos), value_proj, write_proj, read_proj, step_proj.T, step_bias.reshape(1, HEADS),
        decay_rate.reshape(1, HEADS), reset_depth.reshape(1, ROWS), out_proj, router.reshape(1, D),
        pad_vector.reshape(8, D // 8), up_weight, down_weight, cotangent,
    )
    part = ROWS // 2
    return pl.pallas_call(
        finish,
        grid=(2,),
        out_shape=(
            jax.ShapeDtypeStruct((ROWS, D), BF16),
            jax.ShapeDtypeStruct((ru, D), F32),
            jax.ShapeDtypeStruct((rd, D), F32),
        ),
        in_specs=[
            pl.BlockSpec((part, D), lambda i: (i, 0)),
            pl.BlockSpec((part, 2 * SLOTS), lambda i: (i, 0)),
            pl.BlockSpec((SLOTS, D), lambda i: (0, 0)),
            pl.BlockSpec((ru // 2, D), lambda i: (i, 0)),
            pl.BlockSpec((rd // 2, D), lambda i: (i, 0)),
        ],
        out_specs=(
            pl.BlockSpec((part, D), lambda i: (i, 0)),
            pl.BlockSpec((ru // 2, D), lambda i: (i, 0)),
            pl.BlockSpec((rd // 2, D), lambda i: (i, 0)),
        ),
        compiler_params=pltpu.CompilerParams(vmem_limit_bytes=60 * 2**20),
    )(encoded, mct, io, up_sum, down_sum)


def solution(mesh):
    placed = (
        P("seq", None), P(), P(), P(), P(), P(), P(), P(), P("seq"), P(), P(), P(),
        P(None, "mlp"), P(None, "mlp"), P("seq", None),
    )
    return jax.shard_map(
        functools.partial(on_device, mesh.shape["seq"] // PLANE, mesh.shape["mlp"]),
        mesh=mesh,
        in_specs=placed,
        out_specs=(P("seq", None), P("seq", "mlp"), P("seq", "mlp")),
        check_vma=False,
    )
```
